512 devices in a mesh: member: 16 (over x_lo, y), tile: 32 (over z, x_hi, core).
Axes of the slice: x: 4 (x_hi: 2, x_lo: 2; x = x_hi * 2 + x_lo), y: 8, z: 8, core: 2. Of those that a mesh axis runs over, the one named last changes fastest.
Arguments:
- density: float32 [16, 6, 512, 512], P('member', None, 'tile'), may hold values from 0.05 to 5
- scaling: float32 [16, 6, 512, 512], P('member', None, 'tile'), may hold values from 0.2 to 5
- member_weights: float32 [16], P('member'), may hold values from 0.5 to 11
- seams: int32 [3, 4, 6], replicated, may hold values from 0 to 5, as said below
Outputs:
- new_scaling: float32 [16, 6, 512, 512], P('member', None, 'tile')
- dual_scaling: float32 [16, 6, 512, 512], P('member', None, 'tile')
- barycenter: float32 [6, 512, 512], P(None, 'tile')
The draws below stay inside these ranges and needn't reach their ends.
Inputs may be any that keep to these rules, and one draw needn't show every extreme that they name: Edges are numbered 0 first row, 1 last row, 2 first column, 3 last column. The table describes the six faces of a cube, each face's frame turned or mirrored: seams[0, e, f] is the face across edge e of face f, seams[1, e, f] the edge of that face which meets it, and the relation is symmetric; seams[2, e, f] is 1 where positions along the seam run opposite ways on the two faces, and the same from both sides.
All inputs are finite; a program needn't handle non-finite values.
Results may differ from the reference program's by a relative error of at most 0.00007.
Values sent between devices are 32-bit elements; how exact they have to be, the bound alone decides.
No kernel may reach another device: no remote copies, remote signals or barrier semaphores. Data moves between devices by JAX's collectives and lax.ppermute only.
A program may use at most 64 MiB of HBM per device.

```python
import math
import jax
import jax.numpy as jnp
from jax import lax

FACES = 6
STEPS = 4
MEMBERS = 16
SIDE = 512


def draw_seams(key, part):
    key = jax.random.fold_in(key, 5)
    normal = jnp.array([[1, 0, 0], [-1, 0, 0], [0, 1, 0], [0, -1, 0], [0, 0, 1], [0, 0, -1]], jnp.int32)
    across = jnp.array([[0, 1, 0], [0, 0, 1], [0, 0, 1], [1, 0, 0], [1, 0, 0], [0, 1, 0]], jnp.int32)
    downward = jnp.array([[0, 0, 1], [0, 1, 0], [1, 0, 0], [0, 0, 1], [0, 1, 0], [1, 0, 0]], jnp.int32)
    symmetry = jax.random.randint(jax.random.fold_in(key, 1), (6,), 0, 8).astype(jnp.int32)
    swapped = (symmetry % 2 == 1)[:, None]
    sign_a = (1 - 2 * (symmetry // 2 % 2))[:, None]
    sign_b = (1 - 2 * (symmetry // 4 % 2))[:, None]
    axis_a = sign_a * jnp.where(swapped, downward, across)
    axis_b = sign_b * jnp.where(swapped, across, downward)
    order = jax.random.permutation(jax.random.fold_in(key, 2), 6).astype(jnp.int32)
    normal = jnp.zeros((6, 3), jnp.int32).at[order].set(normal)
    axis_a = jnp.zeros((6, 3), jnp.int32).at[order].set(axis_a)
    axis_b = jnp.zeros((6, 3), jnp.int32).at[order].set(axis_b)
    outward = jnp.stack([-axis_b, axis_b, -axis_a, axis_a], axis=1)
    along = jnp.stack([axis_a, axis_a, axis_b, axis_b], axis=1)
    match_face = jnp.all(outward[:, :, None, :] == normal[None, None, :, :], axis=-1).astype(jnp.int32)
    face = jnp.sum(match_face * jnp.arange(6, dtype=jnp.int32)[None, None, :], axis=-1).astype(jnp.int32)
    other_out = outward[face]
    meeting = jnp.all(other_out == normal[:, None, None, :], axis=-1).astype(jnp.int32)
    edge = jnp.sum(meeting * jnp.arange(4, dtype=jnp.int32)[None, None, :], axis=-1).astype(jnp.int32)
    other_along = along[face, edge]
    flip = (jnp.sum(along * other_along, axis=-1) < 0).astype(jnp.int32)
    return jnp.stack([face.T, edge.T, flip.T]).astype(jnp.int32)


def draw_member_weights(key, part):
    key = jax.random.fold_in(key, 3)
    rising = 1.0 + 2.0 * jnp.arange(MEMBERS, dtype=jnp.float32) / (MEMBERS - 1)
    return rising * jax.random.uniform(key, (MEMBERS,), jnp.float32, 0.6, 1.4)


def steps_of(stream_key, extent, shards, low, largest):
    factor_of, own = 1.0, jax.random.fold_in(stream_key, 6)
    for axis_at, shards_of in shards:
        steps = jnp.exp(jax.random.uniform(jax.random.fold_in(own, axis_at), (shards_of,), jnp.float32, low / len(shards), largest / len(shards)))
        factor_of = factor_of * jnp.repeat(steps, extent[axis_at] // shards_of).reshape([-1 if axis == axis_at else 1 for axis in range(len(extent))])
    return factor_of


def setup_inputs(seed: int = 0) -> dict:
    keys = jax.random.split(jax.random.key(seed), 5)
    return {
        "density": jnp.clip(jnp.exp(math.log(5.0) - 4.6051702 * jax.random.uniform(keys[0], (MEMBERS, FACES, SIDE, SIDE), jnp.float32) ** steps_of(keys[0], (MEMBERS, FACES, SIDE, SIDE), ((0, 16), (2, 32)), -0.2, 0.2)), 0.05, 5.0),
        "scaling": jnp.clip(jnp.exp(math.log(5.0) - 3.218876 * jax.random.uniform(keys[1], (MEMBERS, FACES, SIDE, SIDE), jnp.float32) ** steps_of(keys[1], (MEMBERS, FACES, SIDE, SIDE), ((0, 16), (2, 32)), -0.2, 0.2)), 0.2, 5.0),
        "member_weights": draw_member_weights(jax.random.fold_in(keys[4], 71), 0),
        "seams": draw_seams(jax.random.fold_in(keys[4], 71), 0),
    }


KAPPA = 0.24


def ghost_lines(field, seams):
    edges = jnp.stack([field[:, 0, :], field[:, -1, :], field[:, :, 0], field[:, :, -1]], axis=1)
    result = []
    for edge_id in range(4):
        taken = edges[seams[0, edge_id], seams[1, edge_id]]
        result.append(jnp.where((seams[2, edge_id] == 1)[:, None], taken[:, ::-1], taken))
    return result


def diffuse(field, seams):
    upper, lower, left, right = ghost_lines(field, seams)
    widened = jnp.concatenate([upper[:, None, :], field, lower[:, None, :]], axis=1)
    vertical = widened[:, :-2, :] + widened[:, 2:, :]
    lateral = jnp.concatenate([left[:, :, None], field[:, :, :-1]], axis=2) + jnp.concatenate([field[:, :, 1:], right[:, :, None]], axis=2)
    return field + KAPPA * ((vertical + lateral) - 4.0 * field)


def reference(density, scaling, member_weights, seams):
    def kernel(field):
        for counter in range(STEPS):
            field = diffuse(field, seams)
        return field

    def member_pass(pair_args):
        member_density, member_scaling = pair_args
        dual_field = member_density / kernel(member_scaling)
        marginal_field = member_scaling * kernel(dual_field)
        return dual_field, marginal_field

    dual_scaling, marginal = lax.map(member_pass, (density, scaling))
    log_marginal = jnp.log(marginal)
    weighted = jnp.einsum("k,kfrc->frc", member_weights, log_marginal, precision=lax.Precision.HIGHEST)
    log_mean = weighted / jnp.sum(member_weights)
    barycenter = jnp.exp(log_mean)
    new_scaling = (scaling * barycenter) / marginal
    return new_scaling, dual_scaling, barycenter
```

```python
import jax
import jax.numpy as jnp
from jax import lax
from jax.experimental import pallas as pl
from jax.experimental.pallas import tpu as pltpu
from jax.sharding import PartitionSpec as P

KAPPA = 0.24
STEPS = 4
FACES = 6
ROWS = 16
SIDE = 512
HALO = 8
TALL = ROWS + 2 * HALO
WIDE = SIDE + 128
HIGH = lax.Precision.HIGHEST


def iota(shape, dim):
    return lax.broadcasted_iota(jnp.int32, shape, dim)


def reverse_lanes(x):
    index = 127 - iota((8, 128), 1)
    tiles = [
        jnp.take_along_axis(x[:, at : at + 128], index, axis=1)
        for at in range(0, x.shape[1], 128)
    ]
    return jnp.concatenate(tiles[::-1], axis=1) if len(tiles) > 1 else tiles[0]


def column_strips(first, last):
    strips = None
    for g in range(FACES):
        a, b = first(g), last(g)
        lane = iota(a.shape, 1)
        moved = pltpu.roll(jnp.where(lane >= 64, b, a), 16 * g + 8, 1)
        strips = moved if strips is None else jnp.where(lane >= 16 * g, moved, strips)
    return strips


def spread(block):
    return [pltpu.roll(block, 96 - 32 * b, 1) for b in range(3)]


def unspread(b0, b1, b2):
    lane = iota((8, 128), 1)
    return jnp.where(
        lane < 32, pltpu.roll(b0, 32, 1), jnp.where(lane < 64, pltpu.roll(b1, 64, 1), pltpu.roll(b2, 96, 1))
    )


def pack_kernel(place, seams, scaling, density, up, down, message):
    p = place[0]
    count = message.shape[0]
    lane = iota((8, 128), 1)
    sub = iota((8, 128), 0)
    for g in range(FACES):
        up[g] = scaling[g, HALO:]
        up[FACES + g] = density[g, HALO:]
        down[g] = scaling[g, :HALO]
        down[FACES + g] = density[g, :HALO]
    vs = column_strips(lambda g: scaling[g, :, :128], lambda g: scaling[g, :, SIDE - 128 :])
    vd = column_strips(lambda g: density[g, :, :128], lambda g: density[g, :, SIDE - 128 :])
    tail = spread(vd[8:])
    head = (vs[:8], vs[8:], vd[:8])
    block = jnp.concatenate([jnp.where(lane < 96, head[b], tail[b]) for b in range(3)], axis=0)
    is_last = p == count - 1
    is_edge = (p == 0) | is_last

    @pl.when(jnp.logical_not(is_edge))
    def _():
        for q in range(count):
            message[q] = block

    @pl.when(is_edge)
    def _():
        message[0] = block
        message[count - 1] = block
        e = is_last.astype(jnp.int32)
        base = pl.multiple_of(e * 8, 8)
        own_s = jnp.where(is_last, vs[:8], vs[8:])
        own_d = jnp.where(is_last, vd[:8], vd[8:])
        far = jnp.where(is_last, pltpu.roll(own_d, 5, 0), pltpu.roll(own_d, 3, 0))
        free = jnp.where(is_last, (sub >= 5).astype(jnp.int32), (sub <= 2).astype(jnp.int32)) == 1
        lane16 = lane % 16
        coded = jnp.where(
            free & (lane16 < 4),
            pltpu.roll(far, 124, 1),
            jnp.where(free & (lane16 >= 12), pltpu.roll(far, 4, 1), own_s),
        )
        extra = spread(coded)
        pieces = []
        for g in range(FACES):
            turned = seams[2, e, g] == 1
            s = scaling[g, pl.ds(base, 8), :]
            d = density[g, pl.ds(base, 8), :]
            pieces.append((jnp.where(turned, reverse_lanes(s), s), jnp.where(turned, reverse_lanes(d), d)))
        sub_wide = iota((8, SIDE), 0)
        lane_wide = iota((8, SIDE), 1) % 128
        blocks = []
        for b in range(3):
            (s0, d0), (s1, d1) = pieces[2 * b], pieces[2 * b + 1]
            low = jnp.where(is_last, pltpu.roll(d0, 4, 0), d0)
            high = jnp.where(is_last, d1, pltpu.roll(d1, 4, 0))
            blocks.append((s0, s1, jnp.where(sub_wide < 4, low, high)))
        for t in range(3):
            tail_t = jnp.concatenate([extra[t]] * 4, axis=1)
            for r in range(8):
                moved = [pltpu.roll(blocks[b][t], (32 * b - 16 * r + 8) % SIDE, 1) for b in range(3)]
                full = jnp.where(
                    lane_wide < 32,
                    moved[0],
                    jnp.where(lane_wide < 64, moved[1], jnp.where(lane_wide < 96, moved[2], tail_t)),
                )
                for a in range(4):
                    q = 8 * a + r
                    if 0 < q < count - 1:
                        message[q, 8 * t : 8 * t + 8, :] = full[:, 128 * a : 128 * a + 128]


def step(x, where):
    above = pltpu.roll(x, 1, 0)
    below = pltpu.roll(x, TALL - 1, 0)
    left = pltpu.roll(x, 1, 1)
    right = pltpu.roll(x, WIDE - 1, 1)
    if where is not None:
        lane = iota((8, 128), 1)
        sub = iota((8, 128), 0)
        if where == "first":
            at, edge, depth = 0, 8, 7 - sub
        else:
            at, edge, depth = 24, 23, sub
        rows = x[at : at + 8]
        line = jnp.broadcast_to(x[edge : edge + 1, SIDE:], (8, 128))
        on_left = lane == 127 - depth
        on_right = lane == depth
        from_left = jnp.sum(jnp.where(on_left, line, 0.0), axis=1, keepdims=True)
        from_right = jnp.sum(jnp.where(on_right, line, 0.0), axis=1, keepdims=True)
        columns = jnp.where(
            on_left, rows[:, :1], jnp.where(on_right, rows[:, SIDE - 1 : SIDE], 0.0)
        )
        across = jnp.sum(columns, axis=0, keepdims=True)
        fixed_left = jnp.concatenate(
            [jnp.where(lane == 0, from_left, left[at : at + 8, :128]), left[at : at + 8, 128:]], axis=1
        )
        fixed_right = jnp.concatenate(
            [
                right[at : at + 8, : SIDE - 128],
                jnp.where(lane == 127, from_right, right[at : at + 8, SIDE - 128 : SIDE]),
                right[at : at + 8, SIDE:],
            ],
            axis=1,
        )
        ghost = (lane < 8) | (lane >= 120)
        if where == "first":
            left = jnp.concatenate([fixed_left, left[8:]], axis=0)
            right = jnp.concatenate([fixed_right, right[8:]], axis=0)
            tile = jnp.where(ghost & (sub == 0), across, above[8:16, SIDE:])
            tile = jnp.concatenate([above[:8, SIDE:], tile, above[16:, SIDE:]], axis=0)
            above = jnp.concatenate([above[:, :SIDE], tile], axis=1)
        else:
            left = jnp.concatenate([left[:24], fixed_left], axis=0)
            right = jnp.concatenate([right[:24], fixed_right], axis=0)
            tile = jnp.where(ghost & (sub == 7), across, below[16:24, SIDE:])
            tile = jnp.concatenate([below[:16, SIDE:], tile, below[24:, SIDE:]], axis=0)
            below = jnp.concatenate([below[:, :SIDE], tile], axis=1)
    return x + KAPPA * (((above + below) + (left + right)) - 4.0 * x)


def heat_kernel(
    place, seams, weight, scaling, density, up, down, message, dual, marginal, weighted,
    xs, xd, mixed, chunk, all_s, all_d, lines_s, lines_d,
):
    q = place[0]
    count = message.shape[0]
    last = count - 1
    members = weighted.shape[0]
    per = 48 // members
    lane = iota((8, 128), 1)
    sub = iota((8, 128), 0)
    for g in range(FACES):
        for x, field, at in ((xs, scaling, 0), (xd, density, FACES)):
            x[g, :HALO, :SIDE] = up[at + g]
            x[g, HALO : HALO + ROWS, :SIDE] = field[g]
            x[g, HALO + ROWS :, :SIDE] = down[at + g]

    def far_rows(p):
        return unspread(
            message[p, :8, :], message[p, 8:16, :], message[p, 16:24, :]
        )

    mixed[:TALL, :128] = column_strips(lambda g: xs[g, :, :128], lambda g: xs[g, :, SIDE - 128 : SIDE])
    mixed[TALL:, :128] = column_strips(lambda g: xd[g, :, :128], lambda g: xd[g, :, SIDE - 128 : SIDE])

    main, upper, lower = last - q, jnp.minimum(last + 1 - q, last), jnp.maximum(last - 1 - q, 0)
    source = jnp.where(q == 1, last, 0)
    coded = far_rows(source)
    near = jnp.where(q == 1, pltpu.roll(coded, 3, 0), pltpu.roll(coded, 5, 0))
    coded_d = jnp.where(lane % 16 < 8, pltpu.roll(near, 4, 1), pltpu.roll(near, 124, 1))
    parts_s = (
        jnp.where(q == last - 1, coded, message[lower, 8:16, :]),
        message[main, :8, :],
        message[main, 8:16, :],
        jnp.where(q == 1, coded, message[upper, :8, :]),
    )
    parts_d = (
        jnp.where(q == last - 1, coded_d, far_rows(lower)),
        message[main, 16:24, :],
        far_rows(main),
        jnp.where(q == 1, coded_d, message[upper, 16:24, :]),
    )
    for base, parts in ((0, parts_s), (TALL, parts_d)):
        for block in range(4):
            for i in range(8):
                at = base + TALL - 1 - 8 * block - i
                mixed[at : at + 1, 128:256] = parts[block][i : i + 1]

    chunk[...] = jnp.zeros_like(chunk)
    is_edge = (q == 0) | (q == last)

    @pl.when(jnp.logical_not(is_edge))
    def _():
        for e in range(2):
            p = e * last
            for g in range(FACES):
                b, h = g // 2, g % 2
                turn = (128 - 32 * b) % 128
                s = message[p, 8 * h : 8 * h + 8, :]
                d = message[p, 16:24, :]
                if turn:
                    s, d = pltpu.roll(s, turn, 1), pltpu.roll(d, turn, 1)
                if h != e:
                    d = pltpu.roll(d, 4, 0)
                at = 48 * e + 8 * g
                chunk[0, at : at + 8, :] = s
                chunk[1, at : at + 8, :] = d

    for is_first in (True, False):

        @pl.when(q == (0 if is_first else last))
        def _():
            for k, (lines, field) in enumerate(((lines_s, scaling), (lines_d, density))):
                for e in range(2):
                    for g in range(FACES):
                        if is_first:
                            rows = field[g, :HALO] if e == 0 else up[FACES * k + g]
                        else:
                            rows = down[FACES * k + g] if e == 0 else field[g, HALO:]
                        at = 48 * e + 8 * g
                        lines[at : at + 8, :] = rows
                        turned = seams[2, e, g] == 1
                        a, b = rows[:, :128], rows[:, SIDE - 128 :]
                        if is_first:
                            piece = pltpu.roll(jnp.where(turned, reverse_lanes(b), a), 8, 1)
                        else:
                            piece = pltpu.roll(jnp.where(turned, reverse_lanes(a), b), 24, 1)
                        chunk[k, at : at + 8, :] = piece

    for k in range(2):
        mixed[k * TALL : (k + 1) * TALL, 256:] = jnp.transpose(chunk[k])[:TALL]

    target = iota((1, 128), 1)
    wanted = jnp.full((1, 128), -1, jnp.int32)
    for f in range(FACES):
        for e in (2, 3):
            g, meets, turned = seams[0, e, f], seams[1, e, f], seams[2, e, f]
            start = jnp.where(
                meets >= 2,
                128 * turned + 16 * g + jnp.where(meets == 2, 8, 0),
                256 + 48 * meets + 8 * g,
            )
            at = 16 * f + (0 if e == 2 else 8)
            depth = at + 7 - target if e == 2 else target - at
            rising = (meets % 2) == 0
            index = start + jnp.where(rising, depth, 7 - depth)
            wanted = jnp.where((target >= at) & (target < at + 8), index, wanted)
    choice = (iota((384, 128), 0) == wanted).astype(jnp.float32)
    ghosts = jnp.dot(mixed[...], choice, precision=HIGH, preferred_element_type=jnp.float32)
    for f in range(FACES):
        turn = 120 - 16 * f
        xs[f, :, SIDE:] = pltpu.roll(ghosts[:TALL], turn, 1)
        xd[f, :, SIDE:] = pltpu.roll(ghosts[TALL:], turn, 1)

    for is_first in (True, False):

        @pl.when(q == (0 if is_first else last))
        def _():
            def gather(p, carry):
                at = pl.multiple_of(16 * p, 16)
                all_s[pl.ds(at, 16), :] = message[p, :16, :]
                all_d[pl.ds(at, 8), :] = message[p, 16:24, :]
                all_d[pl.ds(at + 8, 8), :] = far_rows(p)
                return carry

            lax.fori_loop(0, count, gather, 0)
            e = 0 if is_first else 1
            of_columns, of_lines = [], []
            for f in range(FACES):
                g, meets = seams[0, e, f], seams[1, e, f]
                depth = 7 - sub if is_first else sub
                rising = (meets % 2) == 0
                index = jnp.where(rising, depth, 7 - depth)
                column_at = jnp.where(meets >= 2, 16 * g + jnp.where(meets == 2, 8, 0), -1000)
                line_at = jnp.where(meets < 2, 48 * meets + 8 * g, -1000)
                of_columns.append((lane == column_at + index).astype(jnp.float32))
                of_lines.append((lane == line_at + index).astype(jnp.float32))
            of_columns = jnp.concatenate(of_columns, axis=0)
            of_lines = jnp.concatenate(of_lines, axis=0)[:, :96]
            for x, columns, lines in ((xs, all_s, lines_s), (xd, all_d, lines_d)):
                taken = lax.dot_general(
                    of_columns, columns[...], (((1,), (1,)), ((), ())),
                    precision=HIGH, preferred_element_type=jnp.float32,
                ) + jnp.dot(of_lines, lines[...], precision=HIGH, preferred_element_type=jnp.float32)
                for f in range(FACES):
                    piece = taken[8 * f : 8 * f + 8]
                    piece = jnp.where(seams[2, e, f] == 1, reverse_lanes(piece), piece)
                    at = 0 if is_first else HALO + ROWS
                    x[f, at : at + 8, :SIDE] = piece

    share = weight[0]
    for k in range(members):
        weighted[k, 8 * per :, :] = jnp.full((8, 128), share, jnp.float32)

    def run(where):
        def face(f, carry):
            x = xs[f]
            for _ in range(STEPS):
                x = step(x, where)
            y = xd[f] / x
            dual[f] = y[HALO : HALO + ROWS, :SIDE]
            for _ in range(STEPS):
                y = step(y, where)
            m = scaling[f] * y[HALO : HALO + ROWS, :SIDE]
            marginal[f] = m
            scaled = share * jnp.log(m)
            for i in range(2):
                for j in range(4):
                    t = 8 * f + 4 * i + j
                    at = pl.multiple_of(8 * lax.rem(t, per), 8)
                    weighted[lax.div(t, per), pl.ds(at, 8), :] = scaled[8 * i : 8 * i + 8, 128 * j : 128 * j + 128]
            return carry

        lax.fori_loop(0, FACES, face, 0)

    @pl.when(q == 0)
    def _():
        run("first")

    @pl.when(q == last)
    def _():
        run("last")

    @pl.when(jnp.logical_not(is_edge))
    def _():
        run(None)


def mean_kernel(parts, result):
    members, rows = result.shape[0], result.shape[1]
    total = parts[0]
    for k in range(1, members):
        total = total + parts[k]
    mean = total[:rows] / total[rows : rows + 1]
    value = jnp.exp(mean)
    for k in range(members):
        result[k] = value


def update_kernel(parts, scaling, marginal, fresh, barycenter):
    members = parts.shape[0]
    per = 48 // members
    for f in range(FACES):
        for i in range(2):
            for j in range(4):
                t = 8 * f + 4 * i + j
                at = 8 * (t % per)
                value = parts[t // per, at : at + 8, :]
                rows, columns = slice(8 * i, 8 * i + 8), slice(128 * j, 128 * j + 128)
                barycenter[f, rows, columns] = value
                fresh[f, rows, columns] = scaling[f, rows, columns] * value / marginal[f, rows, columns]


def body(density, scaling, member_weights, seams):
    tiles = lax.axis_size("tile")
    members = lax.axis_size("member")
    scaling = scaling[0]
    density = density[0]
    place = lax.axis_index("tile").astype(jnp.int32).reshape(1)
    f32 = jnp.float32
    vmem = pl.BlockSpec(memory_space=pltpu.VMEM)
    smem = pl.BlockSpec(memory_space=pltpu.SMEM)
    field = jax.ShapeDtypeStruct((FACES, ROWS, SIDE), f32)
    edge_rows = jax.ShapeDtypeStruct((2 * FACES, HALO, SIDE), f32)
    params = pltpu.CompilerParams(vmem_limit_bytes=24 * 1024 * 1024)
    up, down, message = pl.pallas_call(
        pack_kernel,
        out_shape=(edge_rows, edge_rows, jax.ShapeDtypeStruct((tiles, 24, 128), f32)),
        in_specs=[smem, smem, vmem, vmem],
        out_specs=(vmem, vmem, vmem),
        compiler_params=params,
        name="pack",
    )(place, seams, scaling, density)
    onward = [(i, (i + 1) % tiles) for i in range(tiles)]
    back = [(b, a) for a, b in onward]
    up = lax.ppermute(up, "tile", onward)
    down = lax.ppermute(down, "tile", back)
    message = lax.all_to_all(message, "tile", 0, 0)
    rows = 384 // members
    dual, marginal, weighted = pl.pallas_call(
        heat_kernel,
        out_shape=(field, field, jax.ShapeDtypeStruct((members, rows + 8, 128), f32)),
        in_specs=[smem, smem, smem] + [vmem] * 5,
        out_specs=(vmem, vmem, vmem),
        scratch_shapes=[
            pltpu.VMEM((FACES, TALL, WIDE), f32),
            pltpu.VMEM((FACES, TALL, WIDE), f32),
            pltpu.VMEM((2 * TALL, 384), f32),
            pltpu.VMEM((2, 128, 128), f32),
            pltpu.VMEM((SIDE, 128), f32),
            pltpu.VMEM((SIDE, 128), f32),
            pltpu.VMEM((96, SIDE), f32),
            pltpu.VMEM((96, SIDE), f32),
        ],
        compiler_params=params,
        name="heat",
    )(place, seams, member_weights, scaling, density, up, down, message)
    weighted = lax.all_to_all(weighted, "member", 0, 0)
    means = pl.pallas_call(
        mean_kernel,
        out_shape=jax.ShapeDtypeStruct((members, rows, 128), f32),
        in_specs=[vmem],
        out_specs=vmem,
        compiler_params=params,
        name="mean",
    )(weighted)
    means = lax.all_to_all(means, "member", 0, 0)
    fresh, barycenter = pl.pallas_call(
        update_kernel,
        out_shape=(field, field),
        in_specs=[vmem] * 3,
        out_specs=(vmem, vmem),
        compiler_params=params,
        name="update",
    )(means, scaling, marginal)
    return (fresh[None], dual[None], barycenter)


def solution(mesh):
    return jax.shard_map(
        body,
        mesh=mesh,
        in_specs=(
            P("member", None, "tile", None),
            P("member", None, "tile", None),
            P("member"),
            P(),
        ),
        out_specs=(
            P("member", None, "tile", None),
            P("member", None, "tile", None),
            P(None, "tile", None),
        ),
        check_vma=False,
    )
```

```python
import jax
import jax.numpy as jnp
from jax import lax
from jax.experimental import pallas as pl
from jax.experimental.pallas import tpu as pltpu
from jax.sharding import PartitionSpec as P

KAPPA = 0.24
STEPS = 4
FACES = 6
ROWS = 16
SIDE = 512
HALO = 8
TALL = ROWS + 2 * HALO


def iota(shape, dim):
    return lax.broadcasted_iota(jnp.int32, shape, dim)


def reverse_lanes(x):
    index = 127 - iota((8, 128), 1)
    tiles = [
        jnp.take_along_axis(x[:, at : at + 128], index, axis=1)
        for at in range(0, x.shape[1], 128)
    ]
    return jnp.concatenate(tiles[::-1], axis=1) if len(tiles) > 1 else tiles[0]


def column_strips(first, last):
    strips = None
    for g in range(FACES):
        a, b = first(g), last(g)
        lane = iota(a.shape, 1)
        moved = pltpu.roll(jnp.where(lane >= 64, b, a), 16 * g + 8, 1)
        strips = moved if strips is None else jnp.where(lane >= 16 * g, moved, strips)
    return strips


def spread(block):
    return [pltpu.roll(block, 96 - 32 * b, 1) for b in range(3)]


def unspread(b0, b1, b2):
    lane = iota((8, 128), 1)
    return jnp.where(
        lane < 32, pltpu.roll(b0, 32, 1), jnp.where(lane < 64, pltpu.roll(b1, 64, 1), pltpu.roll(b2, 96, 1))
    )


def pack_kernel(place, seams_at, scaling_at, density_at, up, down, message, seams, scaling, density, arrived):
    p = place[0]
    pairs = ((scaling_at, scaling), (density_at, density), (seams_at, seams))
    copies = [pltpu.make_async_copy(a, b, arrived.at[i]) for i, (a, b) in enumerate(pairs)]
    for copy in copies:
        copy.start()
    for copy in copies:
        copy.wait()
    count = message.shape[0]
    lane = iota((8, 128), 1)
    sub = iota((8, 128), 0)
    for g in range(FACES):
        up[g] = scaling[g, HALO:]
        up[FACES + g] = density[g, HALO:]
        down[g] = scaling[g, :HALO]
        down[FACES + g] = density[g, :HALO]
    vs = column_strips(lambda g: scaling[g, :, :128], lambda g: scaling[g, :, SIDE - 128 :])
    vd = column_strips(lambda g: density[g, :, :128], lambda g: density[g, :, SIDE - 128 :])
    tail = spread(vd[8:])
    head = (vs[:8], vs[8:], vd[:8])
    block = jnp.concatenate([jnp.where(lane < 96, head[b], tail[b]) for b in range(3)], axis=0)
    is_last = p == count - 1
    is_edge = (p == 0) | is_last

    @pl.when(jnp.logical_not(is_edge))
    def _():
        for q in range(count):
            message[q] = block

    @pl.when(is_edge)
    def _():
        message[0] = block
        message[count - 1] = block
        e = is_last.astype(jnp.int32)
        base = pl.multiple_of(e * 8, 8)
        own_s = jnp.where(is_last, vs[:8], vs[8:])
        own_d = jnp.where(is_last, vd[:8], vd[8:])
        far = jnp.where(is_last, pltpu.roll(own_d, 5, 0), pltpu.roll(own_d, 3, 0))
        free = jnp.where(is_last, (sub >= 5).astype(jnp.int32), (sub <= 2).astype(jnp.int32)) == 1
        lane16 = lane % 16
        coded = jnp.where(
            free & (lane16 < 4),
            pltpu.roll(far, 124, 1),
            jnp.where(free & (lane16 >= 12), pltpu.roll(far, 4, 1), own_s),
        )
        extra = spread(coded)
        pieces = []
        for g in range(FACES):
            turned = seams[2, e, g] == 1
            s = scaling[g, pl.ds(base, 8), :]
            d = density[g, pl.ds(base, 8), :]
            pieces.append((jnp.where(turned, reverse_lanes(s), s), jnp.where(turned, reverse_lanes(d), d)))
        sub_wide = iota((8, SIDE), 0)
        lane_wide = iota((8, SIDE), 1) % 128
        blocks = []
        for b in range(3):
            (s0, d0), (s1, d1) = pieces[2 * b], pieces[2 * b + 1]
            low = jnp.where(is_last, pltpu.roll(d0, 4, 0), d0)
            high = jnp.where(is_last, d1, pltpu.roll(d1, 4, 0))
            blocks.append((s0, s1, jnp.where(sub_wide < 4, low, high)))
        for t in range(3):
            tail_t = jnp.concatenate([extra[t]] * 4, axis=1)
            for r in range(8):
                moved = [pltpu.roll(blocks[b][t], (32 * b - 16 * r + 8) % SIDE, 1) for b in range(3)]
                full = jnp.where(
                    lane_wide < 32,
                    moved[0],
                    jnp.where(lane_wide < 64, moved[1], jnp.where(lane_wide < 96, moved[2], tail_t)),
                )
                for a in range(4):
                    q = 8 * a + r
                    if 0 < q < count - 1:
                        message[q, 8 * t : 8 * t + 8, :] = full[:, 128 * a : 128 * a + 128]


def diffuse(x):
    rows, lanes = x.shape
    vertical = pltpu.roll(x, 1, 0) + pltpu.roll(x, rows - 1, 0)
    lateral = pltpu.roll(x, 1, 1) + pltpu.roll(x, lanes - 1, 1)
    return x + KAPPA * ((vertical + lateral) - 4.0 * x)


def diffuse_strip(x, where):
    above = pltpu.roll(x, 1, 0)
    below = pltpu.roll(x, TALL - 1, 0)
    left = pltpu.roll(x, 1, 1)
    right = pltpu.roll(x, 127, 1)
    if where is not None:
        lane = iota((8, 128), 1)
        sub = iota((8, 128), 0)
        at, edge = (0, 8) if where == "first" else (24, 23)
        depth = 7 - sub if where == "first" else sub
        place = lane % 64
        start = lane - place
        line = jnp.broadcast_to(x[edge : edge + 1], (8, 128))
        index = jnp.where(place == 40, start + 39 - depth, jnp.where(place == 23, start + 24 + depth, 0))
        lateral = jnp.take_along_axis(line, index, axis=1)
        index = jnp.where(place >= 32, start + 40, start + 23)
        taken = jnp.take_along_axis(x[at : at + 8], index, axis=1)
        taken = jnp.where((place == 39 - depth) | (place == 24 + depth), taken, 0.0)
        vertical = jnp.sum(taken, axis=0, keepdims=True)
        ghost = (place >= 24) & (place < 40)
        fixed_left = jnp.where(place == 40, lateral, left[at : at + 8])
        fixed_right = jnp.where(place == 23, lateral, right[at : at + 8])
        if where == "first":
            left = jnp.concatenate([fixed_left, left[8:]], axis=0)
            right = jnp.concatenate([fixed_right, right[8:]], axis=0)
            block = jnp.where(ghost & (sub == 0), vertical, above[8:16])
            above = jnp.concatenate([above[:8], block, above[16:]], axis=0)
        else:
            left = jnp.concatenate([left[:24], fixed_left], axis=0)
            right = jnp.concatenate([right[:24], fixed_right], axis=0)
            block = jnp.where(ghost & (sub == 7), vertical, below[16:24])
            below = jnp.concatenate([below[:16], block, below[24:]], axis=0)
    return x + KAPPA * (((above + below) + (left + right)) - 4.0 * x)


def strip_lanes(first, last, h):
    lane = iota(first.shape, 1)
    return jnp.where(
        lane % 64 < 32, pltpu.roll(last, 24 + 64 * h, 1), pltpu.roll(first, 40 + 64 * h, 1)
    )


def swap_depth(x):
    lane = iota((8, 128), 1)
    index = lane + 7 - 2 * (lane % 8)
    return jnp.concatenate(
        [jnp.take_along_axis(x[at : at + 8], index, axis=1) for at in range(0, x.shape[0], 8)], axis=0
    )


def put_weighted(weighted, value, f, i, j):
    per = 48 // weighted.shape[0]
    t = 8 * f + 4 * i + j
    if isinstance(f, int):
        weighted[t // per, 8 * (t % per) : 8 * (t % per) + 8, :] = value
    else:
        at = pl.multiple_of(8 * lax.rem(t, per), 8)
        weighted[lax.div(t, per), pl.ds(at, 8), :] = value


def inner_kernel(weight, scaling, density, up, down, dual, marginal, weighted, strips, own):
    members = weighted.shape[0]
    per = 48 // members
    share = weight[0]
    for k in range(members):
        weighted[k, 8 * per :, :] = jnp.full((8, 128), share, jnp.float32)

    def face(f, carry):
        x = jnp.concatenate([up[f], scaling[f], down[f]], axis=0)
        for _ in range(STEPS):
            x = diffuse(x)
        y = jnp.concatenate([up[FACES + f], density[f], down[FACES + f]], axis=0) / x
        dual[f] = y[HALO : HALO + ROWS]
        for _ in range(STEPS):
            y = diffuse(y)
        m = scaling[f] * y[HALO : HALO + ROWS]
        marginal[f] = m
        scaled = share * jnp.log(m)
        for i in range(2):
            for j in range(4):
                put_weighted(weighted, scaled[8 * i : 8 * i + 8, 128 * j : 128 * j + 128], f, i, j)
        return carry

    lax.fori_loop(0, FACES, face, 0)
    for k, field in enumerate((scaling, density)):

        def ends(g, at):
            columns = slice(at, at + 128)
            return jnp.concatenate(
                [up[FACES * k + g, :, columns], field[g, :, columns], down[FACES * k + g, :, columns]], axis=0
            )

        firsts = [ends(g, 0) for g in range(FACES)]
        lasts = [ends(g, SIDE - 128) for g in range(FACES)]
        lane = iota((TALL, 128), 1)
        for t in range(3):
            strips[k, t] = jnp.where(
                lane < 64,
                strip_lanes(firsts[2 * t], lasts[2 * t], 0),
                strip_lanes(firsts[2 * t + 1], lasts[2 * t + 1], 1),
            )
        own[0, k * TALL : (k + 1) * TALL] = column_strips(lambda g: firsts[g], lambda g: lasts[g])
        own[1, k * TALL : (k + 1) * TALL] = swap_depth(own[0, k * TALL : (k + 1) * TALL])


def seam_kernel(
    place, seams, weight, scaling, density, up, down, message, strips, own, dual_in, marginal_in, weighted_in,
    dual, marginal, weighted, mixed, chunk, table_s, table_d, column_s, column_d, edge, work,
):
    q = place[0]
    count = message.shape[0]
    last = count - 1
    share = weight[0]
    lane = iota((8, 128), 1)
    sub = iota((8, 128), 0)
    is_edge = (q == 0) | (q == last)

    dual[...] = dual_in[...]
    marginal[...] = marginal_in[...]
    weighted[...] = weighted_in[...]

    def far_rows(p):
        return unspread(message[p, :8, :], message[p, 8:16, :], message[p, 16:24, :])

    mirror, upper, lower = last - q, jnp.minimum(last + 1 - q, last), jnp.maximum(last - 1 - q, 0)
    coded = far_rows(jnp.where(q == 1, last, 0))
    near = jnp.where(q == 1, pltpu.roll(coded, 3, 0), pltpu.roll(coded, 5, 0))
    coded_d = jnp.where(lane % 16 < 8, pltpu.roll(near, 4, 1), pltpu.roll(near, 124, 1))
    parts_s = (
        jnp.where(q == last - 1, coded, message[lower, 8:16, :]),
        message[mirror, :8, :],
        message[mirror, 8:16, :],
        jnp.where(q == 1, coded, message[upper, :8, :]),
    )
    parts_d = (
        jnp.where(q == last - 1, coded_d, far_rows(lower)),
        message[mirror, 16:24, :],
        far_rows(mirror),
        jnp.where(q == 1, coded_d, message[upper, 16:24, :]),
    )
    for base, parts in ((0, parts_s), (TALL, parts_d)):
        for block in range(4):
            for i in range(8):
                at = base + TALL - 1 - 8 * block - i
                mixed[2, at : at + 1, :] = parts[block][i : i + 1]

    chunk[:, 96:, :] = jnp.zeros((2, 32, 128), jnp.float32)

    @pl.when(jnp.logical_not(is_edge))
    def _():
        for e in range(2):
            p = e * last
            for g in range(FACES):
                b, h = g // 2, g % 2
                turn = (128 - 32 * b) % 128
                s = message[p, 8 * h : 8 * h + 8, :]
                d = message[p, 16:24, :]
                if turn:
                    s, d = pltpu.roll(s, turn, 1), pltpu.roll(d, turn, 1)
                if h != e:
                    d = pltpu.roll(d, 4, 0)
                at = 48 * e + 8 * g
                chunk[0, at : at + 8, :] = s
                chunk[1, at : at + 8, :] = d

    for is_first in (True, False):

        @pl.when(q == (0 if is_first else last))
        def _():
            e = 0 if is_first else 1

            def gather(p, carry):
                at = pl.multiple_of(16 * p, 16)
                column_s[pl.ds(at, 16), :] = message[p, :16, :]
                column_d[pl.ds(at, 8), :] = message[p, 16:24, :]
                column_d[pl.ds(at + 8, 8), :] = far_rows(p)
                return carry

            lax.fori_loop(0, count, gather, 0, unroll=8)
            for k, (table, columns, field) in enumerate(
                ((table_s, column_s, scaling), (table_d, column_d, density))
            ):
                for a in range(4):
                    rows = slice(128 * a, 128 * a + 128)
                    table[:128, rows] = jnp.transpose(columns[rows, :])
                for e_of in range(2):
                    for g in range(FACES):
                        if is_first:
                            rows = field[g, :HALO] if e_of == 0 else up[FACES * k + g]
                        else:
                            rows = down[FACES * k + g] if e_of == 0 else field[g, HALO:]
                        at = 48 * e_of + 8 * g
                        table[128 + at : 136 + at, :] = rows
                        turned = seams[2, e_of, g] == 1
                        a, b = rows[:, :128], rows[:, SIDE - 128 :]
                        if is_first:
                            piece = pltpu.roll(jnp.where(turned, reverse_lanes(b), a), 8, 1)
                        else:
                            piece = pltpu.roll(jnp.where(turned, reverse_lanes(a), b), 24, 1)
                        chunk[k, at : at + 8, :] = piece
                for f in range(FACES):
                    g, meets = seams[0, e, f], seams[1, e, f]
                    start = jnp.where(
                        meets >= 2, 16 * g + jnp.where(meets == 2, 8, 0), 128 + 48 * meets + 8 * g
                    )
                    rising = (meets % 2) == 0
                    for i in range(8):
                        depth = 7 - i if is_first else i
                        at = start + jnp.where(rising, depth, 7 - depth)
                        edge[k, f, i : i + 1, :] = table[pl.ds(at, 1), :]
                for f in range(FACES):
                    piece = edge[k, f]
                    edge[k, f] = jnp.where(seams[2, e, f] == 1, reverse_lanes(piece), piece)
                at = 0 if is_first else HALO + ROWS
                for t in range(3):
                    pieces = [
                        strip_lanes(edge[k, f, :, :128], edge[k, f, :, SIDE - 128 :], f % 2)
                        for f in (2 * t, 2 * t + 1)
                    ]
                    work[k, t, at : at + 8, :] = jnp.where(lane < 64, pieces[0], pieces[1])

    for k in range(2):
        mixed[4, k * TALL : (k + 1) * TALL, :] = jnp.transpose(chunk[k])[:TALL]
    for v in range(2):
        mixed[v] = own[v]
        if v:
            mixed[2 * v + 1] = swap_depth(mixed[2 * v])
    mixed[5] = swap_depth(mixed[4])

    lane_tall = iota((TALL, 128), 1)
    for k in range(2):
        for t in range(3):
            value = strips[k, t]
            for f in (2 * t, 2 * t + 1):
                for e in (2, 3):
                    g, meets, turned = seams[0, e, f], seams[1, e, f], seams[2, e, f]
                    of_column = meets >= 2
                    rising = (meets % 2) == 0
                    swapped = jnp.where(rising, 1 if e == 2 else 0, 0 if e == 2 else 1)
                    kind = jnp.where(of_column, 2 * turned, 4) + swapped
                    start = jnp.where(of_column, 16 * g + jnp.where(meets == 2, 8, 0), 48 * meets + 8 * g)
                    at = 64 * (f % 2) + (32 if e == 2 else 24)
                    moved = pltpu.roll(
                        mixed[kind, k * TALL : (k + 1) * TALL, :], jnp.bitwise_and(at - start + 128, 127), 1
                    )
                    value = jnp.where((lane_tall >= at) & (lane_tall < at + 8), moved, value)
            rows = [value[:8], value[8:24], value[24:]]
            work[k, t, 8:24, :] = rows[1]

            @pl.when(q != 0)
            def _():
                work[k, t, :8, :] = rows[0]

            @pl.when(q == 0)
            def _():
                work[k, t, :8, :] = jnp.where((lane % 64 >= 24) & (lane % 64 < 40), rows[0], work[k, t, :8, :])

            @pl.when(q != last)
            def _():
                work[k, t, 24:, :] = rows[2]

            @pl.when(q == last)
            def _():
                work[k, t, 24:, :] = jnp.where((lane % 64 >= 24) & (lane % 64 < 40), rows[2], work[k, t, 24:, :])

    for is_first in (True, False):

        @pl.when(q == (0 if is_first else last))
        def _():
            i = 0 if is_first else 1
            near_rows = slice(0, 8) if is_first else slice(8, 16)
            sub_wide = iota((8, SIDE), 0)
            kept = sub_wide >= 4 if is_first else sub_wide < 4

            def stack(ghost, inner):
                return jnp.concatenate([ghost, *inner] if is_first else [*inner, ghost], axis=0)

            def face(f, carry):
                x = stack(edge[0, f], [scaling[f, near_rows, :]])
                for _ in range(STEPS):
                    x = diffuse(x)
                y = stack(edge[1, f], [density[f, near_rows, :]]) / x
                old = dual_in[f]
                ghost, mine = (y[:8], y[8:]) if is_first else (y[8:], y[:8])
                mine = jnp.where(kept, old[near_rows], mine)
                dual[f, near_rows, :] = mine
                y = stack(ghost, [mine, old[8:]] if is_first else [old[:8], mine])
                for _ in range(STEPS):
                    y = diffuse(y)
                m = scaling[f, near_rows, :] * y[8:16]
                marginal[f, near_rows, :] = m
                scaled = share * jnp.log(m)
                for j in range(4):
                    put_weighted(weighted, scaled[:, 128 * j : 128 * j + 128], f, i, j)
                return carry

            lax.fori_loop(0, FACES, face, 0)

    def run(where):
        x = [work[0, t] for t in range(3)]
        for _ in range(STEPS):
            x = [diffuse_strip(v, where) for v in x]
        y = [work[1, t] / x[t] for t in range(3)]
        first = [v[HALO : HALO + ROWS] for v in y]
        for _ in range(STEPS):
            y = [diffuse_strip(v, where) for v in y]
        lane = iota((ROWS, 128), 1)
        per = 48 // weighted.shape[0]
        for t in range(3):
            m = work[0, t, HALO : HALO + ROWS, :] * y[t][HALO : HALO + ROWS]
            scaled = share * jnp.log(m)
            for h in range(2):
                f = 2 * t + h
                for j, turn, mask in ((0, 88 - 64 * h, lane < 8), (3, 104 - 64 * h, lane >= 120)):
                    columns = slice(128 * j, 128 * j + 128)
                    for ref, value in ((dual, first[t]), (marginal, m)):
                        ref[f, :, columns] = jnp.where(mask, pltpu.roll(value, turn, 1), ref[f, :, columns])
                    moved = pltpu.roll(scaled, turn, 1)
                    for i in range(2):
                        at = 8 * f + 4 * i + j
                        rows = slice(8 * (at % per), 8 * (at % per) + 8)
                        weighted[at // per, rows, :] = jnp.where(
                            mask[:8], moved[8 * i : 8 * i + 8], weighted[at // per, rows, :]
                        )

    @pl.when(q == 0)
    def _():
        run("first")

    @pl.when(q == last)
    def _():
        run("last")

    @pl.when(jnp.logical_not(is_edge))
    def _():
        run(None)


def mean_kernel(parts, result):
    members, rows = result.shape[0], result.shape[1]
    total = parts[0]
    for k in range(1, members):
        total = total + parts[k]
    mean = total[:rows] / total[rows : rows + 1]
    value = jnp.exp(mean)
    for k in range(members):
        result[k] = value


def update_kernel(parts, scaling, marginal, fresh, barycenter):
    members = parts.shape[0]
    per = 48 // members
    for f in range(FACES):
        for i in range(2):
            for j in range(4):
                t = 8 * f + 4 * i + j
                at = 8 * (t % per)
                value = parts[t // per, at : at + 8, :]
                rows, columns = slice(8 * i, 8 * i + 8), slice(128 * j, 128 * j + 128)
                barycenter[f, rows, columns] = value
                fresh[f, rows, columns] = scaling[f, rows, columns] * value / marginal[f, rows, columns]


def body(density, scaling, member_weights, seams):
    tiles = lax.axis_size("tile")
    members = lax.axis_size("member")
    scaling = scaling[0]
    density = density[0]
    place = lax.axis_index("tile").astype(jnp.int32).reshape(1)
    f32 = jnp.float32
    vmem = pl.BlockSpec(memory_space=pltpu.VMEM)
    smem = pl.BlockSpec(memory_space=pltpu.SMEM)
    field = jax.ShapeDtypeStruct((FACES, ROWS, SIDE), f32)
    edge_rows = jax.ShapeDtypeStruct((2 * FACES, HALO, SIDE), f32)
    params = pltpu.CompilerParams(vmem_limit_bytes=24 * 1024 * 1024)
    up, down, message = pl.pallas_call(
        pack_kernel,
        out_shape=(edge_rows, edge_rows, jax.ShapeDtypeStruct((tiles, 24, 128), f32)),
        in_specs=[smem] + [pl.BlockSpec(memory_space=pltpu.HBM)] * 3,
        out_specs=(vmem, vmem, vmem),
        scratch_shapes=[
            pltpu.SMEM(seams.shape, jnp.int32),
            pltpu.VMEM(scaling.shape, f32),
            pltpu.VMEM(density.shape, f32),
            pltpu.SemaphoreType.DMA((3,)),
        ],
        compiler_params=params,
        name="pack",
    )(place, seams, scaling, density)
    onward = [(i, (i + 1) % tiles) for i in range(tiles)]
    back = [(b, a) for a, b in onward]
    up = lax.ppermute(up, "tile", onward)
    down = lax.ppermute(down, "tile", back)
    message = lax.all_to_all(message, "tile", 0, 0)
    rows = 384 // members
    sums = jax.ShapeDtypeStruct((members, rows + 8, 128), f32)
    dual, marginal, weighted, strips, own = pl.pallas_call(
        inner_kernel,
        out_shape=(
            field, field, sums,
            jax.ShapeDtypeStruct((2, 3, TALL, 128), f32),
            jax.ShapeDtypeStruct((2, 2 * TALL, 128), f32),
        ),
        in_specs=[smem] + [vmem] * 4,
        out_specs=(vmem,) * 5,
        compiler_params=params,
        name="inner",
    )(member_weights, scaling, density, up, down)
    dual, marginal, weighted = pl.pallas_call(
        seam_kernel,
        out_shape=(field, field, sums),
        in_specs=[smem, smem, smem] + [vmem] * 10,
        out_specs=(vmem, vmem, vmem),
        scratch_shapes=[
            pltpu.VMEM((6, 2 * TALL, 128), f32),
            pltpu.VMEM((2, 128, 128), f32),
            pltpu.VMEM((224, SIDE), f32),
            pltpu.VMEM((224, SIDE), f32),
            pltpu.VMEM((SIDE, 128), f32),
            pltpu.VMEM((SIDE, 128), f32),
            pltpu.VMEM((2, FACES, HALO, SIDE), f32),
            pltpu.VMEM((2, 3, TALL, 128), f32),
        ],
        compiler_params=params,
        name="seam",
    )(place, seams, member_weights, scaling, density, up, down, message, strips, own, dual, marginal, weighted)
    weighted = lax.all_to_all(weighted, "member", 0, 0)
    means = pl.pallas_call(
        mean_kernel,
        out_shape=jax.ShapeDtypeStruct((members, rows, 128), f32),
        in_specs=[vmem],
        out_specs=vmem,
        compiler_params=params,
        name="mean",
    )(weighted)
    means = lax.all_to_all(means, "member", 0, 0)
    fresh, barycenter = pl.pallas_call(
        update_kernel,
        out_shape=(field, field),
        in_specs=[vmem] * 3,
        out_specs=(vmem, vmem),
        compiler_params=params,
        name="update",
    )(means, scaling, marginal)
    return (fresh[None], dual[None], barycenter)


def solution(mesh):
    return jax.shard_map(
        body,
        mesh=mesh,
        in_specs=(
            P("member", None, "tile", None),
            P("member", None, "tile", None),
            P("member"),
            P(),
        ),
        out_specs=(
            P("member", None, "tile", None),
            P("member", None, "tile", None),
            P(None, "tile", None),
        ),
        check_vma=False,
    )
```

```python
import jax
import jax.numpy as jnp
from jax import lax
from jax.experimental import pallas as pl
from jax.experimental.pallas import tpu as pltpu
from jax.sharding import PartitionSpec as P

KAPPA = 0.24
STEPS = 4
FACES = 6
ROWS = 16
SIDE = 512
HALO = 8
TALL = ROWS + 2 * HALO


LONG = pl.CostEstimate(flops=10**10, bytes_accessed=10**10, transcendentals=0)


def iota(shape, dim):
    return lax.broadcasted_iota(jnp.int32, shape, dim)


def reverse_lanes(x):
    index = 127 - iota((8, 128), 1)
    tiles = [
        jnp.take_along_axis(x[:, at : at + 128], index, axis=1)
        for at in range(0, x.shape[1], 128)
    ]
    return jnp.concatenate(tiles[::-1], axis=1) if len(tiles) > 1 else tiles[0]


def column_strips(first, last):
    strips = None
    for g in range(FACES):
        a, b = first(g), last(g)
        lane = iota(a.shape, 1)
        moved = pltpu.roll(jnp.where(lane >= 64, b, a), 16 * g + 8, 1)
        strips = moved if strips is None else jnp.where(lane >= 16 * g, moved, strips)
    return strips


def spread(block):
    return [pltpu.roll(block, 96 - 32 * b, 1) for b in range(3)]


def unspread(b0, b1, b2):
    lane = iota((8, 128), 1)
    return jnp.where(
        lane < 32, pltpu.roll(b0, 32, 1), jnp.where(lane < 64, pltpu.roll(b1, 64, 1), pltpu.roll(b2, 96, 1))
    )


def rows_kernel(scaling, density, up, down, arrived):
    copies = []
    for i, (field, at) in enumerate(((scaling, 0), (density, FACES))):
        faces = pl.ds(at, FACES)
        copies.append(pltpu.make_async_copy(field.at[:, pl.ds(HALO, HALO)], up.at[faces], arrived.at[2 * i]))
        copies.append(pltpu.make_async_copy(field.at[:, pl.ds(0, HALO)], down.at[faces], arrived.at[2 * i + 1]))
    for copy in copies:
        copy.start()
    for copy in copies:
        copy.wait()


def pack_kernel(place, seams, scaling, density, message):
    p = place[0]
    count = message.shape[0]
    lane = iota((8, 128), 1)
    sub = iota((8, 128), 0)
    vs = column_strips(lambda g: scaling[g, :, :128], lambda g: scaling[g, :, SIDE - 128 :])
    vd = column_strips(lambda g: density[g, :, :128], lambda g: density[g, :, SIDE - 128 :])
    tail = spread(vd[8:])
    head = (vs[:8], vs[8:], vd[:8])
    block = jnp.concatenate([jnp.where(lane < 96, head[b], tail[b]) for b in range(3)], axis=0)
    is_last = p == count - 1
    is_edge = (p == 0) | is_last

    @pl.when(jnp.logical_not(is_edge))
    def _():
        for q in range(count):
            message[q] = block

    @pl.when(is_edge)
    def _():
        message[0] = block
        message[count - 1] = block
        e = is_last.astype(jnp.int32)
        base = pl.multiple_of(e * 8, 8)
        own_s = jnp.where(is_last, vs[:8], vs[8:])
        own_d = jnp.where(is_last, vd[:8], vd[8:])
        far = jnp.where(is_last, pltpu.roll(own_d, 5, 0), pltpu.roll(own_d, 3, 0))
        free = jnp.where(is_last, (sub >= 5).astype(jnp.int32), (sub <= 2).astype(jnp.int32)) == 1
        lane16 = lane % 16
        coded = jnp.where(
            free & (lane16 < 4),
            pltpu.roll(far, 124, 1),
            jnp.where(free & (lane16 >= 12), pltpu.roll(far, 4, 1), own_s),
        )
        extra = spread(coded)
        pieces = []
        for g in range(FACES):
            turned = seams[2, e, g] == 1
            s = scaling[g, pl.ds(base, 8), :]
            d = density[g, pl.ds(base, 8), :]
            pieces.append((jnp.where(turned, reverse_lanes(s), s), jnp.where(turned, reverse_lanes(d), d)))
        sub_wide = iota((8, SIDE), 0)
        lane_wide = iota((8, SIDE), 1) % 128
        blocks = []
        for b in range(3):
            (s0, d0), (s1, d1) = pieces[2 * b], pieces[2 * b + 1]
            low = jnp.where(is_last, pltpu.roll(d0, 4, 0), d0)
            high = jnp.where(is_last, d1, pltpu.roll(d1, 4, 0))
            blocks.append((s0, s1, jnp.where(sub_wide < 4, low, high)))
        for t in range(3):
            tail_t = jnp.concatenate([extra[t]] * 4, axis=1)
            for r in range(8):
                moved = [pltpu.roll(blocks[b][t], (32 * b - 16 * r + 8) % SIDE, 1) for b in range(3)]
                full = jnp.where(
                    lane_wide < 32,
                    moved[0],
                    jnp.where(lane_wide < 64, moved[1], jnp.where(lane_wide < 96, moved[2], tail_t)),
                )
                for a in range(4):
                    q = 8 * a + r
                    if 0 < q < count - 1:
                        message[q, 8 * t : 8 * t + 8, :] = full[:, 128 * a : 128 * a + 128]


def diffuse(x):
    rows, lanes = x.shape
    vertical = pltpu.roll(x, 1, 0) + pltpu.roll(x, rows - 1, 0)
    lateral = pltpu.roll(x, 1, 1) + pltpu.roll(x, lanes - 1, 1)
    return x + KAPPA * ((vertical + lateral) - 4.0 * x)


def diffuse_strip(x, where):
    above = pltpu.roll(x, 1, 0)
    below = pltpu.roll(x, TALL - 1, 0)
    left = pltpu.roll(x, 1, 1)
    right = pltpu.roll(x, 127, 1)
    if where is not None:
        lane = iota((8, 128), 1)
        sub = iota((8, 128), 0)
        at, edge = (0, 8) if where == "first" else (24, 23)
        depth = 7 - sub if where == "first" else sub
        place = lane % 64
        start = lane - place
        line = jnp.broadcast_to(x[edge : edge + 1], (8, 128))
        index = jnp.where(place == 40, start + 39 - depth, jnp.where(place == 23, start + 24 + depth, 0))
        lateral = jnp.take_along_axis(line, index, axis=1)
        index = jnp.where(place >= 32, start + 40, start + 23)
        taken = jnp.take_along_axis(x[at : at + 8], index, axis=1)
        taken = jnp.where((place == 39 - depth) | (place == 24 + depth), taken, 0.0)
        vertical = jnp.sum(taken, axis=0, keepdims=True)
        ghost = (place >= 24) & (place < 40)
        fixed_left = jnp.where(place == 40, lateral, left[at : at + 8])
        fixed_right = jnp.where(place == 23, lateral, right[at : at + 8])
        if where == "first":
            left = jnp.concatenate([fixed_left, left[8:]], axis=0)
            right = jnp.concatenate([fixed_right, right[8:]], axis=0)
            block = jnp.where(ghost & (sub == 0), vertical, above[8:16])
            above = jnp.concatenate([above[:8], block, above[16:]], axis=0)
        else:
            left = jnp.concatenate([left[:24], fixed_left], axis=0)
            right = jnp.concatenate([right[:24], fixed_right], axis=0)
            block = jnp.where(ghost & (sub == 7), vertical, below[16:24])
            below = jnp.concatenate([below[:16], block, below[24:]], axis=0)
    return x + KAPPA * (((above + below) + (left + right)) - 4.0 * x)


def strip_lanes(first, last, h):
    lane = iota(first.shape, 1)
    return jnp.where(
        lane % 64 < 32, pltpu.roll(last, 24 + 64 * h, 1), pltpu.roll(first, 40 + 64 * h, 1)
    )


def swap_depth(x):
    lane = iota((8, 128), 1)
    index = lane + 7 - 2 * (lane % 8)
    return jnp.concatenate(
        [jnp.take_along_axis(x[at : at + 8], index, axis=1) for at in range(0, x.shape[0], 8)], axis=0
    )


def put_weighted(weighted, value, f, i, j):
    per = 48 // weighted.shape[0]
    t = 8 * f + 4 * i + j
    if isinstance(f, int):
        weighted[t // per, 8 * (t % per) : 8 * (t % per) + 8, :] = value
    else:
        at = pl.multiple_of(8 * lax.rem(t, per), 8)
        weighted[lax.div(t, per), pl.ds(at, 8), :] = value


def inner_kernel(weight, scaling, density, up, down, dual, marginal, weighted, strips, own):
    members = weighted.shape[0]
    per = 48 // members
    share = weight[0]
    for k in range(members):
        weighted[k, 8 * per :, :] = jnp.full((8, 128), share, jnp.float32)

    def face(f, carry):
        x = jnp.concatenate([up[f], scaling[f], down[f]], axis=0)
        for _ in range(STEPS):
            x = diffuse(x)
        y = jnp.concatenate([up[FACES + f], density[f], down[FACES + f]], axis=0) / x
        dual[f] = y[HALO : HALO + ROWS]
        for _ in range(STEPS):
            y = diffuse(y)
        m = scaling[f] * y[HALO : HALO + ROWS]
        marginal[f] = m
        scaled = share * jnp.log(m)
        for i in range(2):
            for j in range(4):
                put_weighted(weighted, scaled[8 * i : 8 * i + 8, 128 * j : 128 * j + 128], f, i, j)
        return carry

    lax.fori_loop(0, FACES, face, 0)
    for k, field in enumerate((scaling, density)):

        def ends(g, at):
            columns = slice(at, at + 128)
            return jnp.concatenate(
                [up[FACES * k + g, :, columns], field[g, :, columns], down[FACES * k + g, :, columns]], axis=0
            )

        firsts = [ends(g, 0) for g in range(FACES)]
        lasts = [ends(g, SIDE - 128) for g in range(FACES)]
        lane = iota((TALL, 128), 1)
        for t in range(3):
            strips[k, t] = jnp.where(
                lane < 64,
                strip_lanes(firsts[2 * t], lasts[2 * t], 0),
                strip_lanes(firsts[2 * t + 1], lasts[2 * t + 1], 1),
            )
        own[0, k * TALL : (k + 1) * TALL] = column_strips(lambda g: firsts[g], lambda g: lasts[g])
        own[1, k * TALL : (k + 1) * TALL] = swap_depth(own[0, k * TALL : (k + 1) * TALL])


def seam_kernel(
    place, seams, weight, scaling, density, up, down, message, strips, own, dual_in, marginal_in, weighted_in,
    dual, marginal, weighted, mixed, chunk, table_s, table_d, column_s, column_d, edge, work,
):
    q = place[0]
    count = message.shape[0]
    last = count - 1
    share = weight[0]
    lane = iota((8, 128), 1)
    sub = iota((8, 128), 0)
    is_edge = (q == 0) | (q == last)

    dual[...] = dual_in[...]
    marginal[...] = marginal_in[...]
    weighted[...] = weighted_in[...]

    def far_rows(p):
        return unspread(message[p, :8, :], message[p, 8:16, :], message[p, 16:24, :])

    mirror, upper, lower = last - q, jnp.minimum(last + 1 - q, last), jnp.maximum(last - 1 - q, 0)
    coded = far_rows(jnp.where(q == 1, last, 0))
    near = jnp.where(q == 1, pltpu.roll(coded, 3, 0), pltpu.roll(coded, 5, 0))
    coded_d = jnp.where(lane % 16 < 8, pltpu.roll(near, 4, 1), pltpu.roll(near, 124, 1))
    parts_s = (
        jnp.where(q == last - 1, coded, message[lower, 8:16, :]),
        message[mirror, :8, :],
        message[mirror, 8:16, :],
        jnp.where(q == 1, coded, message[upper, :8, :]),
    )
    parts_d = (
        jnp.where(q == last - 1, coded_d, far_rows(lower)),
        message[mirror, 16:24, :],
        far_rows(mirror),
        jnp.where(q == 1, coded_d, message[upper, 16:24, :]),
    )
    for base, parts in ((0, parts_s), (TALL, parts_d)):
        for block in range(4):
            for i in range(8):
                at = base + TALL - 1 - 8 * block - i
                mixed[2, at : at + 1, :] = parts[block][i : i + 1]

    chunk[:, 96:, :] = jnp.zeros((2, 32, 128), jnp.float32)

    @pl.when(jnp.logical_not(is_edge))
    def _():
        for e in range(2):
            p = e * last
            for g in range(FACES):
                b, h = g // 2, g % 2
                turn = (128 - 32 * b) % 128
                s = message[p, 8 * h : 8 * h + 8, :]
                d = message[p, 16:24, :]
                if turn:
                    s, d = pltpu.roll(s, turn, 1), pltpu.roll(d, turn, 1)
                if h != e:
                    d = pltpu.roll(d, 4, 0)
                at = 48 * e + 8 * g
                chunk[0, at : at + 8, :] = s
                chunk[1, at : at + 8, :] = d

    for is_first in (True, False):

        @pl.when(q == (0 if is_first else last))
        def _():
            e = 0 if is_first else 1

            def gather(p, carry):
                at = pl.multiple_of(16 * p, 16)
                column_s[pl.ds(at, 16), :] = message[p, :16, :]
                column_d[pl.ds(at, 8), :] = message[p, 16:24, :]
                column_d[pl.ds(at + 8, 8), :] = far_rows(p)
                return carry

            lax.fori_loop(0, count, gather, 0, unroll=8)
            for k, (table, columns, field) in enumerate(
                ((table_s, column_s, scaling), (table_d, column_d, density))
            ):
                for a in range(4):
                    rows = slice(128 * a, 128 * a + 128)
                    table[:128, rows] = jnp.transpose(columns[rows, :])
                for e_of in range(2):
                    for g in range(FACES):
                        if is_first:
                            rows = field[g, :HALO] if e_of == 0 else up[FACES * k + g]
                        else:
                            rows = down[FACES * k + g] if e_of == 0 else field[g, HALO:]
                        at = 48 * e_of + 8 * g
                        table[128 + at : 136 + at, :] = rows
                        turned = seams[2, e_of, g] == 1
                        a, b = rows[:, :128], rows[:, SIDE - 128 :]
                        if is_first:
                            piece = pltpu.roll(jnp.where(turned, reverse_lanes(b), a), 8, 1)
                        else:
                            piece = pltpu.roll(jnp.where(turned, reverse_lanes(a), b), 24, 1)
                        chunk[k, at : at + 8, :] = piece
                for f in range(FACES):
                    g, meets = seams[0, e, f], seams[1, e, f]
                    start = jnp.where(
                        meets >= 2, 16 * g + jnp.where(meets == 2, 8, 0), 128 + 48 * meets + 8 * g
                    )
                    rising = (meets % 2) == 0
                    for i in range(8):
                        depth = 7 - i if is_first else i
                        at = start + jnp.where(rising, depth, 7 - depth)
                        edge[k, f, i : i + 1, :] = table[pl.ds(at, 1), :]
                for f in range(FACES):
                    piece = edge[k, f]
                    edge[k, f] = jnp.where(seams[2, e, f] == 1, reverse_lanes(piece), piece)
                at = 0 if is_first else HALO + ROWS
                for t in range(3):
                    pieces = [
                        strip_lanes(edge[k, f, :, :128], edge[k, f, :, SIDE - 128 :], f % 2)
                        for f in (2 * t, 2 * t + 1)
                    ]
                    work[k, t, at : at + 8, :] = jnp.where(lane < 64, pieces[0], pieces[1])

    for k in range(2):
        mixed[4, k * TALL : (k + 1) * TALL, :] = jnp.transpose(chunk[k])[:TALL]
    for v in range(2):
        mixed[v] = own[v]
        if v:
            mixed[2 * v + 1] = swap_depth(mixed[2 * v])
    mixed[5] = swap_depth(mixed[4])

    lane_tall = iota((TALL, 128), 1)
    for k in range(2):
        for t in range(3):
            value = strips[k, t]
            for f in (2 * t, 2 * t + 1):
                for e in (2, 3):
                    g, meets, turned = seams[0, e, f], seams[1, e, f], seams[2, e, f]
                    of_column = meets >= 2
                    rising = (meets % 2) == 0
                    swapped = jnp.where(rising, 1 if e == 2 else 0, 0 if e == 2 else 1)
                    kind = jnp.where(of_column, 2 * turned, 4) + swapped
                    start = jnp.where(of_column, 16 * g + jnp.where(meets == 2, 8, 0), 48 * meets + 8 * g)
                    at = 64 * (f % 2) + (32 if e == 2 else 24)
                    moved = pltpu.roll(
                        mixed[kind, k * TALL : (k + 1) * TALL, :], jnp.bitwise_and(at - start + 128, 127), 1
                    )
                    value = jnp.where((lane_tall >= at) & (lane_tall < at + 8), moved, value)
            rows = [value[:8], value[8:24], value[24:]]
            work[k, t, 8:24, :] = rows[1]

            @pl.when(q != 0)
            def _():
                work[k, t, :8, :] = rows[0]

            @pl.when(q == 0)
            def _():
                work[k, t, :8, :] = jnp.where((lane % 64 >= 24) & (lane % 64 < 40), rows[0], work[k, t, :8, :])

            @pl.when(q != last)
            def _():
                work[k, t, 24:, :] = rows[2]

            @pl.when(q == last)
            def _():
                work[k, t, 24:, :] = jnp.where((lane % 64 >= 24) & (lane % 64 < 40), rows[2], work[k, t, 24:, :])

    for is_first in (True, False):

        @pl.when(q == (0 if is_first else last))
        def _():
            i = 0 if is_first else 1
            near_rows = slice(0, 8) if is_first else slice(8, 16)
            sub_wide = iota((8, SIDE), 0)
            kept = sub_wide >= 4 if is_first else sub_wide < 4

            def stack(ghost, inner):
                return jnp.concatenate([ghost, *inner] if is_first else [*inner, ghost], axis=0)

            def face(f, carry):
                x = stack(edge[0, f], [scaling[f, near_rows, :]])
                for _ in range(STEPS):
                    x = diffuse(x)
                y = stack(edge[1, f], [density[f, near_rows, :]]) / x
                old = dual_in[f]
                ghost, mine = (y[:8], y[8:]) if is_first else (y[8:], y[:8])
                mine = jnp.where(kept, old[near_rows], mine)
                dual[f, near_rows, :] = mine
                y = stack(ghost, [mine, old[8:]] if is_first else [old[:8], mine])
                for _ in range(STEPS):
                    y = diffuse(y)
                m = scaling[f, near_rows, :] * y[8:16]
                marginal[f, near_rows, :] = m
                scaled = share * jnp.log(m)
                for j in range(4):
                    put_weighted(weighted, scaled[:, 128 * j : 128 * j + 128], f, i, j)
                return carry

            lax.fori_loop(0, FACES, face, 0)

    def run(where):
        x = [work[0, t] for t in range(3)]
        for _ in range(STEPS):
            x = [diffuse_strip(v, where) for v in x]
        y = [work[1, t] / x[t] for t in range(3)]
        first = [v[HALO : HALO + ROWS] for v in y]
        for _ in range(STEPS):
            y = [diffuse_strip(v, where) for v in y]
        lane = iota((ROWS, 128), 1)
        per = 48 // weighted.shape[0]
        for t in range(3):
            m = work[0, t, HALO : HALO + ROWS, :] * y[t][HALO : HALO + ROWS]
            scaled = share * jnp.log(m)
            for h in range(2):
                f = 2 * t + h
                for j, turn, mask in ((0, 88 - 64 * h, lane < 8), (3, 104 - 64 * h, lane >= 120)):
                    columns = slice(128 * j, 128 * j + 128)
                    for ref, value in ((dual, first[t]), (marginal, m)):
                        ref[f, :, columns] = jnp.where(mask, pltpu.roll(value, turn, 1), ref[f, :, columns])
                    moved = pltpu.roll(scaled, turn, 1)
                    for i in range(2):
                        at = 8 * f + 4 * i + j
                        rows = slice(8 * (at % per), 8 * (at % per) + 8)
                        weighted[at // per, rows, :] = jnp.where(
                            mask[:8], moved[8 * i : 8 * i + 8], weighted[at // per, rows, :]
                        )

    @pl.when(q == 0)
    def _():
        run("first")

    @pl.when(q == last)
    def _():
        run("last")

    @pl.when(jnp.logical_not(is_edge))
    def _():
        run(None)


def mean_kernel(parts, result):
    members, rows = result.shape[0], result.shape[1]
    total = parts[0]
    for k in range(1, members):
        total = total + parts[k]
    mean = total[:rows] / total[rows : rows + 1]
    value = jnp.exp(mean)
    for k in range(members):
        result[k] = value


def update_kernel(parts, scaling, marginal, fresh, barycenter):
    members = parts.shape[0]
    per = 48 // members
    for f in range(FACES):
        for i in range(2):
            for j in range(4):
                t = 8 * f + 4 * i + j
                at = 8 * (t % per)
                value = parts[t // per, at : at + 8, :]
                rows, columns = slice(8 * i, 8 * i + 8), slice(128 * j, 128 * j + 128)
                barycenter[f, rows, columns] = value
                fresh[f, rows, columns] = scaling[f, rows, columns] * value / marginal[f, rows, columns]


def body(density, scaling, member_weights, seams):
    tiles = lax.axis_size("tile")
    members = lax.axis_size("member")
    scaling = scaling[0]
    density = density[0]
    place = lax.axis_index("tile").astype(jnp.int32).reshape(1)
    f32 = jnp.float32
    vmem = pl.BlockSpec(memory_space=pltpu.VMEM)
    smem = pl.BlockSpec(memory_space=pltpu.SMEM)
    field = jax.ShapeDtypeStruct((FACES, ROWS, SIDE), f32)
    edge_rows = jax.ShapeDtypeStruct((2 * FACES, HALO, SIDE), f32)
    params = pltpu.CompilerParams(vmem_limit_bytes=24 * 1024 * 1024)
    anywhere = pl.BlockSpec(memory_space=pl.ANY)
    up, down = pl.pallas_call(
        rows_kernel,
        out_shape=(edge_rows, edge_rows),
        in_specs=[anywhere, anywhere],
        out_specs=(anywhere, anywhere),
        scratch_shapes=[pltpu.SemaphoreType.DMA((4,))],
        name="rows",
    )(scaling, density)
    onward = [(i, (i + 1) % tiles) for i in range(tiles)]
    back = [(b, a) for a, b in onward]
    up = lax.ppermute(up, "tile", onward)
    down = lax.ppermute(down, "tile", back)
    message = pl.pallas_call(
        pack_kernel,
        out_shape=jax.ShapeDtypeStruct((tiles, 24, 128), f32),
        in_specs=[smem, smem, vmem, vmem],
        out_specs=vmem,
        compiler_params=params,
        cost_estimate=LONG,
        name="pack",
    )(place, seams, scaling, density)
    message = lax.all_to_all(message, "tile", 0, 0)
    rows = 384 // members
    sums = jax.ShapeDtypeStruct((members, rows + 8, 128), f32)
    dual, marginal, weighted, strips, own = pl.pallas_call(
        inner_kernel,
        out_shape=(
            field, field, sums,
            jax.ShapeDtypeStruct((2, 3, TALL, 128), f32),
            jax.ShapeDtypeStruct((2, 2 * TALL, 128), f32),
        ),
        in_specs=[smem] + [vmem] * 4,
        out_specs=(vmem,) * 5,
        compiler_params=params,
        cost_estimate=LONG,
        name="inner",
    )(member_weights, scaling, density, up, down)
    dual, marginal, weighted = pl.pallas_call(
        seam_kernel,
        out_shape=(field, field, sums),
        in_specs=[smem, smem, smem] + [vmem] * 10,
        out_specs=(vmem, vmem, vmem),
        scratch_shapes=[
            pltpu.VMEM((6, 2 * TALL, 128), f32),
            pltpu.VMEM((2, 128, 128), f32),
            pltpu.VMEM((224, SIDE), f32),
            pltpu.VMEM((224, SIDE), f32),
            pltpu.VMEM((SIDE, 128), f32),
            pltpu.VMEM((SIDE, 128), f32),
            pltpu.VMEM((2, FACES, HALO, SIDE), f32),
            pltpu.VMEM((2, 3, TALL, 128), f32),
        ],
        compiler_params=params,
        name="seam",
    )(place, seams, member_weights, scaling, density, up, down, message, strips, own, dual, marginal, weighted)
    weighted = lax.all_to_all(weighted, "member", 0, 0)
    means = pl.pallas_call(
        mean_kernel,
        out_shape=jax.ShapeDtypeStruct((members, rows, 128), f32),
        in_specs=[vmem],
        out_specs=vmem,
        compiler_params=params,
        name="mean",
    )(weighted)
    means = lax.all_to_all(means, "member", 0, 0)
    fresh, barycenter = pl.pallas_call(
        update_kernel,
        out_shape=(field, field),
        in_specs=[vmem] * 3,
        out_specs=(vmem, vmem),
        compiler_params=params,
        name="update",
    )(means, scaling, marginal)
    return (fresh[None], dual[None], barycenter)


def solution(mesh):
    return jax.shard_map(
        body,
        mesh=mesh,
        in_specs=(
            P("member", None, "tile", None),
            P("member", None, "tile", None),
            P("member"),
            P(),
        ),
        out_specs=(
            P("member", None, "tile", None),
            P("member", None, "tile", None),
            P(None, "tile", None),
        ),
        check_vma=False,
    )
```

```python
import jax
import jax.numpy as jnp
from jax import lax
from jax.experimental import pallas as pl
from jax.experimental.pallas import tpu as pltpu
from jax.sharding import PartitionSpec as P

KAPPA = 0.24
STEPS = 4
FACES = 6
ROWS = 16
SIDE = 512
HALO = 8
TALL = ROWS + 2 * HALO


def iota(shape, dim):
    return lax.broadcasted_iota(jnp.int32, shape, dim)


def reverse_lanes(x):
    index = 127 - iota((8, 128), 1)
    tiles = [
        jnp.take_along_axis(x[:, at : at + 128], index, axis=1)
        for at in range(0, x.shape[1], 128)
    ]
    return jnp.concatenate(tiles[::-1], axis=1) if len(tiles) > 1 else tiles[0]


def column_strips(first, last):
    strips = None
    for g in range(FACES):
        a, b = first(g), last(g)
        lane = iota(a.shape, 1)
        moved = pltpu.roll(jnp.where(lane >= 64, b, a), 16 * g + 8, 1)
        strips = moved if strips is None else jnp.where(lane >= 16 * g, moved, strips)
    return strips


def spread(block):
    return [pltpu.roll(block, 96 - 32 * b, 1) for b in range(3)]


def unspread(b0, b1, b2):
    lane = iota((8, 128), 1)
    return jnp.where(
        lane < 32, pltpu.roll(b0, 32, 1), jnp.where(lane < 64, pltpu.roll(b1, 64, 1), pltpu.roll(b2, 96, 1))
    )


def join_halves(low, high):
    return jnp.where(iota(low.shape, 0) < 4, low, high)


def halo_rows(rows, k, g, is_up):
    if k == 0:
        return rows[g]
    block = rows[FACES + g // 2]
    return pltpu.roll(block, 4, 0) if (g % 2 == 0) == is_up else block


def pack_kernel(place, seams, scaling, density, up, down, message):
    p = place[0]
    count = message.shape[0]
    lane = iota((8, 128), 1)
    sub = iota((8, 128), 0)
    for g in range(FACES):
        up[g] = scaling[g, HALO:]
        down[g] = scaling[g, :HALO]
    for b in range(3):
        up[FACES + b] = join_halves(
            pltpu.roll(density[2 * b, HALO:], 4, 0), density[2 * b + 1, HALO:]
        )
        down[FACES + b] = join_halves(
            density[2 * b, :HALO], pltpu.roll(density[2 * b + 1, :HALO], 4, 0)
        )
    vs = column_strips(lambda g: scaling[g, :, :128], lambda g: scaling[g, :, SIDE - 128 :])
    vd = column_strips(lambda g: density[g, :, :128], lambda g: density[g, :, SIDE - 128 :])
    tail = spread(vd[8:])
    head = (vs[:8], vs[8:], vd[:8])
    block = jnp.concatenate([jnp.where(lane < 96, head[b], tail[b]) for b in range(3)], axis=0)
    is_last = p == count - 1
    is_edge = (p == 0) | is_last

    @pl.when(jnp.logical_not(is_edge))
    def _():
        for q in range(count):
            message[q] = block

    @pl.when(is_edge)
    def _():
        message[0] = block
        message[count - 1] = block
        e = is_last.astype(jnp.int32)
        base = pl.multiple_of(e * 8, 8)
        own_s = jnp.where(is_last, vs[:8], vs[8:])
        own_d = jnp.where(is_last, vd[:8], vd[8:])
        far = jnp.where(is_last, pltpu.roll(own_d, 5, 0), pltpu.roll(own_d, 3, 0))
        free = jnp.where(is_last, (sub >= 5).astype(jnp.int32), (sub <= 2).astype(jnp.int32)) == 1
        lane16 = lane % 16
        coded = jnp.where(
            free & (lane16 < 4),
            pltpu.roll(far, 124, 1),
            jnp.where(free & (lane16 >= 12), pltpu.roll(far, 4, 1), own_s),
        )
        extra = spread(coded)
        pieces = []
        for g in range(FACES):
            turned = seams[2, e, g] == 1
            s = scaling[g, pl.ds(base, 8), :]
            d = density[g, pl.ds(base, 8), :]
            pieces.append((jnp.where(turned, reverse_lanes(s), s), jnp.where(turned, reverse_lanes(d), d)))
        sub_wide = iota((8, SIDE), 0)
        lane_wide = iota((8, SIDE), 1) % 128
        blocks = []
        for b in range(3):
            (s0, d0), (s1, d1) = pieces[2 * b], pieces[2 * b + 1]
            low = jnp.where(is_last, pltpu.roll(d0, 4, 0), d0)
            high = jnp.where(is_last, d1, pltpu.roll(d1, 4, 0))
            blocks.append((s0, s1, jnp.where(sub_wide < 4, low, high)))
        for t in range(3):
            tail_t = jnp.concatenate([extra[t]] * 4, axis=1)
            for r in range(8):
                moved = [pltpu.roll(blocks[b][t], (32 * b - 16 * r + 8) % SIDE, 1) for b in range(3)]
                full = jnp.where(
                    lane_wide < 32,
                    moved[0],
                    jnp.where(lane_wide < 64, moved[1], jnp.where(lane_wide < 96, moved[2], tail_t)),
                )
                for a in range(4):
                    q = 8 * a + r
                    if 0 < q < count - 1:
                        message[q, 8 * t : 8 * t + 8, :] = full[:, 128 * a : 128 * a + 128]


def diffuse(x):
    rows, lanes = x.shape
    vertical = pltpu.roll(x, 1, 0) + pltpu.roll(x, rows - 1, 0)
    lateral = pltpu.roll(x, 1, 1) + pltpu.roll(x, lanes - 1, 1)
    return x + KAPPA * ((vertical + lateral) - 4.0 * x)


def diffuse_strip(x, where):
    above = pltpu.roll(x, 1, 0)
    below = pltpu.roll(x, TALL - 1, 0)
    left = pltpu.roll(x, 1, 1)
    right = pltpu.roll(x, 127, 1)
    if where is not None:
        lane = iota((8, 128), 1)
        sub = iota((8, 128), 0)
        at, edge = (0, 8) if where == "first" else (24, 23)
        depth = 7 - sub if where == "first" else sub
        place = lane % 64
        start = lane - place
        line = jnp.broadcast_to(x[edge : edge + 1], (8, 128))
        index = jnp.where(place == 40, start + 39 - depth, jnp.where(place == 23, start + 24 + depth, 0))
        lateral = jnp.take_along_axis(line, index, axis=1)
        index = jnp.where(place >= 32, start + 40, start + 23)
        taken = jnp.take_along_axis(x[at : at + 8], index, axis=1)
        taken = jnp.where((place == 39 - depth) | (place == 24 + depth), taken, 0.0)
        vertical = jnp.sum(taken, axis=0, keepdims=True)
        ghost = (place >= 24) & (place < 40)
        fixed_left = jnp.where(place == 40, lateral, left[at : at + 8])
        fixed_right = jnp.where(place == 23, lateral, right[at : at + 8])
        if where == "first":
            left = jnp.concatenate([fixed_left, left[8:]], axis=0)
            right = jnp.concatenate([fixed_right, right[8:]], axis=0)
            block = jnp.where(ghost & (sub == 0), vertical, above[8:16])
            above = jnp.concatenate([above[:8], block, above[16:]], axis=0)
        else:
            left = jnp.concatenate([left[:24], fixed_left], axis=0)
            right = jnp.concatenate([right[:24], fixed_right], axis=0)
            block = jnp.where(ghost & (sub == 7), vertical, below[16:24])
            below = jnp.concatenate([below[:16], block, below[24:]], axis=0)
    return x + KAPPA * (((above + below) + (left + right)) - 4.0 * x)


def strip_lanes(first, last, h):
    lane = iota(first.shape, 1)
    return jnp.where(
        lane % 64 < 32, pltpu.roll(last, 24 + 64 * h, 1), pltpu.roll(first, 40 + 64 * h, 1)
    )


def swap_depth(x):
    lane = iota((8, 128), 1)
    index = lane + 7 - 2 * (lane % 8)
    return jnp.concatenate(
        [jnp.take_along_axis(x[at : at + 8], index, axis=1) for at in range(0, x.shape[0], 8)], axis=0
    )


def put_weighted(weighted, value, f, i, j):
    per = 48 // weighted.shape[0]
    t = 8 * f + 4 * i + j
    if isinstance(f, int):
        weighted[t // per, 8 * (t % per) : 8 * (t % per) + 8, :] = value
    else:
        at = pl.multiple_of(8 * lax.rem(t, per), 8)
        weighted[lax.div(t, per), pl.ds(at, 8), :] = value


def heat_kernel(
    place, seams, weight, scaling, density, up, down, message,
    dual, marginal, weighted, mixed, chunk, table_s, table_d, column_s, column_d, edge, work,
):
    q = place[0]
    count = message.shape[0]
    last = count - 1
    share = weight[0]
    lane = iota((8, 128), 1)
    sub = iota((8, 128), 0)
    is_edge = (q == 0) | (q == last)

    per = 48 // weighted.shape[0]
    for k in range(weighted.shape[0]):
        weighted[k, 8 * per :, :] = jnp.full((8, 128), share, jnp.float32)

    def far_rows(p):
        return unspread(message[p, :8, :], message[p, 8:16, :], message[p, 16:24, :])

    mirror, upper, lower = last - q, jnp.minimum(last + 1 - q, last), jnp.maximum(last - 1 - q, 0)
    coded = far_rows(jnp.where(q == 1, last, 0))
    near = jnp.where(q == 1, pltpu.roll(coded, 3, 0), pltpu.roll(coded, 5, 0))
    coded_d = jnp.where(lane % 16 < 8, pltpu.roll(near, 4, 1), pltpu.roll(near, 124, 1))
    parts_s = (
        jnp.where(q == last - 1, coded, message[lower, 8:16, :]),
        message[mirror, :8, :],
        message[mirror, 8:16, :],
        jnp.where(q == 1, coded, message[upper, :8, :]),
    )
    parts_d = (
        jnp.where(q == last - 1, coded_d, far_rows(lower)),
        message[mirror, 16:24, :],
        far_rows(mirror),
        jnp.where(q == 1, coded_d, message[upper, 16:24, :]),
    )
    for base, parts in ((0, parts_s), (TALL, parts_d)):
        for block in range(4):
            for i in range(8):
                at = base + TALL - 1 - 8 * block - i
                mixed[2, at : at + 1, :] = parts[block][i : i + 1]

    chunk[:, 96:, :] = jnp.zeros((2, 32, 128), jnp.float32)

    @pl.when(jnp.logical_not(is_edge))
    def _():
        for e in range(2):
            p = e * last
            for g in range(FACES):
                b, h = g // 2, g % 2
                turn = (128 - 32 * b) % 128
                s = message[p, 8 * h : 8 * h + 8, :]
                d = message[p, 16:24, :]
                if turn:
                    s, d = pltpu.roll(s, turn, 1), pltpu.roll(d, turn, 1)
                if h != e:
                    d = pltpu.roll(d, 4, 0)
                at = 48 * e + 8 * g
                chunk[0, at : at + 8, :] = s
                chunk[1, at : at + 8, :] = d

    for is_first in (True, False):

        @pl.when(q == (0 if is_first else last))
        def _():
            e = 0 if is_first else 1

            def gather(p, carry):
                at = pl.multiple_of(16 * p, 16)
                column_s[pl.ds(at, 16), :] = message[p, :16, :]
                column_d[pl.ds(at, 8), :] = message[p, 16:24, :]
                column_d[pl.ds(at + 8, 8), :] = far_rows(p)
                return carry

            lax.fori_loop(0, count, gather, 0, unroll=8)
            for k, (table, columns, field) in enumerate(
                ((table_s, column_s, scaling), (table_d, column_d, density))
            ):
                for a in range(4):
                    rows = slice(128 * a, 128 * a + 128)
                    table[:128, rows] = jnp.transpose(columns[rows, :])
                for e_of in range(2):
                    for g in range(FACES):
                        if is_first:
                            rows = field[g, :HALO] if e_of == 0 else halo_rows(up, k, g, True)
                        else:
                            rows = halo_rows(down, k, g, False) if e_of == 0 else field[g, HALO:]
                        at = 48 * e_of + 8 * g
                        table[128 + at : 136 + at, :] = rows
                        turned = seams[2, e_of, g] == 1
                        a, b = rows[:, :128], rows[:, SIDE - 128 :]
                        if is_first:
                            piece = pltpu.roll(jnp.where(turned, reverse_lanes(b), a), 8, 1)
                        else:
                            piece = pltpu.roll(jnp.where(turned, reverse_lanes(a), b), 24, 1)
                        chunk[k, at : at + 8, :] = piece
                for f in range(FACES):
                    g, meets = seams[0, e, f], seams[1, e, f]
                    start = jnp.where(
                        meets >= 2, 16 * g + jnp.where(meets == 2, 8, 0), 128 + 48 * meets + 8 * g
                    )
                    rising = (meets % 2) == 0
                    for i in range(8):
                        depth = 7 - i if is_first else i
                        at = start + jnp.where(rising, depth, 7 - depth)
                        edge[k, f, i : i + 1, :] = table[pl.ds(at, 1), :]
                for f in range(FACES):
                    piece = edge[k, f]
                    edge[k, f] = jnp.where(seams[2, e, f] == 1, reverse_lanes(piece), piece)
                at = 0 if is_first else HALO + ROWS
                for t in range(3):
                    pieces = [
                        strip_lanes(edge[k, f, :, :128], edge[k, f, :, SIDE - 128 :], f % 2)
                        for f in (2 * t, 2 * t + 1)
                    ]
                    work[k, t, at : at + 8, :] = jnp.where(lane < 64, pieces[0], pieces[1])

    for k in range(2):
        mixed[4, k * TALL : (k + 1) * TALL, :] = jnp.transpose(chunk[k])[:TALL]
    lane_tall = iota((TALL, 128), 1)
    strips = []
    for k, field in enumerate((scaling, density)):

        def ends(g, at):
            columns = slice(at, at + 128)
            above = up.at[:, :, columns]
            below = down.at[:, :, columns]
            return jnp.concatenate(
                [halo_rows(above, k, g, True), field[g, :, columns], halo_rows(below, k, g, False)], axis=0
            )

        firsts = [ends(g, 0) for g in range(FACES)]
        lasts = [ends(g, SIDE - 128) for g in range(FACES)]
        strips.append([
            jnp.where(
                lane_tall < 64,
                strip_lanes(firsts[2 * t], lasts[2 * t], 0),
                strip_lanes(firsts[2 * t + 1], lasts[2 * t + 1], 1),
            )
            for t in range(3)
        ])
        mixed[0, k * TALL : (k + 1) * TALL, :] = column_strips(lambda g: firsts[g], lambda g: lasts[g])
    for v in (0, 2, 4):
        mixed[v + 1] = swap_depth(mixed[v])

    for k in range(2):
        for t in range(3):
            value = strips[k][t]
            for f in (2 * t, 2 * t + 1):
                for e in (2, 3):
                    g, meets, turned = seams[0, e, f], seams[1, e, f], seams[2, e, f]
                    of_column = meets >= 2
                    rising = (meets % 2) == 0
                    swapped = jnp.where(rising, 1 if e == 2 else 0, 0 if e == 2 else 1)
                    kind = jnp.where(of_column, 2 * turned, 4) + swapped
                    start = jnp.where(of_column, 16 * g + jnp.where(meets == 2, 8, 0), 48 * meets + 8 * g)
                    at = 64 * (f % 2) + (32 if e == 2 else 24)
                    moved = pltpu.roll(
                        mixed[kind, k * TALL : (k + 1) * TALL, :], jnp.bitwise_and(at - start + 128, 127), 1
                    )
                    value = jnp.where((lane_tall >= at) & (lane_tall < at + 8), moved, value)
            rows = [value[:8], value[8:24], value[24:]]
            work[k, t, 8:24, :] = rows[1]

            @pl.when(q != 0)
            def _():
                work[k, t, :8, :] = rows[0]

            @pl.when(q == 0)
            def _():
                work[k, t, :8, :] = jnp.where((lane % 64 >= 24) & (lane % 64 < 40), rows[0], work[k, t, :8, :])

            @pl.when(q != last)
            def _():
                work[k, t, 24:, :] = rows[2]

            @pl.when(q == last)
            def _():
                work[k, t, 24:, :] = jnp.where((lane % 64 >= 24) & (lane % 64 < 40), rows[2], work[k, t, 24:, :])

    def run(where):
        for f in range(FACES):
            above = [edge[k, f] if where == "first" else halo_rows(up, k, f, True) for k in range(2)]
            below = [edge[k, f] if where == "last" else halo_rows(down, k, f, False) for k in range(2)]
            x = jnp.concatenate([above[0], scaling[f], below[0]], axis=0)
            for _ in range(STEPS):
                x = diffuse(x)
            y = jnp.concatenate([above[1], density[f], below[1]], axis=0) / x
            dual[f] = y[HALO : HALO + ROWS]
            for _ in range(STEPS):
                y = diffuse(y)
            m = scaling[f] * y[HALO : HALO + ROWS]
            marginal[f] = m
            scaled = share * jnp.log(m)
            for i in range(2):
                for j in range(4):
                    put_weighted(weighted, scaled[8 * i : 8 * i + 8, 128 * j : 128 * j + 128], f, i, j)
        x = [work[0, t] for t in range(3)]
        for _ in range(STEPS):
            x = [diffuse_strip(v, where) for v in x]
        y = [work[1, t] / x[t] for t in range(3)]
        first = [v[HALO : HALO + ROWS] for v in y]
        for _ in range(STEPS):
            y = [diffuse_strip(v, where) for v in y]
        lane = iota((ROWS, 128), 1)
        for t in range(3):
            m = work[0, t, HALO : HALO + ROWS, :] * y[t][HALO : HALO + ROWS]
            scaled = share * jnp.log(m)
            for h in range(2):
                f = 2 * t + h
                for j, turn, mask in ((0, 88 - 64 * h, lane < 8), (3, 104 - 64 * h, lane >= 120)):
                    columns = slice(128 * j, 128 * j + 128)
                    for ref, value in ((dual, first[t]), (marginal, m)):
                        ref[f, :, columns] = jnp.where(mask, pltpu.roll(value, turn, 1), ref[f, :, columns])
                    moved = pltpu.roll(scaled, turn, 1)
                    for i in range(2):
                        at = 8 * f + 4 * i + j
                        rows = slice(8 * (at % per), 8 * (at % per) + 8)
                        weighted[at // per, rows, :] = jnp.where(
                            mask[:8], moved[8 * i : 8 * i + 8], weighted[at // per, rows, :]
                        )

    @pl.when(q == 0)
    def _():
        run("first")

    @pl.when(q == last)
    def _():
        run("last")

    @pl.when(jnp.logical_not(is_edge))
    def _():
        run(None)


def mean_kernel(parts, result):
    members, rows = result.shape[0], result.shape[1]
    total = parts[0]
    for k in range(1, members):
        total = total + parts[k]
    mean = total[:rows] / total[rows : rows + 1]
    value = jnp.exp(mean)
    for k in range(members):
        result[k] = value


def update_kernel(parts, scaling, marginal, fresh, barycenter):
    members = parts.shape[0]
    per = 48 // members
    for f in range(FACES):
        for i in range(2):
            for j in range(4):
                t = 8 * f + 4 * i + j
                at = 8 * (t % per)
                value = parts[t // per, at : at + 8, :]
                rows, columns = slice(8 * i, 8 * i + 8), slice(128 * j, 128 * j + 128)
                barycenter[f, rows, columns] = value
                fresh[f, rows, columns] = scaling[f, rows, columns] * value / marginal[f, rows, columns]


def body(density, scaling, member_weights, seams):
    tiles = lax.axis_size("tile")
    members = lax.axis_size("member")
    scaling = scaling[0]
    density = density[0]
    place = lax.axis_index("tile").astype(jnp.int32).reshape(1)
    f32 = jnp.float32
    vmem = pl.BlockSpec(memory_space=pltpu.VMEM)
    smem = pl.BlockSpec(memory_space=pltpu.SMEM)
    field = jax.ShapeDtypeStruct((FACES, ROWS, SIDE), f32)
    edge_rows = jax.ShapeDtypeStruct((FACES + FACES // 2, HALO, SIDE), f32)
    params = pltpu.CompilerParams(vmem_limit_bytes=24 * 1024 * 1024)
    up, down, message = pl.pallas_call(
        pack_kernel,
        out_shape=(edge_rows, edge_rows, jax.ShapeDtypeStruct((tiles, 24, 128), f32)),
        in_specs=[smem, smem, vmem, vmem],
        out_specs=(vmem, vmem, vmem),
        compiler_params=params,
        name="pack",
    )(place, seams, scaling, density)
    onward = [(i, (i + 1) % tiles) for i in range(tiles)]
    back = [(b, a) for a, b in onward]
    up = lax.ppermute(up, "tile", onward)
    down = lax.ppermute(down, "tile", back)
    message = lax.all_to_all(message, "tile", 0, 0)
    rows = 384 // members
    sums = jax.ShapeDtypeStruct((members, rows + 8, 128), f32)
    dual, marginal, weighted = pl.pallas_call(
        heat_kernel,
        out_shape=(field, field, sums),
        in_specs=[smem, smem, smem] + [vmem] * 5,
        out_specs=(vmem, vmem, vmem),
        scratch_shapes=[
            pltpu.VMEM((6, 2 * TALL, 128), f32),
            pltpu.VMEM((2, 128, 128), f32),
            pltpu.VMEM((224, SIDE), f32),
            pltpu.VMEM((224, SIDE), f32),
            pltpu.VMEM((SIDE, 128), f32),
            pltpu.VMEM((SIDE, 128), f32),
            pltpu.VMEM((2, FACES, HALO, SIDE), f32),
            pltpu.VMEM((2, 3, TALL, 128), f32),
        ],
        compiler_params=params,
        name="heat",
    )(place, seams, member_weights, scaling, density, up, down, message)
    weighted = lax.all_to_all(weighted, "member", 0, 0)
    means = pl.pallas_call(
        mean_kernel,
        out_shape=jax.ShapeDtypeStruct((members, rows, 128), f32),
        in_specs=[vmem],
        out_specs=vmem,
        compiler_params=params,
        name="mean",
    )(weighted)
    means = lax.all_to_all(means, "member", 0, 0)
    fresh, barycenter = pl.pallas_call(
        update_kernel,
        out_shape=(field, field),
        in_specs=[vmem] * 3,
        out_specs=(vmem, vmem),
        compiler_params=params,
        name="update",
    )(means, scaling, marginal)
    return (fresh[None], dual[None], barycenter)


def solution(mesh):
    return jax.shard_map(
        body,
        mesh=mesh,
        in_specs=(
            P("member", None, "tile", None),
            P("member", None, "tile", None),
            P("member"),
            P(),
        ),
        out_specs=(
            P("member", None, "tile", None),
            P("member", None, "tile", None),
            P(None, "tile", None),
        ),
        check_vma=False,
    )
```

```python
import jax
import jax.numpy as jnp
from jax import lax
from jax.experimental import pallas as pl
from jax.experimental.pallas import tpu as pltpu
from jax.sharding import PartitionSpec as P

KAPPA = 0.24
STEPS = 4
FACES = 6
ROWS = 16
SIDE = 512
HALO = 8
TALL = ROWS + 2 * HALO


def iota(shape, dim):
    return lax.broadcasted_iota(jnp.int32, shape, dim)


def reverse_lanes(x):
    index = 127 - iota((8, 128), 1)
    tiles = [
        jnp.take_along_axis(x[:, at : at + 128], index, axis=1)
        for at in range(0, x.shape[1], 128)
    ]
    return jnp.concatenate(tiles[::-1], axis=1) if len(tiles) > 1 else tiles[0]


def column_strips(first, last):
    strips = None
    for g in range(FACES):
        a, b = first(g), last(g)
        lane = iota(a.shape, 1)
        moved = pltpu.roll(jnp.where(lane >= 64, b, a), 16 * g + 8, 1)
        strips = moved if strips is None else jnp.where(lane >= 16 * g, moved, strips)
    return strips


def spread(block):
    return [pltpu.roll(block, 96 - 32 * b, 1) for b in range(3)]


def unspread(b0, b1, b2):
    lane = iota((8, 128), 1)
    return jnp.where(
        lane < 32, pltpu.roll(b0, 32, 1), jnp.where(lane < 64, pltpu.roll(b1, 64, 1), pltpu.roll(b2, 96, 1))
    )


def join_halves(low, high):
    return jnp.where(iota(low.shape, 0) < 4, low, high)


def halo_rows(rows, k, g, is_up):
    if k == 0:
        return rows[g]
    block = rows[FACES + g // 2]
    return pltpu.roll(block, 4, 0) if (g % 2 == 0) == is_up else block


def pack_kernel(place, seams_at, scaling_at, density_at, beside, across, message, seams, scaling, density, arrived):
    p = place[0]
    pairs = ((scaling_at, scaling), (density_at, density), (seams_at, seams))
    copies = [pltpu.make_async_copy(a, b, arrived.at[i]) for i, (a, b) in enumerate(pairs)]
    for copy in copies:
        copy.start()
    for copy in copies:
        copy.wait()
    is_even = lax.rem(p, 2) == 0
    count = message.shape[0]
    lane = iota((8, 128), 1)
    sub = iota((8, 128), 0)
    ups = [scaling[g, HALO:] for g in range(FACES)]
    downs = [scaling[g, :HALO] for g in range(FACES)]
    for b in range(3):
        d0, d1 = density[2 * b], density[2 * b + 1]
        ups.append(join_halves(pltpu.roll(d0[HALO:], 4, 0), d1[HALO:]))
        downs.append(join_halves(d0[:HALO], pltpu.roll(d1[:HALO], 4, 0)))
    for b, (u, d) in enumerate(zip(ups, downs)):
        beside[b] = jnp.where(is_even, u, d)
        across[b] = jnp.where(is_even, d, u)
    vs = column_strips(lambda g: scaling[g, :, :128], lambda g: scaling[g, :, SIDE - 128 :])
    vd = column_strips(lambda g: density[g, :, :128], lambda g: density[g, :, SIDE - 128 :])
    tail = spread(vd[8:])
    head = (vs[:8], vs[8:], vd[:8])
    block = jnp.concatenate([jnp.where(lane < 96, head[b], tail[b]) for b in range(3)], axis=0)
    is_last = p == count - 1
    is_edge = (p == 0) | is_last

    @pl.when(jnp.logical_not(is_edge))
    def _():
        for q in range(count):
            message[q] = block

    @pl.when(is_edge)
    def _():
        message[0] = block
        message[count - 1] = block
        e = is_last.astype(jnp.int32)
        base = pl.multiple_of(e * 8, 8)
        own_s = jnp.where(is_last, vs[:8], vs[8:])
        own_d = jnp.where(is_last, vd[:8], vd[8:])
        far = jnp.where(is_last, pltpu.roll(own_d, 5, 0), pltpu.roll(own_d, 3, 0))
        free = jnp.where(is_last, (sub >= 5).astype(jnp.int32), (sub <= 2).astype(jnp.int32)) == 1
        lane16 = lane % 16
        coded = jnp.where(
            free & (lane16 < 4),
            pltpu.roll(far, 124, 1),
            jnp.where(free & (lane16 >= 12), pltpu.roll(far, 4, 1), own_s),
        )
        extra = spread(coded)
        pieces = []
        for g in range(FACES):
            turned = seams[2, e, g] == 1
            s = scaling[g, pl.ds(base, 8), :]
            d = density[g, pl.ds(base, 8), :]
            pieces.append((jnp.where(turned, reverse_lanes(s), s), jnp.where(turned, reverse_lanes(d), d)))
        sub_wide = iota((8, SIDE), 0)
        lane_wide = iota((8, SIDE), 1) % 128
        blocks = []
        for b in range(3):
            (s0, d0), (s1, d1) = pieces[2 * b], pieces[2 * b + 1]
            low = jnp.where(is_last, pltpu.roll(d0, 4, 0), d0)
            high = jnp.where(is_last, d1, pltpu.roll(d1, 4, 0))
            blocks.append((s0, s1, jnp.where(sub_wide < 4, low, high)))
        for t in range(3):
            tail_t = jnp.concatenate([extra[t]] * 4, axis=1)
            for r in range(8):
                moved = [pltpu.roll(blocks[b][t], (32 * b - 16 * r + 8) % SIDE, 1) for b in range(3)]
                full = jnp.where(
                    lane_wide < 32,
                    moved[0],
                    jnp.where(lane_wide < 64, moved[1], jnp.where(lane_wide < 96, moved[2], tail_t)),
                )
                for a in range(4):
                    q = 8 * a + r
                    if 0 < q < count - 1:
                        message[q, 8 * t : 8 * t + 8, :] = full[:, 128 * a : 128 * a + 128]


def diffuse(x):
    rows, lanes = x.shape
    vertical = pltpu.roll(x, 1, 0) + pltpu.roll(x, rows - 1, 0)
    lateral = pltpu.roll(x, 1, 1) + pltpu.roll(x, lanes - 1, 1)
    return x + KAPPA * ((vertical + lateral) - 4.0 * x)


def diffuse_strip(x, where):
    above = pltpu.roll(x, 1, 0)
    below = pltpu.roll(x, TALL - 1, 0)
    left = pltpu.roll(x, 1, 1)
    right = pltpu.roll(x, 127, 1)
    if where is not None:
        lane = iota((8, 128), 1)
        sub = iota((8, 128), 0)
        at, edge = (0, 8) if where == "first" else (24, 23)
        depth = 7 - sub if where == "first" else sub
        place = lane % 64
        start = lane - place
        line = jnp.broadcast_to(x[edge : edge + 1], (8, 128))
        index = jnp.where(place == 40, start + 39 - depth, jnp.where(place == 23, start + 24 + depth, 0))
        lateral = jnp.take_along_axis(line, index, axis=1)
        index = jnp.where(place >= 32, start + 40, start + 23)
        taken = jnp.take_along_axis(x[at : at + 8], index, axis=1)
        taken = jnp.where((place == 39 - depth) | (place == 24 + depth), taken, 0.0)
        vertical = jnp.sum(taken, axis=0, keepdims=True)
        ghost = (place >= 24) & (place < 40)
        fixed_left = jnp.where(place == 40, lateral, left[at : at + 8])
        fixed_right = jnp.where(place == 23, lateral, right[at : at + 8])
        if where == "first":
            left = jnp.concatenate([fixed_left, left[8:]], axis=0)
            right = jnp.concatenate([fixed_right, right[8:]], axis=0)
            block = jnp.where(ghost & (sub == 0), vertical, above[8:16])
            above = jnp.concatenate([above[:8], block, above[16:]], axis=0)
        else:
            left = jnp.concatenate([left[:24], fixed_left], axis=0)
            right = jnp.concatenate([right[:24], fixed_right], axis=0)
            block = jnp.where(ghost & (sub == 7), vertical, below[16:24])
            below = jnp.concatenate([below[:16], block, below[24:]], axis=0)
    return x + KAPPA * (((above + below) + (left + right)) - 4.0 * x)


def strip_lanes(first, last, h):
    lane = iota(first.shape, 1)
    return jnp.where(
        lane % 64 < 32, pltpu.roll(last, 24 + 64 * h, 1), pltpu.roll(first, 40 + 64 * h, 1)
    )


def swap_depth(x):
    lane = iota((8, 128), 1)
    index = lane + 7 - 2 * (lane % 8)
    return jnp.concatenate(
        [jnp.take_along_axis(x[at : at + 8], index, axis=1) for at in range(0, x.shape[0], 8)], axis=0
    )


def put_weighted(weighted, value, f, i, j):
    per = 48 // weighted.shape[0]
    t = 8 * f + 4 * i + j
    if isinstance(f, int):
        weighted[t // per, 8 * (t % per) : 8 * (t % per) + 8, :] = value
    else:
        at = pl.multiple_of(8 * lax.rem(t, per), 8)
        weighted[lax.div(t, per), pl.ds(at, 8), :] = value


def heat_kernel(
    place, seams, weight, scaling, density, beside, across, message,
    dual, marginal, weighted, up, down, mixed, chunk, table_s, table_d, column_s, column_d, edge, work,
):
    q = place[0]
    count = message.shape[0]
    last = count - 1
    is_even = lax.rem(q, 2) == 0
    for b in range(FACES + FACES // 2):
        up[b] = jnp.where(is_even, across[b], beside[b])
        down[b] = jnp.where(is_even, beside[b], across[b])
    share = weight[0]
    lane = iota((8, 128), 1)
    sub = iota((8, 128), 0)
    is_edge = (q == 0) | (q == last)

    per = 48 // weighted.shape[0]
    for k in range(weighted.shape[0]):
        weighted[k, 8 * per :, :] = jnp.full((8, 128), share, jnp.float32)

    def far_rows(p):
        return unspread(message[p, :8, :], message[p, 8:16, :], message[p, 16:24, :])

    mirror, upper, lower = last - q, jnp.minimum(last + 1 - q, last), jnp.maximum(last - 1 - q, 0)
    coded = far_rows(jnp.where(q == 1, last, 0))
    near = jnp.where(q == 1, pltpu.roll(coded, 3, 0), pltpu.roll(coded, 5, 0))
    coded_d = jnp.where(lane % 16 < 8, pltpu.roll(near, 4, 1), pltpu.roll(near, 124, 1))
    parts_s = (
        jnp.where(q == last - 1, coded, message[lower, 8:16, :]),
        message[mirror, :8, :],
        message[mirror, 8:16, :],
        jnp.where(q == 1, coded, message[upper, :8, :]),
    )
    parts_d = (
        jnp.where(q == last - 1, coded_d, far_rows(lower)),
        message[mirror, 16:24, :],
        far_rows(mirror),
        jnp.where(q == 1, coded_d, message[upper, 16:24, :]),
    )
    for base, parts in ((0, parts_s), (TALL, parts_d)):
        for block in range(4):
            for i in range(8):
                at = base + TALL - 1 - 8 * block - i
                mixed[2, at : at + 1, :] = parts[block][i : i + 1]

    chunk[:, 96:, :] = jnp.zeros((2, 32, 128), jnp.float32)

    @pl.when(jnp.logical_not(is_edge))
    def _():
        for e in range(2):
            p = e * last
            for g in range(FACES):
                b, h = g // 2, g % 2
                turn = (128 - 32 * b) % 128
                s = message[p, 8 * h : 8 * h + 8, :]
                d = message[p, 16:24, :]
                if turn:
                    s, d = pltpu.roll(s, turn, 1), pltpu.roll(d, turn, 1)
                if h != e:
                    d = pltpu.roll(d, 4, 0)
                at = 48 * e + 8 * g
                chunk[0, at : at + 8, :] = s
                chunk[1, at : at + 8, :] = d

    for is_first in (True, False):

        @pl.when(q == (0 if is_first else last))
        def _():
            e = 0 if is_first else 1

            def gather(p, carry):
                at = pl.multiple_of(16 * p, 16)
                column_s[pl.ds(at, 16), :] = message[p, :16, :]
                column_d[pl.ds(at, 8), :] = message[p, 16:24, :]
                column_d[pl.ds(at + 8, 8), :] = far_rows(p)
                return carry

            lax.fori_loop(0, count, gather, 0, unroll=8)
            for k, (table, columns, field) in enumerate(
                ((table_s, column_s, scaling), (table_d, column_d, density))
            ):
                for a in range(4):
                    rows = slice(128 * a, 128 * a + 128)
                    table[:128, rows] = jnp.transpose(columns[rows, :])
                for e_of in range(2):
                    for g in range(FACES):
                        if is_first:
                            rows = field[g, :HALO] if e_of == 0 else halo_rows(up, k, g, True)
                        else:
                            rows = halo_rows(down, k, g, False) if e_of == 0 else field[g, HALO:]
                        at = 48 * e_of + 8 * g
                        table[128 + at : 136 + at, :] = rows
                        turned = seams[2, e_of, g] == 1
                        a, b = rows[:, :128], rows[:, SIDE - 128 :]
                        if is_first:
                            piece = pltpu.roll(jnp.where(turned, reverse_lanes(b), a), 8, 1)
                        else:
                            piece = pltpu.roll(jnp.where(turned, reverse_lanes(a), b), 24, 1)
                        chunk[k, at : at + 8, :] = piece
                for f in range(FACES):
                    g, meets = seams[0, e, f], seams[1, e, f]
                    start = jnp.where(
                        meets >= 2, 16 * g + jnp.where(meets == 2, 8, 0), 128 + 48 * meets + 8 * g
                    )
                    rising = (meets % 2) == 0
                    for i in range(8):
                        depth = 7 - i if is_first else i
                        at = start + jnp.where(rising, depth, 7 - depth)
                        edge[k, f, i : i + 1, :] = table[pl.ds(at, 1), :]
                for f in range(FACES):
                    piece = edge[k, f]
                    edge[k, f] = jnp.where(seams[2, e, f] == 1, reverse_lanes(piece), piece)
                at = 0 if is_first else HALO + ROWS
                for t in range(3):
                    pieces = [
                        strip_lanes(edge[k, f, :, :128], edge[k, f, :, SIDE - 128 :], f % 2)
                        for f in (2 * t, 2 * t + 1)
                    ]
                    work[k, t, at : at + 8, :] = jnp.where(lane < 64, pieces[0], pieces[1])

    for k in range(2):
        mixed[4, k * TALL : (k + 1) * TALL, :] = jnp.transpose(chunk[k])[:TALL]
    lane_tall = iota((TALL, 128), 1)
    strips = []
    for k, field in enumerate((scaling, density)):

        def ends(g, at):
            columns = slice(at, at + 128)
            above = up.at[:, :, columns]
            below = down.at[:, :, columns]
            return jnp.concatenate(
                [halo_rows(above, k, g, True), field[g, :, columns], halo_rows(below, k, g, False)], axis=0
            )

        firsts = [ends(g, 0) for g in range(FACES)]
        lasts = [ends(g, SIDE - 128) for g in range(FACES)]
        strips.append([
            jnp.where(
                lane_tall < 64,
                strip_lanes(firsts[2 * t], lasts[2 * t], 0),
                strip_lanes(firsts[2 * t + 1], lasts[2 * t + 1], 1),
            )
            for t in range(3)
        ])
        mixed[0, k * TALL : (k + 1) * TALL, :] = column_strips(lambda g: firsts[g], lambda g: lasts[g])
    for v in (0, 2, 4):
        mixed[v + 1] = swap_depth(mixed[v])

    for k in range(2):
        for t in range(3):
            value = strips[k][t]
            for f in (2 * t, 2 * t + 1):
                for e in (2, 3):
                    g, meets, turned = seams[0, e, f], seams[1, e, f], seams[2, e, f]
                    of_column = meets >= 2
                    rising = (meets % 2) == 0
                    swapped = jnp.where(rising, 1 if e == 2 else 0, 0 if e == 2 else 1)
                    kind = jnp.where(of_column, 2 * turned, 4) + swapped
                    start = jnp.where(of_column, 16 * g + jnp.where(meets == 2, 8, 0), 48 * meets + 8 * g)
                    at = 64 * (f % 2) + (32 if e == 2 else 24)
                    moved = pltpu.roll(
                        mixed[kind, k * TALL : (k + 1) * TALL, :], jnp.bitwise_and(at - start + 128, 127), 1
                    )
                    value = jnp.where((lane_tall >= at) & (lane_tall < at + 8), moved, value)
            rows = [value[:8], value[8:24], value[24:]]
            work[k, t, 8:24, :] = rows[1]

            @pl.when(q != 0)
            def _():
                work[k, t, :8, :] = rows[0]

            @pl.when(q == 0)
            def _():
                work[k, t, :8, :] = jnp.where((lane % 64 >= 24) & (lane % 64 < 40), rows[0], work[k, t, :8, :])

            @pl.when(q != last)
            def _():
                work[k, t, 24:, :] = rows[2]

            @pl.when(q == last)
            def _():
                work[k, t, 24:, :] = jnp.where((lane % 64 >= 24) & (lane % 64 < 40), rows[2], work[k, t, 24:, :])

    def run(where):
        for f in range(FACES):
            above = [edge[k, f] if where == "first" else halo_rows(up, k, f, True) for k in range(2)]
            below = [edge[k, f] if where == "last" else halo_rows(down, k, f, False) for k in range(2)]
            x = jnp.concatenate([above[0], scaling[f], below[0]], axis=0)
            for _ in range(STEPS):
                x = diffuse(x)
            y = jnp.concatenate([above[1], density[f], below[1]], axis=0) / x
            dual[f] = y[HALO : HALO + ROWS]
            for _ in range(STEPS):
                y = diffuse(y)
            m = scaling[f] * y[HALO : HALO + ROWS]
            marginal[f] = m
            scaled = share * jnp.log(m)
            for i in range(2):
                for j in range(4):
                    put_weighted(weighted, scaled[8 * i : 8 * i + 8, 128 * j : 128 * j + 128], f, i, j)
        x = [work[0, t] for t in range(3)]
        for _ in range(STEPS):
            x = [diffuse_strip(v, where) for v in x]
        y = [work[1, t] / x[t] for t in range(3)]
        first = [v[HALO : HALO + ROWS] for v in y]
        for _ in range(STEPS):
            y = [diffuse_strip(v, where) for v in y]
        lane = iota((ROWS, 128), 1)
        for t in range(3):
            m = work[0, t, HALO : HALO + ROWS, :] * y[t][HALO : HALO + ROWS]
            scaled = share * jnp.log(m)
            for h in range(2):
                f = 2 * t + h
                for j, turn, mask in ((0, 88 - 64 * h, lane < 8), (3, 104 - 64 * h, lane >= 120)):
                    columns = slice(128 * j, 128 * j + 128)
                    for ref, value in ((dual, first[t]), (marginal, m)):
                        ref[f, :, columns] = jnp.where(mask, pltpu.roll(value, turn, 1), ref[f, :, columns])
                    moved = pltpu.roll(scaled, turn, 1)
                    for i in range(2):
                        at = 8 * f + 4 * i + j
                        rows = slice(8 * (at % per), 8 * (at % per) + 8)
                        weighted[at // per, rows, :] = jnp.where(
                            mask[:8], moved[8 * i : 8 * i + 8], weighted[at // per, rows, :]
                        )

    @pl.when(q == 0)
    def _():
        run("first")

    @pl.when(q == last)
    def _():
        run("last")

    @pl.when(jnp.logical_not(is_edge))
    def _():
        run(None)


def mean_kernel(parts, result):
    members, rows = result.shape[0], result.shape[1]
    total = parts[0]
    for k in range(1, members):
        total = total + parts[k]
    mean = total[:rows] / total[rows : rows + 1]
    value = jnp.exp(mean)
    for k in range(members):
        result[k] = value


def update_kernel(parts, scaling, marginal, fresh, barycenter):
    members = parts.shape[0]
    per = 48 // members
    for f in range(FACES):
        for i in range(2):
            for j in range(4):
                t = 8 * f + 4 * i + j
                at = 8 * (t % per)
                value = parts[t // per, at : at + 8, :]
                rows, columns = slice(8 * i, 8 * i + 8), slice(128 * j, 128 * j + 128)
                barycenter[f, rows, columns] = value
                fresh[f, rows, columns] = scaling[f, rows, columns] * value / marginal[f, rows, columns]


def body(density, scaling, member_weights, seams):
    tiles = lax.axis_size("tile")
    members = lax.axis_size("member")
    scaling = scaling[0]
    density = density[0]
    place = lax.axis_index("tile").astype(jnp.int32).reshape(1)
    f32 = jnp.float32
    vmem = pl.BlockSpec(memory_space=pltpu.VMEM)
    smem = pl.BlockSpec(memory_space=pltpu.SMEM)
    field = jax.ShapeDtypeStruct((FACES, ROWS, SIDE), f32)
    edge_rows = jax.ShapeDtypeStruct((FACES + FACES // 2, HALO, SIDE), f32)
    params = pltpu.CompilerParams(vmem_limit_bytes=24 * 1024 * 1024)
    beside, across, message = pl.pallas_call(
        pack_kernel,
        out_shape=(edge_rows, edge_rows, jax.ShapeDtypeStruct((tiles, 24, 128), f32)),
        in_specs=[smem] + [pl.BlockSpec(memory_space=pl.ANY)] * 3,
        out_specs=(vmem, vmem, vmem),
        scratch_shapes=[
            pltpu.SMEM(seams.shape, jnp.int32),
            pltpu.VMEM(scaling.shape, f32),
            pltpu.VMEM(density.shape, f32),
            pltpu.SemaphoreType.DMA((3,)),
        ],
        name="pack",
    )(place, seams, scaling, density)
    beside = lax.ppermute(beside, "tile", [(i, i ^ 1) for i in range(tiles)])
    across = lax.ppermute(across, "tile", [(i, (i + 1 if i % 2 else i - 1) % tiles) for i in range(tiles)])
    message = lax.all_to_all(message, "tile", 0, 0)
    rows = 384 // members
    sums = jax.ShapeDtypeStruct((members, rows + 8, 128), f32)
    dual, marginal, weighted = pl.pallas_call(
        heat_kernel,
        out_shape=(field, field, sums),
        in_specs=[smem, smem, smem] + [vmem] * 5,
        out_specs=(vmem, vmem, vmem),
        scratch_shapes=[
            pltpu.VMEM(edge_rows.shape, f32),
            pltpu.VMEM(edge_rows.shape, f32),
            pltpu.VMEM((6, 2 * TALL, 128), f32),
            pltpu.VMEM((2, 128, 128), f32),
            pltpu.VMEM((224, SIDE), f32),
            pltpu.VMEM((224, SIDE), f32),
            pltpu.VMEM((SIDE, 128), f32),
            pltpu.VMEM((SIDE, 128), f32),
            pltpu.VMEM((2, FACES, HALO, SIDE), f32),
            pltpu.VMEM((2, 3, TALL, 128), f32),
        ],
        compiler_params=params,
        name="heat",
    )(place, seams, member_weights, scaling, density, beside, across, message)
    weighted = lax.all_to_all(weighted, "member", 0, 0)
    means = pl.pallas_call(
        mean_kernel,
        out_shape=jax.ShapeDtypeStruct((members, rows, 128), f32),
        in_specs=[vmem],
        out_specs=vmem,
        compiler_params=params,
        name="mean",
    )(weighted)
    means = lax.all_to_all(means, "member", 0, 0)
    fresh, barycenter = pl.pallas_call(
        update_kernel,
        out_shape=(field, field),
        in_specs=[vmem] * 3,
        out_specs=(vmem, vmem),
        compiler_params=params,
        name="update",
    )(means, scaling, marginal)
    return (fresh[None], dual[None], barycenter)


def solution(mesh):
    return jax.shard_map(
        body,
        mesh=mesh,
        in_specs=(
            P("member", None, "tile", None),
            P("member", None, "tile", None),
            P("member"),
            P(),
        ),
        out_specs=(
            P("member", None, "tile", None),
            P("member", None, "tile", None),
            P(None, "tile", None),
        ),
        check_vma=False,
    )
```

```python
import jax
import jax.numpy as jnp
from jax import lax
from jax.experimental import pallas as pl
from jax.experimental.pallas import tpu as pltpu
from jax.sharding import PartitionSpec as P

KAPPA = 0.24
STEPS = 4
FACES = 6
ROWS = 16
SIDE = 512
HALO = 8
TALL = ROWS + 2 * HALO


def iota(shape, dim):
    return lax.broadcasted_iota(jnp.int32, shape, dim)


def reverse_lanes(x):
    index = 127 - iota((8, 128), 1)
    tiles = [
        jnp.take_along_axis(x[:, at : at + 128], index, axis=1)
        for at in range(0, x.shape[1], 128)
    ]
    return jnp.concatenate(tiles[::-1], axis=1) if len(tiles) > 1 else tiles[0]


def column_strips(first, last):
    strips = None
    for g in range(FACES):
        a, b = first(g), last(g)
        lane = iota(a.shape, 1)
        moved = pltpu.roll(jnp.where(lane >= 64, b, a), 16 * g + 8, 1)
        strips = moved if strips is None else jnp.where(lane >= 16 * g, moved, strips)
    return strips


def spread(block):
    return [pltpu.roll(block, 96 - 32 * b, 1) for b in range(3)]


def unspread(b0, b1, b2):
    lane = iota((8, 128), 1)
    return jnp.where(
        lane < 32, pltpu.roll(b0, 32, 1), jnp.where(lane < 64, pltpu.roll(b1, 64, 1), pltpu.roll(b2, 96, 1))
    )


def join_halves(low, high):
    return jnp.where(iota(low.shape, 0) < 4, low, high)


def halo_rows(rows, k, g, is_up):
    if k == 0:
        return rows[g]
    block = rows[FACES + g // 2]
    return pltpu.roll(block, 4, 0) if (g % 2 == 0) == is_up else block


def pack_kernel(place, seams_at, scaling_at, density_at, across, beside, message, seams, scaling, density, arrived):
    p = place[0]
    pairs = ((scaling_at, scaling), (density_at, density), (seams_at, seams))
    copies = [pltpu.make_async_copy(a, b, arrived.at[i]) for i, (a, b) in enumerate(pairs)]
    for copy in copies:
        copy.start()
    for copy in copies:
        copy.wait()
    is_even = lax.rem(p, 2) == 0
    count = message.shape[0]
    lane = iota((8, 128), 1)
    sub = iota((8, 128), 0)
    ups = [scaling[g, HALO:] for g in range(FACES)]
    downs = [scaling[g, :HALO] for g in range(FACES)]
    for b in range(3):
        d0, d1 = density[2 * b], density[2 * b + 1]
        ups.append(join_halves(pltpu.roll(d0[HALO:], 4, 0), d1[HALO:]))
        downs.append(join_halves(d0[:HALO], pltpu.roll(d1[:HALO], 4, 0)))
    for b, (u, d) in enumerate(zip(ups, downs)):
        beside[b] = jnp.where(is_even, u, d)
        across[b] = jnp.where(is_even, d, u)
    vs = column_strips(lambda g: scaling[g, :, :128], lambda g: scaling[g, :, SIDE - 128 :])
    vd = column_strips(lambda g: density[g, :, :128], lambda g: density[g, :, SIDE - 128 :])
    tail = spread(vd[8:])
    head = (vs[:8], vs[8:], vd[:8])
    block = jnp.concatenate([jnp.where(lane < 96, head[b], tail[b]) for b in range(3)], axis=0)
    is_last = p == count - 1
    is_edge = (p == 0) | is_last

    @pl.when(jnp.logical_not(is_edge))
    def _():
        for q in range(count):
            message[q] = block

    @pl.when(is_edge)
    def _():
        message[0] = block
        message[count - 1] = block
        e = is_last.astype(jnp.int32)
        base = pl.multiple_of(e * 8, 8)
        own_s = jnp.where(is_last, vs[:8], vs[8:])
        own_d = jnp.where(is_last, vd[:8], vd[8:])
        far = jnp.where(is_last, pltpu.roll(own_d, 5, 0), pltpu.roll(own_d, 3, 0))
        free = jnp.where(is_last, (sub >= 5).astype(jnp.int32), (sub <= 2).astype(jnp.int32)) == 1
        lane16 = lane % 16
        coded = jnp.where(
            free & (lane16 < 4),
            pltpu.roll(far, 124, 1),
            jnp.where(free & (lane16 >= 12), pltpu.roll(far, 4, 1), own_s),
        )
        extra = spread(coded)
        pieces = []
        for g in range(FACES):
            turned = seams[2, e, g] == 1
            s = scaling[g, pl.ds(base, 8), :]
            d = density[g, pl.ds(base, 8), :]
            pieces.append((jnp.where(turned, reverse_lanes(s), s), jnp.where(turned, reverse_lanes(d), d)))
        sub_wide = iota((8, SIDE), 0)
        lane_wide = iota((8, SIDE), 1) % 128
        blocks = []
        for b in range(3):
            (s0, d0), (s1, d1) = pieces[2 * b], pieces[2 * b + 1]
            low = jnp.where(is_last, pltpu.roll(d0, 4, 0), d0)
            high = jnp.where(is_last, d1, pltpu.roll(d1, 4, 0))
            blocks.append((s0, s1, jnp.where(sub_wide < 4, low, high)))
        for t in range(3):
            tail_t = jnp.concatenate([extra[t]] * 4, axis=1)
            for r in range(8):
                moved = [pltpu.roll(blocks[b][t], (32 * b - 16 * r + 8) % SIDE, 1) for b in range(3)]
                full = jnp.where(
                    lane_wide < 32,
                    moved[0],
                    jnp.where(lane_wide < 64, moved[1], jnp.where(lane_wide < 96, moved[2], tail_t)),
                )
                for a in range(4):
                    q = 8 * a + r
                    if 0 < q < count - 1:
                        message[q, 8 * t : 8 * t + 8, :] = full[:, 128 * a : 128 * a + 128]


def diffuse(x):
    rows, lanes = x.shape
    vertical = pltpu.roll(x, 1, 0) + pltpu.roll(x, rows - 1, 0)
    lateral = pltpu.roll(x, 1, 1) + pltpu.roll(x, lanes - 1, 1)
    return x + KAPPA * ((vertical + lateral) - 4.0 * x)


def diffuse_strip(x, where):
    above = pltpu.roll(x, 1, 0)
    below = pltpu.roll(x, TALL - 1, 0)
    left = pltpu.roll(x, 1, 1)
    right = pltpu.roll(x, 127, 1)
    if where is not None:
        lane = iota((8, 128), 1)
        sub = iota((8, 128), 0)
        at, edge = (0, 8) if where == "first" else (24, 23)
        depth = 7 - sub if where == "first" else sub
        place = lane % 64
        start = lane - place
        line = jnp.broadcast_to(x[edge : edge + 1], (8, 128))
        index = jnp.where(place == 40, start + 39 - depth, jnp.where(place == 23, start + 24 + depth, 0))
        lateral = jnp.take_along_axis(line, index, axis=1)
        index = jnp.where(place >= 32, start + 40, start + 23)
        taken = jnp.take_along_axis(x[at : at + 8], index, axis=1)
        taken = jnp.where((place == 39 - depth) | (place == 24 + depth), taken, 0.0)
        vertical = jnp.sum(taken, axis=0, keepdims=True)
        ghost = (place >= 24) & (place < 40)
        fixed_left = jnp.where(place == 40, lateral, left[at : at + 8])
        fixed_right = jnp.where(place == 23, lateral, right[at : at + 8])
        if where == "first":
            left = jnp.concatenate([fixed_left, left[8:]], axis=0)
            right = jnp.concatenate([fixed_right, right[8:]], axis=0)
            block = jnp.where(ghost & (sub == 0), vertical, above[8:16])
            above = jnp.concatenate([above[:8], block, above[16:]], axis=0)
        else:
            left = jnp.concatenate([left[:24], fixed_left], axis=0)
            right = jnp.concatenate([right[:24], fixed_right], axis=0)
            block = jnp.where(ghost & (sub == 7), vertical, below[16:24])
            below = jnp.concatenate([below[:16], block, below[24:]], axis=0)
    return x + KAPPA * (((above + below) + (left + right)) - 4.0 * x)


def strip_lanes(first, last, h):
    lane = iota(first.shape, 1)
    return jnp.where(
        lane % 64 < 32, pltpu.roll(last, 24 + 64 * h, 1), pltpu.roll(first, 40 + 64 * h, 1)
    )


def swap_depth(x):
    lane = iota((8, 128), 1)
    index = lane + 7 - 2 * (lane % 8)
    return jnp.concatenate(
        [jnp.take_along_axis(x[at : at + 8], index, axis=1) for at in range(0, x.shape[0], 8)], axis=0
    )


def put_weighted(weighted, value, f, i, j):
    per = 48 // weighted.shape[0]
    t = 8 * f + 4 * i + j
    if isinstance(f, int):
        weighted[t // per, 8 * (t % per) : 8 * (t % per) + 8, :] = value
    else:
        at = pl.multiple_of(8 * lax.rem(t, per), 8)
        weighted[lax.div(t, per), pl.ds(at, 8), :] = value


def heat_kernel(
    place, seams, weight, scaling, density, across, beside, message,
    dual, marginal, weighted, up, down, mixed, chunk, table_s, table_d, column_s, column_d, edge, work,
):
    q = place[0]
    count = message.shape[0]
    last = count - 1
    is_even = lax.rem(q, 2) == 0
    for b in range(FACES + FACES // 2):
        up[b] = jnp.where(is_even, across[b], beside[b])
        down[b] = jnp.where(is_even, beside[b], across[b])
    share = weight[0]
    lane = iota((8, 128), 1)
    sub = iota((8, 128), 0)
    is_edge = (q == 0) | (q == last)

    per = 48 // weighted.shape[0]
    for k in range(weighted.shape[0]):
        weighted[k, 8 * per :, :] = jnp.full((8, 128), share, jnp.float32)

    def far_rows(p):
        return unspread(message[p, :8, :], message[p, 8:16, :], message[p, 16:24, :])

    mirror, upper, lower = last - q, jnp.minimum(last + 1 - q, last), jnp.maximum(last - 1 - q, 0)
    coded = far_rows(jnp.where(q == 1, last, 0))
    near = jnp.where(q == 1, pltpu.roll(coded, 3, 0), pltpu.roll(coded, 5, 0))
    coded_d = jnp.where(lane % 16 < 8, pltpu.roll(near, 4, 1), pltpu.roll(near, 124, 1))
    parts_s = (
        jnp.where(q == last - 1, coded, message[lower, 8:16, :]),
        message[mirror, :8, :],
        message[mirror, 8:16, :],
        jnp.where(q == 1, coded, message[upper, :8, :]),
    )
    parts_d = (
        jnp.where(q == last - 1, coded_d, far_rows(lower)),
        message[mirror, 16:24, :],
        far_rows(mirror),
        jnp.where(q == 1, coded_d, message[upper, 16:24, :]),
    )
    for base, parts in ((0, parts_s), (TALL, parts_d)):
        for block in range(4):
            for i in range(8):
                at = base + TALL - 1 - 8 * block - i
                mixed[2, at : at + 1, :] = parts[block][i : i + 1]

    chunk[:, 96:, :] = jnp.zeros((2, 32, 128), jnp.float32)

    @pl.when(jnp.logical_not(is_edge))
    def _():
        for e in range(2):
            p = e * last
            for g in range(FACES):
                b, h = g // 2, g % 2
                turn = (128 - 32 * b) % 128
                s = message[p, 8 * h : 8 * h + 8, :]
                d = message[p, 16:24, :]
                if turn:
                    s, d = pltpu.roll(s, turn, 1), pltpu.roll(d, turn, 1)
                if h != e:
                    d = pltpu.roll(d, 4, 0)
                at = 48 * e + 8 * g
                chunk[0, at : at + 8, :] = s
                chunk[1, at : at + 8, :] = d

    for is_first in (True, False):

        @pl.when(q == (0 if is_first else last))
        def _():
            e = 0 if is_first else 1

            def gather(p, carry):
                at = pl.multiple_of(16 * p, 16)
                column_s[pl.ds(at, 16), :] = message[p, :16, :]
                column_d[pl.ds(at, 8), :] = message[p, 16:24, :]
                column_d[pl.ds(at + 8, 8), :] = far_rows(p)
                return carry

            lax.fori_loop(0, count, gather, 0, unroll=8)
            for k, (table, columns, field) in enumerate(
                ((table_s, column_s, scaling), (table_d, column_d, density))
            ):
                for a in range(4):
                    rows = slice(128 * a, 128 * a + 128)
                    table[:128, rows] = jnp.transpose(columns[rows, :])
                for e_of in range(2):
                    for g in range(FACES):
                        if is_first:
                            rows = field[g, :HALO] if e_of == 0 else halo_rows(up, k, g, True)
                        else:
                            rows = halo_rows(down, k, g, False) if e_of == 0 else field[g, HALO:]
                        at = 48 * e_of + 8 * g
                        table[128 + at : 136 + at, :] = rows
                        turned = seams[2, e_of, g] == 1
                        a, b = rows[:, :128], rows[:, SIDE - 128 :]
                        if is_first:
                            piece = pltpu.roll(jnp.where(turned, reverse_lanes(b), a), 8, 1)
                        else:
                            piece = pltpu.roll(jnp.where(turned, reverse_lanes(a), b), 24, 1)
                        chunk[k, at : at + 8, :] = piece
                for f in range(FACES):
                    g, meets = seams[0, e, f], seams[1, e, f]
                    start = jnp.where(
                        meets >= 2, 16 * g + jnp.where(meets == 2, 8, 0), 128 + 48 * meets + 8 * g
                    )
                    rising = (meets % 2) == 0
                    for i in range(8):
                        depth = 7 - i if is_first else i
                        at = start + jnp.where(rising, depth, 7 - depth)
                        edge[k, f, i : i + 1, :] = table[pl.ds(at, 1), :]
                for f in range(FACES):
                    piece = edge[k, f]
                    edge[k, f] = jnp.where(seams[2, e, f] == 1, reverse_lanes(piece), piece)
                at = 0 if is_first else HALO + ROWS
                for t in range(3):
                    pieces = [
                        strip_lanes(edge[k, f, :, :128], edge[k, f, :, SIDE - 128 :], f % 2)
                        for f in (2 * t, 2 * t + 1)
                    ]
                    work[k, t, at : at + 8, :] = jnp.where(lane < 64, pieces[0], pieces[1])

    for k in range(2):
        mixed[4, k * TALL : (k + 1) * TALL, :] = jnp.transpose(chunk[k])[:TALL]
    lane_tall = iota((TALL, 128), 1)
    strips = []
    for k, field in enumerate((scaling, density)):

        def ends(g, at):
            columns = slice(at, at + 128)
            above = up.at[:, :, columns]
            below = down.at[:, :, columns]
            return jnp.concatenate(
                [halo_rows(above, k, g, True), field[g, :, columns], halo_rows(below, k, g, False)], axis=0
            )

        firsts = [ends(g, 0) for g in range(FACES)]
        lasts = [ends(g, SIDE - 128) for g in range(FACES)]
        strips.append([
            jnp.where(
                lane_tall < 64,
                strip_lanes(firsts[2 * t], lasts[2 * t], 0),
                strip_lanes(firsts[2 * t + 1], lasts[2 * t + 1], 1),
            )
            for t in range(3)
        ])
        mixed[0, k * TALL : (k + 1) * TALL, :] = column_strips(lambda g: firsts[g], lambda g: lasts[g])
    for v in (0, 2, 4):
        mixed[v + 1] = swap_depth(mixed[v])

    for k in range(2):
        for t in range(3):
            value = strips[k][t]
            for f in (2 * t, 2 * t + 1):
                for e in (2, 3):
                    g, meets, turned = seams[0, e, f], seams[1, e, f], seams[2, e, f]
                    of_column = meets >= 2
                    rising = (meets % 2) == 0
                    swapped = jnp.where(rising, 1 if e == 2 else 0, 0 if e == 2 else 1)
                    kind = jnp.where(of_column, 2 * turned, 4) + swapped
                    start = jnp.where(of_column, 16 * g + jnp.where(meets == 2, 8, 0), 48 * meets + 8 * g)
                    at = 64 * (f % 2) + (32 if e == 2 else 24)
                    moved = pltpu.roll(
                        mixed[kind, k * TALL : (k + 1) * TALL, :], jnp.bitwise_and(at - start + 128, 127), 1
                    )
                    value = jnp.where((lane_tall >= at) & (lane_tall < at + 8), moved, value)
            rows = [value[:8], value[8:24], value[24:]]
            work[k, t, 8:24, :] = rows[1]

            @pl.when(q != 0)
            def _():
                work[k, t, :8, :] = rows[0]

            @pl.when(q == 0)
            def _():
                work[k, t, :8, :] = jnp.where((lane % 64 >= 24) & (lane % 64 < 40), rows[0], work[k, t, :8, :])

            @pl.when(q != last)
            def _():
                work[k, t, 24:, :] = rows[2]

            @pl.when(q == last)
            def _():
                work[k, t, 24:, :] = jnp.where((lane % 64 >= 24) & (lane % 64 < 40), rows[2], work[k, t, 24:, :])

    def run(where):
        for f in range(FACES):
            above = [edge[k, f] if where == "first" else halo_rows(up, k, f, True) for k in range(2)]
            below = [edge[k, f] if where == "last" else halo_rows(down, k, f, False) for k in range(2)]
            x = jnp.concatenate([above[0], scaling[f], below[0]], axis=0)
            for _ in range(STEPS):
                x = diffuse(x)
            y = jnp.concatenate([above[1], density[f], below[1]], axis=0) / x
            dual[f] = y[HALO : HALO + ROWS]
            for _ in range(STEPS):
                y = diffuse(y)
            m = scaling[f] * y[HALO : HALO + ROWS]
            marginal[f] = m
            scaled = share * jnp.log(m)
            for i in range(2):
                for j in range(4):
                    put_weighted(weighted, scaled[8 * i : 8 * i + 8, 128 * j : 128 * j + 128], f, i, j)
        x = [work[0, t] for t in range(3)]
        for _ in range(STEPS):
            x = [diffuse_strip(v, where) for v in x]
        y = [work[1, t] / x[t] for t in range(3)]
        first = [v[HALO : HALO + ROWS] for v in y]
        for _ in range(STEPS):
            y = [diffuse_strip(v, where) for v in y]
        lane = iota((ROWS, 128), 1)
        for t in range(3):
            m = work[0, t, HALO : HALO + ROWS, :] * y[t][HALO : HALO + ROWS]
            scaled = share * jnp.log(m)
            for h in range(2):
                f = 2 * t + h
                for j, turn, mask in ((0, 88 - 64 * h, lane < 8), (3, 104 - 64 * h, lane >= 120)):
                    columns = slice(128 * j, 128 * j + 128)
                    for ref, value in ((dual, first[t]), (marginal, m)):
                        ref[f, :, columns] = jnp.where(mask, pltpu.roll(value, turn, 1), ref[f, :, columns])
                    moved = pltpu.roll(scaled, turn, 1)
                    for i in range(2):
                        at = 8 * f + 4 * i + j
                        rows = slice(8 * (at % per), 8 * (at % per) + 8)
                        weighted[at // per, rows, :] = jnp.where(
                            mask[:8], moved[8 * i : 8 * i + 8], weighted[at // per, rows, :]
                        )

    @pl.when(q == 0)
    def _():
        run("first")

    @pl.when(q == last)
    def _():
        run("last")

    @pl.when(jnp.logical_not(is_edge))
    def _():
        run(None)


def mean_kernel(parts, result):
    members, rows = result.shape[0], result.shape[1]
    total = parts[0]
    for k in range(1, members):
        total = total + parts[k]
    mean = total[:rows] / total[rows : rows + 1]
    value = jnp.exp(mean)
    for k in range(members):
        result[k] = value


def update_kernel(parts, scaling, marginal, fresh, barycenter):
    members = parts.shape[0]
    per = 48 // members
    for f in range(FACES):
        for i in range(2):
            for j in range(4):
                t = 8 * f + 4 * i + j
                at = 8 * (t % per)
                value = parts[t // per, at : at + 8, :]
                rows, columns = slice(8 * i, 8 * i + 8), slice(128 * j, 128 * j + 128)
                barycenter[f, rows, columns] = value
                fresh[f, rows, columns] = scaling[f, rows, columns] * value / marginal[f, rows, columns]


def body(density, scaling, member_weights, seams):
    tiles = lax.axis_size("tile")
    members = lax.axis_size("member")
    scaling = scaling[0]
    density = density[0]
    place = lax.axis_index("tile").astype(jnp.int32).reshape(1)
    f32 = jnp.float32
    vmem = pl.BlockSpec(memory_space=pltpu.VMEM)
    smem = pl.BlockSpec(memory_space=pltpu.SMEM)
    field = jax.ShapeDtypeStruct((FACES, ROWS, SIDE), f32)
    edge_rows = jax.ShapeDtypeStruct((FACES + FACES // 2, HALO, SIDE), f32)
    params = pltpu.CompilerParams(vmem_limit_bytes=24 * 1024 * 1024)
    across, beside, message = pl.pallas_call(
        pack_kernel,
        out_shape=(edge_rows, edge_rows, jax.ShapeDtypeStruct((tiles, 24, 128), f32)),
        in_specs=[smem] + [pl.BlockSpec(memory_space=pl.ANY)] * 3,
        out_specs=(vmem, vmem, vmem),
        scratch_shapes=[
            pltpu.SMEM(seams.shape, jnp.int32),
            pltpu.VMEM(scaling.shape, f32),
            pltpu.VMEM(density.shape, f32),
            pltpu.SemaphoreType.DMA((3,)),
        ],
        name="pack",
    )(place, seams, scaling, density)
    across = lax.ppermute(across, "tile", [(i, (i + 1 if i % 2 else i - 1) % tiles) for i in range(tiles)])
    beside = lax.ppermute(beside, "tile", [(i, i ^ 1) for i in range(tiles)])
    message = lax.all_to_all(message, "tile", 0, 0)
    rows = 384 // members
    sums = jax.ShapeDtypeStruct((members, rows + 8, 128), f32)
    dual, marginal, weighted = pl.pallas_call(
        heat_kernel,
        out_shape=(field, field, sums),
        in_specs=[smem, smem, smem] + [vmem] * 5,
        out_specs=(vmem, vmem, vmem),
        scratch_shapes=[
            pltpu.VMEM(edge_rows.shape, f32),
            pltpu.VMEM(edge_rows.shape, f32),
            pltpu.VMEM((6, 2 * TALL, 128), f32),
            pltpu.VMEM((2, 128, 128), f32),
            pltpu.VMEM((224, SIDE), f32),
            pltpu.VMEM((224, SIDE), f32),
            pltpu.VMEM((SIDE, 128), f32),
            pltpu.VMEM((SIDE, 128), f32),
            pltpu.VMEM((2, FACES, HALO, SIDE), f32),
            pltpu.VMEM((2, 3, TALL, 128), f32),
        ],
        compiler_params=params,
        name="heat",
    )(place, seams, member_weights, scaling, density, across, beside, message)
    weighted = lax.all_to_all(weighted, "member", 0, 0)
    means = pl.pallas_call(
        mean_kernel,
        out_shape=jax.ShapeDtypeStruct((members, rows, 128), f32),
        in_specs=[vmem],
        out_specs=vmem,
        compiler_params=params,
        name="mean",
    )(weighted)
    means = lax.all_to_all(means, "member", 0, 0)
    fresh, barycenter = pl.pallas_call(
        update_kernel,
        out_shape=(field, field),
        in_specs=[vmem] * 3,
        out_specs=(vmem, vmem),
        compiler_params=params,
        name="update",
    )(means, scaling, marginal)
    return (fresh[None], dual[None], barycenter)


def solution(mesh):
    return jax.shard_map(
        body,
        mesh=mesh,
        in_specs=(
            P("member", None, "tile", None),
            P("member", None, "tile", None),
            P("member"),
            P(),
        ),
        out_specs=(
            P("member", None, "tile", None),
            P("member", None, "tile", None),
            P(None, "tile", None),
        ),
        check_vma=False,
    )
```

```python
import jax
import jax.numpy as jnp
from jax import lax
from jax.experimental import pallas as pl
from jax.experimental.pallas import tpu as pltpu
from jax.sharding import PartitionSpec as P

KAPPA = 0.24
STEPS = 4
FACES = 6
ROWS = 16
SIDE = 512
HALO = 8
TALL = ROWS + 2 * HALO


def iota(shape, dim):
    return lax.broadcasted_iota(jnp.int32, shape, dim)


def reverse_lanes(x):
    index = 127 - iota((8, 128), 1)
    tiles = [
        jnp.take_along_axis(x[:, at : at + 128], index, axis=1)
        for at in range(0, x.shape[1], 128)
    ]
    return jnp.concatenate(tiles[::-1], axis=1) if len(tiles) > 1 else tiles[0]


def column_strips(first, last):
    strips = None
    for g in range(FACES):
        a, b = first(g), last(g)
        lane = iota(a.shape, 1)
        moved = pltpu.roll(jnp.where(lane >= 64, b, a), 16 * g + 8, 1)
        strips = moved if strips is None else jnp.where(lane >= 16 * g, moved, strips)
    return strips


def spread(block):
    return [pltpu.roll(block, 96 - 32 * b, 1) for b in range(3)]


def unspread(b0, b1, b2):
    lane = iota((8, 128), 1)
    return jnp.where(
        lane < 32, pltpu.roll(b0, 32, 1), jnp.where(lane < 64, pltpu.roll(b1, 64, 1), pltpu.roll(b2, 96, 1))
    )


def join_halves(low, high):
    return jnp.where(iota(low.shape, 0) < 4, low, high)


def halo_rows(rows, k, g, is_up):
    if k == 0:
        return rows[g]
    block = rows[FACES + g // 2]
    return pltpu.roll(block, 4, 0) if (g % 2 == 0) == is_up else block


def pack_kernel(place, seams_at, scaling_at, density_at, across, beside, message, seams, scaling, density, arrived):
    p = place[0]
    pairs = ((scaling_at, scaling), (density_at, density), (seams_at, seams))
    copies = [pltpu.make_async_copy(a, b, arrived.at[i]) for i, (a, b) in enumerate(pairs)]
    for copy in copies:
        copy.start()
    for copy in copies:
        copy.wait()
    is_even = lax.rem(p, 2) == 0
    count = message.shape[0]
    lane = iota((8, 128), 1)
    sub = iota((8, 128), 0)
    ups = [scaling[g, HALO:] for g in range(FACES)]
    downs = [scaling[g, :HALO] for g in range(FACES)]
    for b in range(3):
        d0, d1 = density[2 * b], density[2 * b + 1]
        ups.append(join_halves(pltpu.roll(d0[HALO:], 4, 0), d1[HALO:]))
        downs.append(join_halves(d0[:HALO], pltpu.roll(d1[:HALO], 4, 0)))
    for b, (u, d) in enumerate(zip(ups, downs)):
        beside[b] = jnp.where(is_even, u, d)
        across[b] = jnp.where(is_even, d, u)
    vs = column_strips(lambda g: scaling[g, :, :128], lambda g: scaling[g, :, SIDE - 128 :])
    vd = column_strips(lambda g: density[g, :, :128], lambda g: density[g, :, SIDE - 128 :])
    tail = spread(vd[8:])
    head = (vs[:8], vs[8:], vd[:8])
    block = jnp.concatenate([jnp.where(lane < 96, head[b], tail[b]) for b in range(3)], axis=0)
    is_last = p == count - 1
    is_edge = (p == 0) | is_last

    @pl.when(jnp.logical_not(is_edge))
    def _():
        for q in range(count):
            message[q] = block

    @pl.when(is_edge)
    def _():
        message[0] = block
        message[count - 1] = block
        e = is_last.astype(jnp.int32)
        base = pl.multiple_of(e * 8, 8)
        own_s = jnp.where(is_last, vs[:8], vs[8:])
        own_d = jnp.where(is_last, vd[:8], vd[8:])
        far = jnp.where(is_last, pltpu.roll(own_d, 5, 0), pltpu.roll(own_d, 3, 0))
        free = jnp.where(is_last, (sub >= 5).astype(jnp.int32), (sub <= 2).astype(jnp.int32)) == 1
        lane16 = lane % 16
        coded = jnp.where(
            free & (lane16 < 4),
            pltpu.roll(far, 124, 1),
            jnp.where(free & (lane16 >= 12), pltpu.roll(far, 4, 1), own_s),
        )
        extra = spread(coded)
        pieces = []
        for g in range(FACES):
            turned = seams[2, e, g] == 1
            s = scaling[g, pl.ds(base, 8), :]
            d = density[g, pl.ds(base, 8), :]
            pieces.append((jnp.where(turned, reverse_lanes(s), s), jnp.where(turned, reverse_lanes(d), d)))
        sub_wide = iota((8, SIDE), 0)
        lane_wide = iota((8, SIDE), 1) % 128
        blocks = []
        for b in range(3):
            (s0, d0), (s1, d1) = pieces[2 * b], pieces[2 * b + 1]
            low = jnp.where(is_last, pltpu.roll(d0, 4, 0), d0)
            high = jnp.where(is_last, d1, pltpu.roll(d1, 4, 0))
            blocks.append((s0, s1, jnp.where(sub_wide < 4, low, high)))
        for t in range(3):
            tail_t = jnp.concatenate([extra[t]] * 4, axis=1)
            for r in range(8):
                moved = [pltpu.roll(blocks[b][t], (32 * b - 16 * r + 8) % SIDE, 1) for b in range(3)]
                full = jnp.where(
                    lane_wide < 32,
                    moved[0],
                    jnp.where(lane_wide < 64, moved[1], jnp.where(lane_wide < 96, moved[2], tail_t)),
                )
                for a in range(4):
                    q = 8 * a + r
                    if 0 < q < count - 1:
                        message[q, 8 * t : 8 * t + 8, :] = full[:, 128 * a : 128 * a + 128]


def diffuse(blocks):
    lane = iota((8, 128), 1)
    sub = iota((8, 128), 0)
    high, wide = len(blocks), len(blocks[0])
    result = []
    for i in range(high):
        line = []
        for j in range(wide):
            x = blocks[i][j]
            above = pltpu.roll(jnp.where(sub == 7, blocks[i - 1][j], x), 1, 0)
            below = pltpu.roll(jnp.where(sub == 0, blocks[(i + 1) % high][j], x), 7, 0)
            left = pltpu.roll(jnp.where(lane == 127, blocks[i][j - 1], x), 1, 1)
            right = pltpu.roll(jnp.where(lane == 0, blocks[i][(j + 1) % wide], x), 127, 1)
            line.append((1.0 - 4.0 * KAPPA) * x + KAPPA * ((above + below) + (left + right)))
        result.append(line)
    return result


def diffuse_strip(x, where):
    above = pltpu.roll(x, 1, 0)
    below = pltpu.roll(x, TALL - 1, 0)
    left = pltpu.roll(x, 1, 1)
    right = pltpu.roll(x, 127, 1)
    if where is not None:
        lane = iota((8, 128), 1)
        sub = iota((8, 128), 0)
        at, edge = (0, 8) if where == "first" else (24, 23)
        depth = 7 - sub if where == "first" else sub
        place = lane % 64
        start = lane - place
        line = jnp.broadcast_to(x[edge : edge + 1], (8, 128))
        index = jnp.where(place == 40, start + 39 - depth, jnp.where(place == 23, start + 24 + depth, 0))
        lateral = jnp.take_along_axis(line, index, axis=1)
        index = jnp.where(place >= 32, start + 40, start + 23)
        taken = jnp.take_along_axis(x[at : at + 8], index, axis=1)
        taken = jnp.where((place == 39 - depth) | (place == 24 + depth), taken, 0.0)
        vertical = jnp.sum(taken, axis=0, keepdims=True)
        ghost = (place >= 24) & (place < 40)
        fixed_left = jnp.where(place == 40, lateral, left[at : at + 8])
        fixed_right = jnp.where(place == 23, lateral, right[at : at + 8])
        if where == "first":
            left = jnp.concatenate([fixed_left, left[8:]], axis=0)
            right = jnp.concatenate([fixed_right, right[8:]], axis=0)
            block = jnp.where(ghost & (sub == 0), vertical, above[8:16])
            above = jnp.concatenate([above[:8], block, above[16:]], axis=0)
        else:
            left = jnp.concatenate([left[:24], fixed_left], axis=0)
            right = jnp.concatenate([right[:24], fixed_right], axis=0)
            block = jnp.where(ghost & (sub == 7), vertical, below[16:24])
            below = jnp.concatenate([below[:16], block, below[24:]], axis=0)
    return x + KAPPA * (((above + below) + (left + right)) - 4.0 * x)


def strip_lanes(first, last, h):
    lane = iota(first.shape, 1)
    return jnp.where(
        lane % 64 < 32, pltpu.roll(last, 24 + 64 * h, 1), pltpu.roll(first, 40 + 64 * h, 1)
    )


def swap_depth(x):
    lane = iota((8, 128), 1)
    index = lane + 7 - 2 * (lane % 8)
    return jnp.concatenate(
        [jnp.take_along_axis(x[at : at + 8], index, axis=1) for at in range(0, x.shape[0], 8)], axis=0
    )


def put_weighted(weighted, value, f, i, j):
    per = 48 // weighted.shape[0]
    t = 8 * f + 4 * i + j
    if isinstance(f, int):
        weighted[t // per, 8 * (t % per) : 8 * (t % per) + 8, :] = value
    else:
        at = pl.multiple_of(8 * lax.rem(t, per), 8)
        weighted[lax.div(t, per), pl.ds(at, 8), :] = value


def heat_kernel(
    place, seams, weight, scaling, density, across, beside, message,
    dual, marginal, weighted, up, down, mixed, chunk, table_s, table_d, column_s, column_d, edge, work,
):
    q = place[0]
    count = message.shape[0]
    last = count - 1
    is_even = lax.rem(q, 2) == 0
    for b in range(FACES + FACES // 2):
        up[b] = jnp.where(is_even, across[b], beside[b])
        down[b] = jnp.where(is_even, beside[b], across[b])
    share = weight[0]
    lane = iota((8, 128), 1)
    sub = iota((8, 128), 0)
    is_edge = (q == 0) | (q == last)

    per = 48 // weighted.shape[0]
    for k in range(weighted.shape[0]):
        weighted[k, 8 * per :, :] = jnp.full((8, 128), share, jnp.float32)

    def far_rows(p):
        return unspread(message[p, :8, :], message[p, 8:16, :], message[p, 16:24, :])

    mirror, upper, lower = last - q, jnp.minimum(last + 1 - q, last), jnp.maximum(last - 1 - q, 0)
    coded = far_rows(jnp.where(q == 1, last, 0))
    near = jnp.where(q == 1, pltpu.roll(coded, 3, 0), pltpu.roll(coded, 5, 0))
    coded_d = jnp.where(lane % 16 < 8, pltpu.roll(near, 4, 1), pltpu.roll(near, 124, 1))
    parts_s = (
        jnp.where(q == last - 1, coded, message[lower, 8:16, :]),
        message[mirror, :8, :],
        message[mirror, 8:16, :],
        jnp.where(q == 1, coded, message[upper, :8, :]),
    )
    parts_d = (
        jnp.where(q == last - 1, coded_d, far_rows(lower)),
        message[mirror, 16:24, :],
        far_rows(mirror),
        jnp.where(q == 1, coded_d, message[upper, 16:24, :]),
    )
    for base, parts in ((0, parts_s), (TALL, parts_d)):
        for block in range(4):
            for i in range(8):
                at = base + TALL - 1 - 8 * block - i
                mixed[2, at : at + 1, :] = parts[block][i : i + 1]

    chunk[:, 96:, :] = jnp.zeros((2, 32, 128), jnp.float32)

    @pl.when(jnp.logical_not(is_edge))
    def _():
        for e in range(2):
            p = e * last
            for g in range(FACES):
                b, h = g // 2, g % 2
                turn = (128 - 32 * b) % 128
                s = message[p, 8 * h : 8 * h + 8, :]
                d = message[p, 16:24, :]
                if turn:
                    s, d = pltpu.roll(s, turn, 1), pltpu.roll(d, turn, 1)
                if h != e:
                    d = pltpu.roll(d, 4, 0)
                at = 48 * e + 8 * g
                chunk[0, at : at + 8, :] = s
                chunk[1, at : at + 8, :] = d

    for is_first in (True, False):

        @pl.when(q == (0 if is_first else last))
        def _():
            e = 0 if is_first else 1

            def gather(p, carry):
                at = pl.multiple_of(16 * p, 16)
                column_s[pl.ds(at, 16), :] = message[p, :16, :]
                column_d[pl.ds(at, 8), :] = message[p, 16:24, :]
                column_d[pl.ds(at + 8, 8), :] = far_rows(p)
                return carry

            lax.fori_loop(0, count, gather, 0, unroll=8)
            for k, (table, columns, field) in enumerate(
                ((table_s, column_s, scaling), (table_d, column_d, density))
            ):
                for a in range(4):
                    rows = slice(128 * a, 128 * a + 128)
                    table[:128, rows] = jnp.transpose(columns[rows, :])
                for e_of in range(2):
                    for g in range(FACES):
                        if is_first:
                            rows = field[g, :HALO] if e_of == 0 else halo_rows(up, k, g, True)
                        else:
                            rows = halo_rows(down, k, g, False) if e_of == 0 else field[g, HALO:]
                        at = 48 * e_of + 8 * g
                        table[128 + at : 136 + at, :] = rows
                        turned = seams[2, e_of, g] == 1
                        a, b = rows[:, :128], rows[:, SIDE - 128 :]
                        if is_first:
                            piece = pltpu.roll(jnp.where(turned, reverse_lanes(b), a), 8, 1)
                        else:
                            piece = pltpu.roll(jnp.where(turned, reverse_lanes(a), b), 24, 1)
                        chunk[k, at : at + 8, :] = piece
                for f in range(FACES):
                    g, meets = seams[0, e, f], seams[1, e, f]
                    start = jnp.where(
                        meets >= 2, 16 * g + jnp.where(meets == 2, 8, 0), 128 + 48 * meets + 8 * g
                    )
                    rising = (meets % 2) == 0
                    for i in range(8):
                        depth = 7 - i if is_first else i
                        at = start + jnp.where(rising, depth, 7 - depth)
                        edge[k, f, i : i + 1, :] = table[pl.ds(at, 1), :]
                for f in range(FACES):
                    piece = edge[k, f]
                    edge[k, f] = jnp.where(seams[2, e, f] == 1, reverse_lanes(piece), piece)
                at = 0 if is_first else HALO + ROWS
                for t in range(3):
                    pieces = [
                        strip_lanes(edge[k, f, :, :128], edge[k, f, :, SIDE - 128 :], f % 2)
                        for f in (2 * t, 2 * t + 1)
                    ]
                    work[k, t, at : at + 8, :] = jnp.where(lane < 64, pieces[0], pieces[1])

    for k in range(2):
        mixed[4, k * TALL : (k + 1) * TALL, :] = jnp.transpose(chunk[k])[:TALL]
    lane_tall = iota((TALL, 128), 1)
    strips = []
    for k, field in enumerate((scaling, density)):

        def ends(g, at):
            columns = slice(at, at + 128)
            above = up.at[:, :, columns]
            below = down.at[:, :, columns]
            return jnp.concatenate(
                [halo_rows(above, k, g, True), field[g, :, columns], halo_rows(below, k, g, False)], axis=0
            )

        firsts = [ends(g, 0) for g in range(FACES)]
        lasts = [ends(g, SIDE - 128) for g in range(FACES)]
        strips.append([
            jnp.where(
                lane_tall < 64,
                strip_lanes(firsts[2 * t], lasts[2 * t], 0),
                strip_lanes(firsts[2 * t + 1], lasts[2 * t + 1], 1),
            )
            for t in range(3)
        ])
        mixed[0, k * TALL : (k + 1) * TALL, :] = column_strips(lambda g: firsts[g], lambda g: lasts[g])
    for v in (0, 2, 4):
        mixed[v + 1] = swap_depth(mixed[v])

    for k in range(2):
        for t in range(3):
            value = strips[k][t]
            for f in (2 * t, 2 * t + 1):
                for e in (2, 3):
                    g, meets, turned = seams[0, e, f], seams[1, e, f], seams[2, e, f]
                    of_column = meets >= 2
                    rising = (meets % 2) == 0
                    swapped = jnp.where(rising, 1 if e == 2 else 0, 0 if e == 2 else 1)
                    kind = jnp.where(of_column, 2 * turned, 4) + swapped
                    start = jnp.where(of_column, 16 * g + jnp.where(meets == 2, 8, 0), 48 * meets + 8 * g)
                    at = 64 * (f % 2) + (32 if e == 2 else 24)
                    moved = pltpu.roll(
                        mixed[kind, k * TALL : (k + 1) * TALL, :], jnp.bitwise_and(at - start + 128, 127), 1
                    )
                    value = jnp.where((lane_tall >= at) & (lane_tall < at + 8), moved, value)
            rows = [value[:8], value[8:24], value[24:]]
            work[k, t, 8:24, :] = rows[1]

            @pl.when(q != 0)
            def _():
                work[k, t, :8, :] = rows[0]

            @pl.when(q == 0)
            def _():
                work[k, t, :8, :] = jnp.where((lane % 64 >= 24) & (lane % 64 < 40), rows[0], work[k, t, :8, :])

            @pl.when(q != last)
            def _():
                work[k, t, 24:, :] = rows[2]

            @pl.when(q == last)
            def _():
                work[k, t, 24:, :] = jnp.where((lane % 64 >= 24) & (lane % 64 < 40), rows[2], work[k, t, 24:, :])

    def run(where):
        def tall(k, f):
            field = (scaling, density)[k]
            above = edge[k, f] if where == "first" else halo_rows(up, k, f, True)
            below = edge[k, f] if where == "last" else halo_rows(down, k, f, False)
            lines = (above, field[f, :HALO], field[f, HALO:], below)
            return [[line[:, at : at + 128] for at in range(0, SIDE, 128)] for line in lines]

        for some in (range(0, 3), range(3, FACES)):
            x = [tall(0, f) for f in some]
            for _ in range(STEPS):
                x = [diffuse(v) for v in x]
            y = [
                [[d / h for d, h in zip(*lines)] for lines in zip(tall(1, f), v)]
                for f, v in zip(some, x)
            ]
            for f, v in zip(some, y):
                for i in range(2):
                    for j in range(4):
                        dual[f, 8 * i : 8 * i + 8, 128 * j : 128 * j + 128] = v[i + 1][j]
            for _ in range(STEPS):
                y = [diffuse(v) for v in y]
            for f, v in zip(some, y):
                for i in range(2):
                    for j in range(4):
                        at = (f, slice(8 * i, 8 * i + 8), slice(128 * j, 128 * j + 128))
                        m = scaling[at] * v[i + 1][j]
                        marginal[at] = m
                        put_weighted(weighted, share * jnp.log(m), f, i, j)
        x = [work[0, t] for t in range(3)]
        for _ in range(STEPS):
            x = [diffuse_strip(v, where) for v in x]
        y = [work[1, t] / x[t] for t in range(3)]
        first = [v[HALO : HALO + ROWS] for v in y]
        for _ in range(STEPS):
            y = [diffuse_strip(v, where) for v in y]
        lane = iota((ROWS, 128), 1)
        for t in range(3):
            m = work[0, t, HALO : HALO + ROWS, :] * y[t][HALO : HALO + ROWS]
            scaled = share * jnp.log(m)
            for h in range(2):
                f = 2 * t + h
                for j, turn, mask in ((0, 88 - 64 * h, lane < 8), (3, 104 - 64 * h, lane >= 120)):
                    columns = slice(128 * j, 128 * j + 128)
                    for ref, value in ((dual, first[t]), (marginal, m)):
                        ref[f, :, columns] = jnp.where(mask, pltpu.roll(value, turn, 1), ref[f, :, columns])
                    moved = pltpu.roll(scaled, turn, 1)
                    for i in range(2):
                        at = 8 * f + 4 * i + j
                        rows = slice(8 * (at % per), 8 * (at % per) + 8)
                        weighted[at // per, rows, :] = jnp.where(
                            mask[:8], moved[8 * i : 8 * i + 8], weighted[at // per, rows, :]
                        )

    @pl.when(q == 0)
    def _():
        run("first")

    @pl.when(q == last)
    def _():
        run("last")

    @pl.when(jnp.logical_not(is_edge))
    def _():
        run(None)


def mean_kernel(parts, result):
    members, rows = result.shape[0], result.shape[1]
    total = parts[0]
    for k in range(1, members):
        total = total + parts[k]
    mean = total[:rows] / total[rows : rows + 1]
    value = jnp.exp(mean)
    for k in range(members):
        result[k] = value


def update_kernel(parts, scaling, marginal, fresh, barycenter):
    members = parts.shape[0]
    per = 48 // members
    for f in range(FACES):
        for i in range(2):
            for j in range(4):
                t = 8 * f + 4 * i + j
                at = 8 * (t % per)
                value = parts[t // per, at : at + 8, :]
                rows, columns = slice(8 * i, 8 * i + 8), slice(128 * j, 128 * j + 128)
                barycenter[f, rows, columns] = value
                fresh[f, rows, columns] = scaling[f, rows, columns] * value / marginal[f, rows, columns]


def body(density, scaling, member_weights, seams):
    tiles = lax.axis_size("tile")
    members = lax.axis_size("member")
    scaling = scaling[0]
    density = density[0]
    place = lax.axis_index("tile").astype(jnp.int32).reshape(1)
    f32 = jnp.float32
    vmem = pl.BlockSpec(memory_space=pltpu.VMEM)
    smem = pl.BlockSpec(memory_space=pltpu.SMEM)
    field = jax.ShapeDtypeStruct((FACES, ROWS, SIDE), f32)
    edge_rows = jax.ShapeDtypeStruct((FACES + FACES // 2, HALO, SIDE), f32)
    params = pltpu.CompilerParams(vmem_limit_bytes=24 * 1024 * 1024)
    across, beside, message = pl.pallas_call(
        pack_kernel,
        out_shape=(edge_rows, edge_rows, jax.ShapeDtypeStruct((tiles, 24, 128), f32)),
        in_specs=[smem] + [pl.BlockSpec(memory_space=pl.ANY)] * 3,
        out_specs=(vmem, vmem, vmem),
        scratch_shapes=[
            pltpu.SMEM(seams.shape, jnp.int32),
            pltpu.VMEM(scaling.shape, f32),
            pltpu.VMEM(density.shape, f32),
            pltpu.SemaphoreType.DMA((3,)),
        ],
        name="pack",
    )(place, seams, scaling, density)
    across = lax.ppermute(across, "tile", [(i, (i + 1 if i % 2 else i - 1) % tiles) for i in range(tiles)])
    beside = lax.ppermute(beside, "tile", [(i, i ^ 1) for i in range(tiles)])
    message = lax.all_to_all(message, "tile", 0, 0)
    rows = 384 // members
    sums = jax.ShapeDtypeStruct((members, rows + 8, 128), f32)
    dual, marginal, weighted = pl.pallas_call(
        heat_kernel,
        out_shape=(field, field, sums),
        in_specs=[smem, smem, smem] + [vmem] * 5,
        out_specs=(vmem, vmem, vmem),
        scratch_shapes=[
            pltpu.VMEM(edge_rows.shape, f32),
            pltpu.VMEM(edge_rows.shape, f32),
            pltpu.VMEM((6, 2 * TALL, 128), f32),
            pltpu.VMEM((2, 128, 128), f32),
            pltpu.VMEM((224, SIDE), f32),
            pltpu.VMEM((224, SIDE), f32),
            pltpu.VMEM((SIDE, 128), f32),
            pltpu.VMEM((SIDE, 128), f32),
            pltpu.VMEM((2, FACES, HALO, SIDE), f32),
            pltpu.VMEM((2, 3, TALL, 128), f32),
        ],
        compiler_params=params,
        name="heat",
    )(place, seams, member_weights, scaling, density, across, beside, message)
    weighted = lax.all_to_all(weighted, "member", 0, 0)
    means = pl.pallas_call(
        mean_kernel,
        out_shape=jax.ShapeDtypeStruct((members, rows, 128), f32),
        in_specs=[vmem],
        out_specs=vmem,
        compiler_params=params,
        name="mean",
    )(weighted)
    means = lax.all_to_all(means, "member", 0, 0)
    fresh, barycenter = pl.pallas_call(
        update_kernel,
        out_shape=(field, field),
        in_specs=[vmem] * 3,
        out_specs=(vmem, vmem),
        compiler_params=params,
        name="update",
    )(means, scaling, marginal)
    return (fresh[None], dual[None], barycenter)


def solution(mesh):
    return jax.shard_map(
        body,
        mesh=mesh,
        in_specs=(
            P("member", None, "tile", None),
            P("member", None, "tile", None),
            P("member"),
            P(),
        ),
        out_specs=(
            P("member", None, "tile", None),
            P("member", None, "tile", None),
            P(None, "tile", None),
        ),
        check_vma=False,
    )
```

```python
import jax
import jax.numpy as jnp
from jax import lax
from jax.experimental import pallas as pl
from jax.experimental.pallas import tpu as pltpu
from jax.sharding import PartitionSpec as P

KAPPA = 0.24
STEPS = 4
FACES = 6
ROWS = 16
SIDE = 512
HALO = 8
TALL = ROWS + 2 * HALO


def iota(shape, dim):
    return lax.broadcasted_iota(jnp.int32, shape, dim)


def reverse_lanes(x):
    index = 127 - iota((8, 128), 1)
    tiles = [
        jnp.take_along_axis(x[:, at : at + 128], index, axis=1)
        for at in range(0, x.shape[1], 128)
    ]
    return jnp.concatenate(tiles[::-1], axis=1) if len(tiles) > 1 else tiles[0]


def column_strips(first, last):
    strips = None
    for g in range(FACES):
        a, b = first(g), last(g)
        lane = iota(a.shape, 1)
        moved = pltpu.roll(jnp.where(lane >= 64, b, a), 16 * g + 8, 1)
        strips = moved if strips is None else jnp.where(lane >= 16 * g, moved, strips)
    return strips


PIECE = 18


def put_message(message, q, t0, t1, t2):
    lane = iota((8, 128), 1)
    sub = iota((8, 128), 0)
    at = PIECE * q
    message[at : at + 8, :] = jnp.where(lane < 96, t0, pltpu.roll(t2, 96, 1))
    message[at + 8 : at + 16, :] = jnp.where(lane < 96, t1, pltpu.roll(t2, 64, 1))
    rest = jnp.take_along_axis(t2, 64 + lane % 32, axis=1)
    rest = jnp.where(lane // 32 == sub % 4, rest, 0.0)
    message[at + 16 : at + 17, :] = jnp.sum(rest[:4], axis=0, keepdims=True)
    message[at + 17 : at + 18, :] = jnp.sum(rest[4:], axis=0, keepdims=True)


def get_message(message, p):
    lane = iota((8, 128), 1)
    sub = iota((8, 128), 0)
    at = PIECE * p
    t0 = message[pl.ds(at, 8), :]
    t1 = message[pl.ds(at + 8, 8), :]
    rest = jnp.where(sub < 4, message[pl.ds(at + 16, 1), :], message[pl.ds(at + 17, 1), :])
    rest = jnp.take_along_axis(rest, (lane + 64 + 32 * (sub % 4)) % 128, axis=1)
    t2 = jnp.where(lane < 32, pltpu.roll(t0, 32, 1), jnp.where(lane < 64, pltpu.roll(t1, 64, 1), rest))
    return t0, t1, t2


def join_density(near, far):
    lane = iota((8, 128), 1) % 16
    moved = jnp.where(lane < 8, pltpu.roll(far, 124, 1), pltpu.roll(far, 4, 1))
    return jnp.where((lane >= 4) & (lane < 12), near, moved)


def far_density(block):
    lane = iota((8, 128), 1) % 16
    return jnp.where(lane < 8, pltpu.roll(block, 4, 1), pltpu.roll(block, 124, 1))


def join_halves(low, high):
    return jnp.where(iota(low.shape, 0) < 4, low, high)


def halo_rows(rows, k, g, is_up):
    if k == 0:
        return rows[g]
    block = rows[FACES + g // 2]
    return pltpu.roll(block, 4, 0) if (g % 2 == 0) == is_up else block


def pack_kernel(place, seams_at, scaling_at, density_at, across, beside, message, seams, scaling, density, arrived):
    p = place[0]
    pairs = ((scaling_at, scaling), (density_at, density), (seams_at, seams))
    copies = [pltpu.make_async_copy(a, b, arrived.at[i]) for i, (a, b) in enumerate(pairs)]
    for copy in copies:
        copy.start()
    for copy in copies:
        copy.wait()
    is_even = lax.rem(p, 2) == 0
    count = message.shape[0] // PIECE
    lane = iota((8, 128), 1)
    sub = iota((8, 128), 0)
    ups = [scaling[g, HALO:] for g in range(FACES)]
    downs = [scaling[g, :HALO] for g in range(FACES)]
    for b in range(3):
        d0, d1 = density[2 * b], density[2 * b + 1]
        ups.append(join_halves(pltpu.roll(d0[HALO:], 4, 0), d1[HALO:]))
        downs.append(join_halves(d0[:HALO], pltpu.roll(d1[:HALO], 4, 0)))
    for b, (u, d) in enumerate(zip(ups, downs)):
        beside[b] = jnp.where(is_even, u, d)
        across[b] = jnp.where(is_even, d, u)
    vs = column_strips(lambda g: scaling[g, :, :128], lambda g: scaling[g, :, SIDE - 128 :])
    vd = column_strips(lambda g: density[g, :, :128], lambda g: density[g, :, SIDE - 128 :])
    columns = (vs[:8], vs[8:], join_density(vd[:8], vd[8:]))
    is_last = p == count - 1
    is_edge = (p == 0) | is_last

    @pl.when(jnp.logical_not(is_edge))
    def _():
        for q in range(count):
            put_message(message, q, *columns)

    @pl.when(is_edge)
    def _():
        put_message(message, 0, *columns)
        put_message(message, count - 1, *columns)
        e = is_last.astype(jnp.int32)
        base = pl.multiple_of(e * 8, 8)
        own_s = jnp.where(is_last, vs[:8], vs[8:])
        own_d = jnp.where(is_last, vd[:8], vd[8:])
        turned_d = pltpu.roll(own_d, 4, 0)
        even_d, odd_d = jnp.where(is_last, own_d, turned_d), jnp.where(is_last, turned_d, own_d)
        lane32 = lane % 32

        def coded(v, h):
            return jnp.where(lane32 < 8, pltpu.roll(v, 120 - 16 * h, 1), pltpu.roll(v, 24 - 16 * h, 1))

        room = jnp.where(is_last, 7 - sub, sub)
        free = (lane32 <= room) | (lane32 >= 31 - room)
        extra = (
            (free, coded(own_s, 0)),
            (free, coded(own_s, 1)),
            ((lane32 < 4) | (lane32 >= 28), jnp.where(sub < 4, coded(even_d, 0), coded(odd_d, 1))),
        )
        pieces = []
        for g in range(FACES):
            turned = seams[2, e, g] == 1
            s = scaling[g, pl.ds(base, 8), :]
            d = density[g, pl.ds(base, 8), :]
            pieces.append((jnp.where(turned, reverse_lanes(s), s), jnp.where(turned, reverse_lanes(d), d)))
        sub_wide = iota((8, SIDE), 0)
        lane_wide = iota((8, SIDE), 1) % 128
        blocks = []
        for b in range(3):
            (s0, d0), (s1, d1) = pieces[2 * b], pieces[2 * b + 1]
            low = jnp.where(is_last, pltpu.roll(d0, 4, 0), d0)
            high = jnp.where(is_last, d1, pltpu.roll(d1, 4, 0))
            blocks.append((s0, s1, jnp.where(sub_wide < 4, low, high)))
        for r in range(8):
            full = []
            for t in range(3):
                moved = [pltpu.roll(blocks[b][t], (32 * b - 16 * r + 8) % SIDE, 1) for b in range(3)]
                full.append(
                    jnp.where(lane_wide < 32, moved[0], jnp.where(lane_wide < 64, moved[1], moved[2]))
                )
            for a in range(4):
                q = 8 * a + r
                tiles = [x[:, 128 * a : 128 * a + 128] for x in full]
                if q in (1, count - 2):
                    tiles = [jnp.where(mask, other, tile) for (mask, other), tile in zip(extra, tiles)]
                if 0 < q < count - 1:
                    put_message(message, q, *tiles)


def diffuse(blocks):
    lane = iota((8, 128), 1)
    sub = iota((8, 128), 0)
    high, wide = len(blocks), len(blocks[0])
    result = []
    for i in range(high):
        line = []
        for j in range(wide):
            x = blocks[i][j]
            above = pltpu.roll(jnp.where(sub == 7, blocks[i - 1][j], x), 1, 0)
            below = pltpu.roll(jnp.where(sub == 0, blocks[(i + 1) % high][j], x), 7, 0)
            left = pltpu.roll(jnp.where(lane == 127, blocks[i][j - 1], x), 1, 1)
            right = pltpu.roll(jnp.where(lane == 0, blocks[i][(j + 1) % wide], x), 127, 1)
            line.append((1.0 - 4.0 * KAPPA) * x + KAPPA * ((above + below) + (left + right)))
        result.append(line)
    return result


def diffuse_strip(x, where):
    above = pltpu.roll(x, 1, 0)
    below = pltpu.roll(x, TALL - 1, 0)
    left = pltpu.roll(x, 1, 1)
    right = pltpu.roll(x, 127, 1)
    if where is not None:
        lane = iota((8, 128), 1)
        sub = iota((8, 128), 0)
        at, edge = (0, 8) if where == "first" else (24, 23)
        depth = 7 - sub if where == "first" else sub
        place = lane % 64
        start = lane - place
        line = jnp.broadcast_to(x[edge : edge + 1], (8, 128))
        index = jnp.where(place == 40, start + 39 - depth, jnp.where(place == 23, start + 24 + depth, 0))
        lateral = jnp.take_along_axis(line, index, axis=1)
        index = jnp.where(place >= 32, start + 40, start + 23)
        taken = jnp.take_along_axis(x[at : at + 8], index, axis=1)
        taken = jnp.where((place == 39 - depth) | (place == 24 + depth), taken, 0.0)
        vertical = jnp.sum(taken, axis=0, keepdims=True)
        ghost = (place >= 24) & (place < 40)
        fixed_left = jnp.where(place == 40, lateral, left[at : at + 8])
        fixed_right = jnp.where(place == 23, lateral, right[at : at + 8])
        if where == "first":
            left = jnp.concatenate([fixed_left, left[8:]], axis=0)
            right = jnp.concatenate([fixed_right, right[8:]], axis=0)
            block = jnp.where(ghost & (sub == 0), vertical, above[8:16])
            above = jnp.concatenate([above[:8], block, above[16:]], axis=0)
        else:
            left = jnp.concatenate([left[:24], fixed_left], axis=0)
            right = jnp.concatenate([right[:24], fixed_right], axis=0)
            block = jnp.where(ghost & (sub == 7), vertical, below[16:24])
            below = jnp.concatenate([below[:16], block, below[24:]], axis=0)
    return x + KAPPA * (((above + below) + (left + right)) - 4.0 * x)


def strip_lanes(first, last, h):
    lane = iota(first.shape, 1)
    return jnp.where(
        lane % 64 < 32, pltpu.roll(last, 24 + 64 * h, 1), pltpu.roll(first, 40 + 64 * h, 1)
    )


def swap_depth(x):
    lane = iota((8, 128), 1)
    index = lane + 7 - 2 * (lane % 8)
    return jnp.concatenate(
        [jnp.take_along_axis(x[at : at + 8], index, axis=1) for at in range(0, x.shape[0], 8)], axis=0
    )


def put_weighted(weighted, value, f, i, j):
    per = 48 // weighted.shape[0]
    t = 8 * f + 4 * i + j
    if isinstance(f, int):
        weighted[t // per, 8 * (t % per) : 8 * (t % per) + 8, :] = value
    else:
        at = pl.multiple_of(8 * lax.rem(t, per), 8)
        weighted[lax.div(t, per), pl.ds(at, 8), :] = value


def heat_kernel(
    place, seams, weight, scaling, density, across, beside, message,
    dual, marginal, weighted, up, down, mixed, chunk, table_s, table_d, column_s, column_d, edge, work,
):
    q = place[0]
    count = message.shape[0] // PIECE
    last = count - 1
    is_even = lax.rem(q, 2) == 0
    for b in range(FACES + FACES // 2):
        up[b] = jnp.where(is_even, across[b], beside[b])
        down[b] = jnp.where(is_even, beside[b], across[b])
    share = weight[0]
    lane = iota((8, 128), 1)
    sub = iota((8, 128), 0)
    is_edge = (q == 0) | (q == last)

    per = 48 // weighted.shape[0]
    for k in range(weighted.shape[0]):
        weighted[k, 8 * per :, :] = jnp.full((8, 128), share, jnp.float32)

    lane32 = lane % 32
    tiles = get_message(message, jnp.where(q == 1, last, 0))
    turned_d = pltpu.roll(tiles[2], 4, 0)
    even_d, odd_d = jnp.where(q == 1, tiles[2], turned_d), jnp.where(q == 1, turned_d, tiles[2])

    def decoded(even, odd):
        is_right = lane % 16 < 8
        return jnp.where(
            lane32 < 16,
            jnp.where(is_right, pltpu.roll(even, 104, 1), pltpu.roll(even, 8, 1)),
            jnp.where(is_right, pltpu.roll(odd, 120, 1), pltpu.roll(odd, 24, 1)),
        )

    coded_s = decoded(tiles[0], tiles[1])
    coded_d = decoded(even_d, odd_d)
    mirror = get_message(message, last - q)
    upper = get_message(message, jnp.minimum(last + 1 - q, last))
    lower = get_message(message, jnp.maximum(last - 1 - q, 0))
    parts_s = (
        jnp.where(q == last - 1, coded_s, lower[1]),
        mirror[0],
        mirror[1],
        jnp.where(q == 1, coded_s, upper[0]),
    )
    parts_d = (
        jnp.where(q == last - 1, coded_d, far_density(lower[2])),
        mirror[2],
        far_density(mirror[2]),
        jnp.where(q == 1, coded_d, upper[2]),
    )
    for base, parts in ((0, parts_s), (TALL, parts_d)):
        for block in range(4):
            for i in range(8):
                at = base + TALL - 1 - 8 * block - i
                mixed[2, at : at + 1, :] = parts[block][i : i + 1]

    chunk[:, 96:, :] = jnp.zeros((2, 32, 128), jnp.float32)

    @pl.when(jnp.logical_not(is_edge))
    def _():
        for e in range(2):
            tiles = get_message(message, e * last)
            for g in range(FACES):
                b, h = g // 2, g % 2
                turn = (128 - 32 * b) % 128
                s, d = tiles[h], tiles[2]
                if turn:
                    s, d = pltpu.roll(s, turn, 1), pltpu.roll(d, turn, 1)
                if h != e:
                    d = pltpu.roll(d, 4, 0)
                at = 48 * e + 8 * g
                chunk[0, at : at + 8, :] = s
                chunk[1, at : at + 8, :] = d

    for is_first in (True, False):

        @pl.when(q == (0 if is_first else last))
        def _():
            e = 0 if is_first else 1

            def gather(p, carry):
                at = pl.multiple_of(16 * p, 16)
                t0, t1, t2 = get_message(message, p)
                column_s[pl.ds(at, 8), :] = t0
                column_s[pl.ds(at + 8, 8), :] = t1
                column_d[pl.ds(at, 8), :] = t2
                column_d[pl.ds(at + 8, 8), :] = far_density(t2)
                return carry

            lax.fori_loop(0, count, gather, 0, unroll=8)
            for k, (table, columns, field) in enumerate(
                ((table_s, column_s, scaling), (table_d, column_d, density))
            ):
                for a in range(4):
                    rows = slice(128 * a, 128 * a + 128)
                    table[:128, rows] = jnp.transpose(columns[rows, :])
                for e_of in range(2):
                    for g in range(FACES):
                        if is_first:
                            rows = field[g, :HALO] if e_of == 0 else halo_rows(up, k, g, True)
                        else:
                            rows = halo_rows(down, k, g, False) if e_of == 0 else field[g, HALO:]
                        at = 48 * e_of + 8 * g
                        table[128 + at : 136 + at, :] = rows
                        turned = seams[2, e_of, g] == 1
                        a, b = rows[:, :128], rows[:, SIDE - 128 :]
                        if is_first:
                            piece = pltpu.roll(jnp.where(turned, reverse_lanes(b), a), 8, 1)
                        else:
                            piece = pltpu.roll(jnp.where(turned, reverse_lanes(a), b), 24, 1)
                        chunk[k, at : at + 8, :] = piece
                for f in range(FACES):
                    g, meets = seams[0, e, f], seams[1, e, f]
                    start = jnp.where(
                        meets >= 2, 16 * g + jnp.where(meets == 2, 8, 0), 128 + 48 * meets + 8 * g
                    )
                    rising = (meets % 2) == 0
                    for i in range(8):
                        depth = 7 - i if is_first else i
                        at = start + jnp.where(rising, depth, 7 - depth)
                        edge[k, f, i : i + 1, :] = table[pl.ds(at, 1), :]
                for f in range(FACES):
                    piece = edge[k, f]
                    edge[k, f] = jnp.where(seams[2, e, f] == 1, reverse_lanes(piece), piece)
                at = 0 if is_first else HALO + ROWS
                for t in range(3):
                    pieces = [
                        strip_lanes(edge[k, f, :, :128], edge[k, f, :, SIDE - 128 :], f % 2)
                        for f in (2 * t, 2 * t + 1)
                    ]
                    work[k, t, at : at + 8, :] = jnp.where(lane < 64, pieces[0], pieces[1])

    for k in range(2):
        mixed[4, k * TALL : (k + 1) * TALL, :] = jnp.transpose(chunk[k])[:TALL]
    lane_tall = iota((TALL, 128), 1)
    strips = []
    for k, field in enumerate((scaling, density)):

        def ends(g, at):
            columns = slice(at, at + 128)
            above = up.at[:, :, columns]
            below = down.at[:, :, columns]
            return jnp.concatenate(
                [halo_rows(above, k, g, True), field[g, :, columns], halo_rows(below, k, g, False)], axis=0
            )

        firsts = [ends(g, 0) for g in range(FACES)]
        lasts = [ends(g, SIDE - 128) for g in range(FACES)]
        strips.append([
            jnp.where(
                lane_tall < 64,
                strip_lanes(firsts[2 * t], lasts[2 * t], 0),
                strip_lanes(firsts[2 * t + 1], lasts[2 * t + 1], 1),
            )
            for t in range(3)
        ])
        mixed[0, k * TALL : (k + 1) * TALL, :] = column_strips(lambda g: firsts[g], lambda g: lasts[g])
    for v in (0, 2, 4):
        mixed[v + 1] = swap_depth(mixed[v])

    for k in range(2):
        for t in range(3):
            value = strips[k][t]
            for f in (2 * t, 2 * t + 1):
                for e in (2, 3):
                    g, meets, turned = seams[0, e, f], seams[1, e, f], seams[2, e, f]
                    of_column = meets >= 2
                    rising = (meets % 2) == 0
                    swapped = jnp.where(rising, 1 if e == 2 else 0, 0 if e == 2 else 1)
                    kind = jnp.where(of_column, 2 * turned, 4) + swapped
                    start = jnp.where(of_column, 16 * g + jnp.where(meets == 2, 8, 0), 48 * meets + 8 * g)
                    at = 64 * (f % 2) + (32 if e == 2 else 24)
                    moved = pltpu.roll(
                        mixed[kind, k * TALL : (k + 1) * TALL, :], jnp.bitwise_and(at - start + 128, 127), 1
                    )
                    value = jnp.where((lane_tall >= at) & (lane_tall < at + 8), moved, value)
            rows = [value[:8], value[8:24], value[24:]]
            work[k, t, 8:24, :] = rows[1]

            @pl.when(q != 0)
            def _():
                work[k, t, :8, :] = rows[0]

            @pl.when(q == 0)
            def _():
                work[k, t, :8, :] = jnp.where((lane % 64 >= 24) & (lane % 64 < 40), rows[0], work[k, t, :8, :])

            @pl.when(q != last)
            def _():
                work[k, t, 24:, :] = rows[2]

            @pl.when(q == last)
            def _():
                work[k, t, 24:, :] = jnp.where((lane % 64 >= 24) & (lane % 64 < 40), rows[2], work[k, t, 24:, :])

    def run(where):
        def tall(k, f):
            field = (scaling, density)[k]
            above = edge[k, f] if where == "first" else halo_rows(up, k, f, True)
            below = edge[k, f] if where == "last" else halo_rows(down, k, f, False)
            lines = (above, field[f, :HALO], field[f, HALO:], below)
            return [[line[:, at : at + 128] for at in range(0, SIDE, 128)] for line in lines]

        for some in (range(0, 3), range(3, FACES)):
            x = [tall(0, f) for f in some]
            for _ in range(STEPS):
                x = [diffuse(v) for v in x]
            y = [
                [[d / h for d, h in zip(*lines)] for lines in zip(tall(1, f), v)]
                for f, v in zip(some, x)
            ]
            for f, v in zip(some, y):
                for i in range(2):
                    for j in range(4):
                        dual[f, 8 * i : 8 * i + 8, 128 * j : 128 * j + 128] = v[i + 1][j]
            for _ in range(STEPS):
                y = [diffuse(v) for v in y]
            for f, v in zip(some, y):
                for i in range(2):
                    for j in range(4):
                        at = (f, slice(8 * i, 8 * i + 8), slice(128 * j, 128 * j + 128))
                        m = scaling[at] * v[i + 1][j]
                        marginal[at] = m
                        put_weighted(weighted, share * jnp.log(m), f, i, j)
        x = [work[0, t] for t in range(3)]
        for _ in range(STEPS):
            x = [diffuse_strip(v, where) for v in x]
        y = [work[1, t] / x[t] for t in range(3)]
        first = [v[HALO : HALO + ROWS] for v in y]
        for _ in range(STEPS):
            y = [diffuse_strip(v, where) for v in y]
        lane = iota((ROWS, 128), 1)
        for t in range(3):
            m = work[0, t, HALO : HALO + ROWS, :] * y[t][HALO : HALO + ROWS]
            scaled = share * jnp.log(m)
            for h in range(2):
                f = 2 * t + h
                for j, turn, mask in ((0, 88 - 64 * h, lane < 8), (3, 104 - 64 * h, lane >= 120)):
                    columns = slice(128 * j, 128 * j + 128)
                    for ref, value in ((dual, first[t]), (marginal, m)):
                        ref[f, :, columns] = jnp.where(mask, pltpu.roll(value, turn, 1), ref[f, :, columns])
                    moved = pltpu.roll(scaled, turn, 1)
                    for i in range(2):
                        at = 8 * f + 4 * i + j
                        rows = slice(8 * (at % per), 8 * (at % per) + 8)
                        weighted[at // per, rows, :] = jnp.where(
                            mask[:8], moved[8 * i : 8 * i + 8], weighted[at // per, rows, :]
                        )

    @pl.when(q == 0)
    def _():
        run("first")

    @pl.when(q == last)
    def _():
        run("last")

    @pl.when(jnp.logical_not(is_edge))
    def _():
        run(None)


def mean_kernel(parts, result):
    members, rows = result.shape[0], result.shape[1]
    total = parts[0]
    for k in range(1, members):
        total = total + parts[k]
    mean = total[:rows] / total[rows : rows + 1]
    value = jnp.exp(mean)
    for k in range(members):
        result[k] = value


def update_kernel(parts, scaling, marginal, fresh, barycenter):
    members = parts.shape[0]
    per = 48 // members
    for f in range(FACES):
        for i in range(2):
            for j in range(4):
                t = 8 * f + 4 * i + j
                at = 8 * (t % per)
                value = parts[t // per, at : at + 8, :]
                rows, columns = slice(8 * i, 8 * i + 8), slice(128 * j, 128 * j + 128)
                barycenter[f, rows, columns] = value
                fresh[f, rows, columns] = scaling[f, rows, columns] * value / marginal[f, rows, columns]


def body(density, scaling, member_weights, seams):
    tiles = lax.axis_size("tile")
    members = lax.axis_size("member")
    scaling = scaling[0]
    density = density[0]
    place = lax.axis_index("tile").astype(jnp.int32).reshape(1)
    f32 = jnp.float32
    vmem = pl.BlockSpec(memory_space=pltpu.VMEM)
    smem = pl.BlockSpec(memory_space=pltpu.SMEM)
    field = jax.ShapeDtypeStruct((FACES, ROWS, SIDE), f32)
    edge_rows = jax.ShapeDtypeStruct((FACES + FACES // 2, HALO, SIDE), f32)
    params = pltpu.CompilerParams(vmem_limit_bytes=24 * 1024 * 1024)
    across, beside, message = pl.pallas_call(
        pack_kernel,
        out_shape=(edge_rows, edge_rows, jax.ShapeDtypeStruct((PIECE * tiles, 128), f32)),
        in_specs=[smem] + [pl.BlockSpec(memory_space=pl.ANY)] * 3,
        out_specs=(vmem, vmem, vmem),
        scratch_shapes=[
            pltpu.SMEM(seams.shape, jnp.int32),
            pltpu.VMEM(scaling.shape, f32),
            pltpu.VMEM(density.shape, f32),
            pltpu.SemaphoreType.DMA((3,)),
        ],
        name="pack",
    )(place, seams, scaling, density)
    across = lax.ppermute(across, "tile", [(i, (i + 1 if i % 2 else i - 1) % tiles) for i in range(tiles)])
    beside = lax.ppermute(beside, "tile", [(i, i ^ 1) for i in range(tiles)])
    message = lax.all_to_all(message.reshape(tiles, PIECE * 128), "tile", 0, 0, tiled=True)
    message = message.reshape(PIECE * tiles, 128)
    rows = 384 // members
    sums = jax.ShapeDtypeStruct((members, rows + 8, 128), f32)
    dual, marginal, weighted = pl.pallas_call(
        heat_kernel,
        out_shape=(field, field, sums),
        in_specs=[smem, smem, smem] + [vmem] * 5,
        out_specs=(vmem, vmem, vmem),
        scratch_shapes=[
            pltpu.VMEM(edge_rows.shape, f32),
            pltpu.VMEM(edge_rows.shape, f32),
            pltpu.VMEM((6, 2 * TALL, 128), f32),
            pltpu.VMEM((2, 128, 128), f32),
            pltpu.VMEM((224, SIDE), f32),
            pltpu.VMEM((224, SIDE), f32),
            pltpu.VMEM((SIDE, 128), f32),
            pltpu.VMEM((SIDE, 128), f32),
            pltpu.VMEM((2, FACES, HALO, SIDE), f32),
            pltpu.VMEM((2, 3, TALL, 128), f32),
        ],
        compiler_params=params,
        name="heat",
    )(place, seams, member_weights, scaling, density, across, beside, message)
    weighted = lax.all_to_all(weighted, "member", 0, 0)
    means = pl.pallas_call(
        mean_kernel,
        out_shape=jax.ShapeDtypeStruct((members, rows, 128), f32),
        in_specs=[vmem],
        out_specs=vmem,
        compiler_params=params,
        name="mean",
    )(weighted)
    means = lax.all_to_all(means, "member", 0, 0)
    fresh, barycenter = pl.pallas_call(
        update_kernel,
        out_shape=(field, field),
        in_specs=[vmem] * 3,
        out_specs=(vmem, vmem),
        compiler_params=params,
        name="update",
    )(means, scaling, marginal)
    return (fresh[None], dual[None], barycenter)


def solution(mesh):
    return jax.shard_map(
        body,
        mesh=mesh,
        in_specs=(
            P("member", None, "tile", None),
            P("member", None, "tile", None),
            P("member"),
            P(),
        ),
        out_specs=(
            P("member", None, "tile", None),
            P("member", None, "tile", None),
            P(None, "tile", None),
        ),
        check_vma=False,
    )
```

```python
import jax
import jax.numpy as jnp
from jax import lax
from jax.experimental import pallas as pl
from jax.experimental.pallas import tpu as pltpu
from jax.sharding import PartitionSpec as P

KAPPA = 0.24
STEPS = 4
FACES = 6
ROWS = 16
SIDE = 512
HALO = 8
TALL = ROWS + 2 * HALO


def iota(shape, dim):
    return lax.broadcasted_iota(jnp.int32, shape, dim)


def reverse_lanes(x):
    index = 127 - iota((8, 128), 1)
    tiles = [
        jnp.take_along_axis(x[:, at : at + 128], index, axis=1)
        for at in range(0, x.shape[1], 128)
    ]
    return jnp.concatenate(tiles[::-1], axis=1) if len(tiles) > 1 else tiles[0]


def column_strips(first, last):
    strips = None
    for g in range(FACES):
        a, b = first(g), last(g)
        lane = iota(a.shape, 1)
        moved = pltpu.roll(jnp.where(lane >= 64, b, a), 16 * g + 8, 1)
        strips = moved if strips is None else jnp.where(lane >= 16 * g, moved, strips)
    return strips


PIECE = 18


def put_message(message, q, t0, t1, t2):
    lane = iota((8, 128), 1)
    sub = iota((8, 128), 0)
    at = PIECE * q
    message[at : at + 8, :] = jnp.where(lane < 96, t0, pltpu.roll(t2, 96, 1))
    message[at + 8 : at + 16, :] = jnp.where(lane < 96, t1, pltpu.roll(t2, 64, 1))
    rest = jnp.take_along_axis(t2, 64 + lane % 32, axis=1)
    rest = jnp.where(lane // 32 == sub % 4, rest, 0.0)
    rest = rest + pltpu.roll(rest, 1, 0)
    rest = rest + pltpu.roll(rest, 2, 0)
    message[at + 16 : at + 17, :] = rest[3:4]
    message[at + 17 : at + 18, :] = rest[7:8]


def get_message(message, p):
    lane = iota((8, 128), 1)
    sub = iota((8, 128), 0)
    at = PIECE * p
    t0 = message[pl.ds(at, 8), :]
    t1 = message[pl.ds(at + 8, 8), :]
    rest = jnp.where(sub < 4, message[pl.ds(at + 16, 1), :], message[pl.ds(at + 17, 1), :])
    rest = jnp.take_along_axis(rest, (lane + 64 + 32 * (sub % 4)) % 128, axis=1)
    t2 = jnp.where(lane < 32, pltpu.roll(t0, 32, 1), jnp.where(lane < 64, pltpu.roll(t1, 64, 1), rest))
    return t0, t1, t2


def join_density(near, far):
    lane = iota((8, 128), 1) % 16
    moved = jnp.where(lane < 8, pltpu.roll(far, 124, 1), pltpu.roll(far, 4, 1))
    return jnp.where((lane >= 4) & (lane < 12), near, moved)


def far_density(block):
    lane = iota((8, 128), 1) % 16
    return jnp.where(lane < 8, pltpu.roll(block, 4, 1), pltpu.roll(block, 124, 1))


def join_halves(low, high):
    return jnp.where(iota(low.shape, 0) < 4, low, high)


def halo_rows(rows, k, g, is_up):
    if k == 0:
        return rows[g]
    block = rows[FACES + g // 2]
    return pltpu.roll(block, 4, 0) if (g % 2 == 0) == is_up else block


def pack_kernel(place, seams_at, scaling_at, density_at, across, beside, message, seams, scaling, density, arrived):
    p = place[0]
    pairs = ((scaling_at, scaling), (density_at, density), (seams_at, seams))
    copies = [pltpu.make_async_copy(a, b, arrived.at[i]) for i, (a, b) in enumerate(pairs)]
    for copy in copies:
        copy.start()
    for copy in copies:
        copy.wait()
    is_even = lax.rem(p, 2) == 0
    count = message.shape[0] // PIECE
    lane = iota((8, 128), 1)
    sub = iota((8, 128), 0)
    ups = [scaling[g, HALO:] for g in range(FACES)]
    downs = [scaling[g, :HALO] for g in range(FACES)]
    for b in range(3):
        d0, d1 = density[2 * b], density[2 * b + 1]
        ups.append(join_halves(pltpu.roll(d0[HALO:], 4, 0), d1[HALO:]))
        downs.append(join_halves(d0[:HALO], pltpu.roll(d1[:HALO], 4, 0)))
    for b, (u, d) in enumerate(zip(ups, downs)):
        beside[b] = jnp.where(is_even, u, d)
        across[b] = jnp.where(is_even, d, u)
    vs = column_strips(lambda g: scaling[g, :, :128], lambda g: scaling[g, :, SIDE - 128 :])
    vd = column_strips(lambda g: density[g, :, :128], lambda g: density[g, :, SIDE - 128 :])
    columns = (vs[:8], vs[8:], join_density(vd[:8], vd[8:]))
    is_last = p == count - 1
    is_edge = (p == 0) | is_last

    @pl.when(jnp.logical_not(is_edge))
    def _():
        for q in range(count):
            put_message(message, q, *columns)

    @pl.when(is_edge)
    def _():
        put_message(message, 0, *columns)
        put_message(message, count - 1, *columns)
        e = is_last.astype(jnp.int32)
        base = pl.multiple_of(e * 8, 8)
        own_s = jnp.where(is_last, vs[:8], vs[8:])
        own_d = jnp.where(is_last, vd[:8], vd[8:])
        turned_d = pltpu.roll(own_d, 4, 0)
        even_d, odd_d = jnp.where(is_last, own_d, turned_d), jnp.where(is_last, turned_d, own_d)
        lane32 = lane % 32

        def coded(v, h):
            return jnp.where(lane32 < 8, pltpu.roll(v, 120 - 16 * h, 1), pltpu.roll(v, 24 - 16 * h, 1))

        room = jnp.where(is_last, 7 - sub, sub)
        free = (lane32 <= room) | (lane32 >= 31 - room)
        extra = (
            (free, coded(own_s, 0)),
            (free, coded(own_s, 1)),
            ((lane32 < 4) | (lane32 >= 28), jnp.where(sub < 4, coded(even_d, 0), coded(odd_d, 1))),
        )
        pieces = []
        for g in range(FACES):
            turned = seams[2, e, g] == 1
            s = scaling[g, pl.ds(base, 8), :]
            d = density[g, pl.ds(base, 8), :]
            pieces.append((jnp.where(turned, reverse_lanes(s), s), jnp.where(turned, reverse_lanes(d), d)))
        sub_wide = iota((8, SIDE), 0)
        lane_wide = iota((8, SIDE), 1) % 128
        blocks = []
        for b in range(3):
            (s0, d0), (s1, d1) = pieces[2 * b], pieces[2 * b + 1]
            low = jnp.where(is_last, pltpu.roll(d0, 4, 0), d0)
            high = jnp.where(is_last, d1, pltpu.roll(d1, 4, 0))
            blocks.append((s0, s1, jnp.where(sub_wide < 4, low, high)))
        for r in range(8):
            full = []
            for t in range(3):
                moved = [pltpu.roll(blocks[b][t], (32 * b - 16 * r + 8) % SIDE, 1) for b in range(3)]
                full.append(
                    jnp.where(lane_wide < 32, moved[0], jnp.where(lane_wide < 64, moved[1], moved[2]))
                )
            for a in range(4):
                q = 8 * a + r
                tiles = [x[:, 128 * a : 128 * a + 128] for x in full]
                if q in (1, count - 2):
                    tiles = [jnp.where(mask, other, tile) for (mask, other), tile in zip(extra, tiles)]
                if 0 < q < count - 1:
                    put_message(message, q, *tiles)


def diffuse(blocks):
    lane = iota((8, 128), 1)
    sub = iota((8, 128), 0)
    high, wide = len(blocks), len(blocks[0])
    result = []
    for i in range(high):
        line = []
        for j in range(wide):
            x = blocks[i][j]
            above = pltpu.roll(jnp.where(sub == 7, blocks[i - 1][j], x), 1, 0)
            below = pltpu.roll(jnp.where(sub == 0, blocks[(i + 1) % high][j], x), 7, 0)
            left = pltpu.roll(jnp.where(lane == 127, blocks[i][j - 1], x), 1, 1)
            right = pltpu.roll(jnp.where(lane == 0, blocks[i][(j + 1) % wide], x), 127, 1)
            line.append((1.0 - 4.0 * KAPPA) * x + KAPPA * ((above + below) + (left + right)))
        result.append(line)
    return result


def diffuse_strip(x, where):
    above = pltpu.roll(x, 1, 0)
    below = pltpu.roll(x, TALL - 1, 0)
    left = pltpu.roll(x, 1, 1)
    right = pltpu.roll(x, 127, 1)
    if where is not None:
        lane = iota((8, 128), 1)
        sub = iota((8, 128), 0)
        at, edge = (0, 8) if where == "first" else (24, 23)
        depth = 7 - sub if where == "first" else sub
        place = lane % 64
        start = lane - place
        line = jnp.broadcast_to(x[edge : edge + 1], (8, 128))
        index = jnp.where(place == 40, start + 39 - depth, jnp.where(place == 23, start + 24 + depth, 0))
        lateral = jnp.take_along_axis(line, index, axis=1)
        index = jnp.where(place >= 32, start + 40, start + 23)
        taken = jnp.take_along_axis(x[at : at + 8], index, axis=1)
        taken = jnp.where((place == 39 - depth) | (place == 24 + depth), taken, 0.0)
        vertical = jnp.sum(taken, axis=0, keepdims=True)
        ghost = (place >= 24) & (place < 40)
        fixed_left = jnp.where(place == 40, lateral, left[at : at + 8])
        fixed_right = jnp.where(place == 23, lateral, right[at : at + 8])
        if where == "first":
            left = jnp.concatenate([fixed_left, left[8:]], axis=0)
            right = jnp.concatenate([fixed_right, right[8:]], axis=0)
            block = jnp.where(ghost & (sub == 0), vertical, above[8:16])
            above = jnp.concatenate([above[:8], block, above[16:]], axis=0)
        else:
            left = jnp.concatenate([left[:24], fixed_left], axis=0)
            right = jnp.concatenate([right[:24], fixed_right], axis=0)
            block = jnp.where(ghost & (sub == 7), vertical, below[16:24])
            below = jnp.concatenate([below[:16], block, below[24:]], axis=0)
    return x + KAPPA * (((above + below) + (left + right)) - 4.0 * x)


def strip_lanes(first, last, h):
    lane = iota(first.shape, 1)
    return jnp.where(
        lane % 64 < 32, pltpu.roll(last, 24 + 64 * h, 1), pltpu.roll(first, 40 + 64 * h, 1)
    )


def swap_depth(x):
    lane = iota((8, 128), 1)
    index = lane + 7 - 2 * (lane % 8)
    return jnp.concatenate(
        [jnp.take_along_axis(x[at : at + 8], index, axis=1) for at in range(0, x.shape[0], 8)], axis=0
    )


CELLS = FACES * ROWS * SIDE // 128


def weighted_rows(weighted, f, i, j):
    share = CELLS // ((weighted.shape[0] - CELLS))
    t = 8 * (8 * f + 4 * i + j)
    at = t // share * (share + 1) + t % share
    return slice(at, at + 8)


def heat_kernel(
    place, seams, weight, scaling, density, across, beside, message,
    dual, marginal, weighted, up, down, mixed, chunk, table_s, table_d, column_s, column_d, edge, work,
):
    q = place[0]
    count = message.shape[0] // PIECE
    last = count - 1
    is_even = lax.rem(q, 2) == 0
    for b in range(FACES + FACES // 2):
        up[b] = jnp.where(is_even, across[b], beside[b])
        down[b] = jnp.where(is_even, beside[b], across[b])
    share = weight[0]
    lane = iota((8, 128), 1)
    sub = iota((8, 128), 0)
    is_edge = (q == 0) | (q == last)

    members = weighted.shape[0] - CELLS
    for k in range(1, members + 1):
        at = k * (CELLS // members + 1) - 1
        weighted[at : at + 1, :] = jnp.full((1, 128), share, jnp.float32)

    lane32 = lane % 32
    tiles = get_message(message, jnp.where(q == 1, last, 0))
    turned_d = pltpu.roll(tiles[2], 4, 0)
    even_d, odd_d = jnp.where(q == 1, tiles[2], turned_d), jnp.where(q == 1, turned_d, tiles[2])

    def decoded(even, odd):
        is_right = lane % 16 < 8
        return jnp.where(
            lane32 < 16,
            jnp.where(is_right, pltpu.roll(even, 104, 1), pltpu.roll(even, 8, 1)),
            jnp.where(is_right, pltpu.roll(odd, 120, 1), pltpu.roll(odd, 24, 1)),
        )

    coded_s = decoded(tiles[0], tiles[1])
    coded_d = decoded(even_d, odd_d)
    mirror = get_message(message, last - q)
    upper = get_message(message, jnp.minimum(last + 1 - q, last))
    lower = get_message(message, jnp.maximum(last - 1 - q, 0))
    parts_s = (
        jnp.where(q == last - 1, coded_s, lower[1]),
        mirror[0],
        mirror[1],
        jnp.where(q == 1, coded_s, upper[0]),
    )
    parts_d = (
        jnp.where(q == last - 1, coded_d, far_density(lower[2])),
        mirror[2],
        far_density(mirror[2]),
        jnp.where(q == 1, coded_d, upper[2]),
    )
    for base, parts in ((0, parts_s), (TALL, parts_d)):
        for block in range(4):
            for i in range(8):
                at = base + TALL - 1 - 8 * block - i
                mixed[2, at : at + 1, :] = parts[block][i : i + 1]

    chunk[:, 96:, :] = jnp.zeros((2, 32, 128), jnp.float32)

    @pl.when(jnp.logical_not(is_edge))
    def _():
        for e in range(2):
            tiles = get_message(message, e * last)
            for g in range(FACES):
                b, h = g // 2, g % 2
                turn = (128 - 32 * b) % 128
                s, d = tiles[h], tiles[2]
                if turn:
                    s, d = pltpu.roll(s, turn, 1), pltpu.roll(d, turn, 1)
                if h != e:
                    d = pltpu.roll(d, 4, 0)
                at = 48 * e + 8 * g
                chunk[0, at : at + 8, :] = s
                chunk[1, at : at + 8, :] = d

    for is_first in (True, False):

        @pl.when(q == (0 if is_first else last))
        def _():
            e = 0 if is_first else 1

            def gather(p, carry):
                at = pl.multiple_of(16 * p, 16)
                t0, t1, t2 = get_message(message, p)
                column_s[pl.ds(at, 8), :] = t0
                column_s[pl.ds(at + 8, 8), :] = t1
                column_d[pl.ds(at, 8), :] = t2
                column_d[pl.ds(at + 8, 8), :] = far_density(t2)
                return carry

            lax.fori_loop(0, count, gather, 0, unroll=8)
            for k, (table, columns, field) in enumerate(
                ((table_s, column_s, scaling), (table_d, column_d, density))
            ):
                for a in range(4):
                    rows = slice(128 * a, 128 * a + 128)
                    table[:128, rows] = jnp.transpose(columns[rows, :])
                for e_of in range(2):
                    for g in range(FACES):
                        if is_first:
                            rows = field[g, :HALO] if e_of == 0 else halo_rows(up, k, g, True)
                        else:
                            rows = halo_rows(down, k, g, False) if e_of == 0 else field[g, HALO:]
                        at = 48 * e_of + 8 * g
                        table[128 + at : 136 + at, :] = rows
                        turned = seams[2, e_of, g] == 1
                        a, b = rows[:, :128], rows[:, SIDE - 128 :]
                        if is_first:
                            piece = pltpu.roll(jnp.where(turned, reverse_lanes(b), a), 8, 1)
                        else:
                            piece = pltpu.roll(jnp.where(turned, reverse_lanes(a), b), 24, 1)
                        chunk[k, at : at + 8, :] = piece
                for f in range(FACES):
                    g, meets = seams[0, e, f], seams[1, e, f]
                    start = jnp.where(
                        meets >= 2, 16 * g + jnp.where(meets == 2, 8, 0), 128 + 48 * meets + 8 * g
                    )
                    rising = (meets % 2) == 0
                    for i in range(8):
                        depth = 7 - i if is_first else i
                        at = start + jnp.where(rising, depth, 7 - depth)
                        edge[k, f, i : i + 1, :] = table[pl.ds(at, 1), :]
                for f in range(FACES):
                    piece = edge[k, f]
                    edge[k, f] = jnp.where(seams[2, e, f] == 1, reverse_lanes(piece), piece)
                at = 0 if is_first else HALO + ROWS
                for t in range(3):
                    pieces = [
                        strip_lanes(edge[k, f, :, :128], edge[k, f, :, SIDE - 128 :], f % 2)
                        for f in (2 * t, 2 * t + 1)
                    ]
                    work[k, t, at : at + 8, :] = jnp.where(lane < 64, pieces[0], pieces[1])

    for k in range(2):
        mixed[4, k * TALL : (k + 1) * TALL, :] = jnp.transpose(chunk[k])[:TALL]
    lane_tall = iota((TALL, 128), 1)
    strips = []
    for k, field in enumerate((scaling, density)):

        def ends(g, at):
            columns = slice(at, at + 128)
            above = up.at[:, :, columns]
            below = down.at[:, :, columns]
            return jnp.concatenate(
                [halo_rows(above, k, g, True), field[g, :, columns], halo_rows(below, k, g, False)], axis=0
            )

        firsts = [ends(g, 0) for g in range(FACES)]
        lasts = [ends(g, SIDE - 128) for g in range(FACES)]
        strips.append([
            jnp.where(
                lane_tall < 64,
                strip_lanes(firsts[2 * t], lasts[2 * t], 0),
                strip_lanes(firsts[2 * t + 1], lasts[2 * t + 1], 1),
            )
            for t in range(3)
        ])
        mixed[0, k * TALL : (k + 1) * TALL, :] = column_strips(lambda g: firsts[g], lambda g: lasts[g])
    for v in (0, 2, 4):
        mixed[v + 1] = swap_depth(mixed[v])

    for k in range(2):
        for t in range(3):
            value = strips[k][t]
            for f in (2 * t, 2 * t + 1):
                for e in (2, 3):
                    g, meets, turned = seams[0, e, f], seams[1, e, f], seams[2, e, f]
                    of_column = meets >= 2
                    rising = (meets % 2) == 0
                    swapped = jnp.where(rising, 1 if e == 2 else 0, 0 if e == 2 else 1)
                    kind = jnp.where(of_column, 2 * turned, 4) + swapped
                    start = jnp.where(of_column, 16 * g + jnp.where(meets == 2, 8, 0), 48 * meets + 8 * g)
                    at = 64 * (f % 2) + (32 if e == 2 else 24)
                    moved = pltpu.roll(
                        mixed[kind, k * TALL : (k + 1) * TALL, :], jnp.bitwise_and(at - start + 128, 127), 1
                    )
                    value = jnp.where((lane_tall >= at) & (lane_tall < at + 8), moved, value)
            rows = [value[:8], value[8:24], value[24:]]
            work[k, t, 8:24, :] = rows[1]

            @pl.when(q != 0)
            def _():
                work[k, t, :8, :] = rows[0]

            @pl.when(q == 0)
            def _():
                work[k, t, :8, :] = jnp.where((lane % 64 >= 24) & (lane % 64 < 40), rows[0], work[k, t, :8, :])

            @pl.when(q != last)
            def _():
                work[k, t, 24:, :] = rows[2]

            @pl.when(q == last)
            def _():
                work[k, t, 24:, :] = jnp.where((lane % 64 >= 24) & (lane % 64 < 40), rows[2], work[k, t, 24:, :])

    def run(where):
        def tall(k, f):
            field = (scaling, density)[k]
            above = edge[k, f] if where == "first" else halo_rows(up, k, f, True)
            below = edge[k, f] if where == "last" else halo_rows(down, k, f, False)
            lines = (above, field[f, :HALO], field[f, HALO:], below)
            return [[line[:, at : at + 128] for at in range(0, SIDE, 128)] for line in lines]

        for some in (range(0, 3), range(3, FACES)):
            x = [tall(0, f) for f in some]
            for _ in range(STEPS):
                x = [diffuse(v) for v in x]
            y = [
                [[d / h for d, h in zip(*lines)] for lines in zip(tall(1, f), v)]
                for f, v in zip(some, x)
            ]
            for f, v in zip(some, y):
                for i in range(2):
                    for j in range(4):
                        dual[f, 8 * i : 8 * i + 8, 128 * j : 128 * j + 128] = v[i + 1][j]
            for _ in range(STEPS):
                y = [diffuse(v) for v in y]
            for f, v in zip(some, y):
                for i in range(2):
                    for j in range(4):
                        at = (f, slice(8 * i, 8 * i + 8), slice(128 * j, 128 * j + 128))
                        m = scaling[at] * v[i + 1][j]
                        marginal[at] = m
                        weighted[weighted_rows(weighted, f, i, j), :] = share * jnp.log(m)
        x = [work[0, t] for t in range(3)]
        for _ in range(STEPS):
            x = [diffuse_strip(v, where) for v in x]
        y = [work[1, t] / x[t] for t in range(3)]
        first = [v[HALO : HALO + ROWS] for v in y]
        for _ in range(STEPS):
            y = [diffuse_strip(v, where) for v in y]
        lane = iota((ROWS, 128), 1)
        for t in range(3):
            m = work[0, t, HALO : HALO + ROWS, :] * y[t][HALO : HALO + ROWS]
            scaled = share * jnp.log(m)
            for h in range(2):
                f = 2 * t + h
                for j, turn, mask in ((0, 88 - 64 * h, lane < 8), (3, 104 - 64 * h, lane >= 120)):
                    columns = slice(128 * j, 128 * j + 128)
                    for ref, value in ((dual, first[t]), (marginal, m)):
                        ref[f, :, columns] = jnp.where(mask, pltpu.roll(value, turn, 1), ref[f, :, columns])
                    moved = pltpu.roll(scaled, turn, 1)
                    for i in range(2):
                        rows = weighted_rows(weighted, f, i, j)
                        weighted[rows, :] = jnp.where(mask[:8], moved[8 * i : 8 * i + 8], weighted[rows, :])

    @pl.when(q == 0)
    def _():
        run("first")

    @pl.when(q == last)
    def _():
        run("last")

    @pl.when(jnp.logical_not(is_edge))
    def _():
        run(None)


def mean_kernel(parts, result):
    members, rows = result.shape[0], result.shape[1]
    total = parts[: rows + 1, :]
    for k in range(1, members):
        total = total + parts[k * (rows + 1) : (k + 1) * (rows + 1), :]
    mean = total[:rows] / total[rows : rows + 1]
    value = jnp.exp(mean)
    for k in range(members):
        result[k] = value


def update_kernel(parts, scaling, marginal, fresh, barycenter):
    members = parts.shape[0]
    per = 48 // members
    for f in range(FACES):
        for i in range(2):
            for j in range(4):
                t = 8 * f + 4 * i + j
                at = 8 * (t % per)
                value = parts[t // per, at : at + 8, :]
                rows, columns = slice(8 * i, 8 * i + 8), slice(128 * j, 128 * j + 128)
                barycenter[f, rows, columns] = value
                fresh[f, rows, columns] = scaling[f, rows, columns] * value / marginal[f, rows, columns]


def body(density, scaling, member_weights, seams):
    tiles = lax.axis_size("tile")
    members = lax.axis_size("member")
    scaling = scaling[0]
    density = density[0]
    place = lax.axis_index("tile").astype(jnp.int32).reshape(1)
    f32 = jnp.float32
    vmem = pl.BlockSpec(memory_space=pltpu.VMEM)
    smem = pl.BlockSpec(memory_space=pltpu.SMEM)
    field = jax.ShapeDtypeStruct((FACES, ROWS, SIDE), f32)
    edge_rows = jax.ShapeDtypeStruct((FACES + FACES // 2, HALO, SIDE), f32)
    params = pltpu.CompilerParams(vmem_limit_bytes=24 * 1024 * 1024)
    across, beside, message = pl.pallas_call(
        pack_kernel,
        out_shape=(edge_rows, edge_rows, jax.ShapeDtypeStruct((PIECE * tiles, 128), f32)),
        in_specs=[smem] + [pl.BlockSpec(memory_space=pl.ANY)] * 3,
        out_specs=(vmem, vmem, vmem),
        scratch_shapes=[
            pltpu.SMEM(seams.shape, jnp.int32),
            pltpu.VMEM(scaling.shape, f32),
            pltpu.VMEM(density.shape, f32),
            pltpu.SemaphoreType.DMA((3,)),
        ],
        name="pack",
    )(place, seams, scaling, density)
    across = lax.ppermute(across, "tile", [(i, (i + 1 if i % 2 else i - 1) % tiles) for i in range(tiles)])
    beside = lax.ppermute(beside, "tile", [(i, i ^ 1) for i in range(tiles)])
    message = lax.all_to_all(message.reshape(tiles, PIECE * 128), "tile", 0, 0, tiled=True)
    message = message.reshape(PIECE * tiles, 128)
    rows = 384 // members
    sums = jax.ShapeDtypeStruct((CELLS + members, 128), f32)
    dual, marginal, weighted = pl.pallas_call(
        heat_kernel,
        out_shape=(field, field, sums),
        in_specs=[smem, smem, smem] + [vmem] * 5,
        out_specs=(vmem, vmem, vmem),
        scratch_shapes=[
            pltpu.VMEM(edge_rows.shape, f32),
            pltpu.VMEM(edge_rows.shape, f32),
            pltpu.VMEM((6, 2 * TALL, 128), f32),
            pltpu.VMEM((2, 128, 128), f32),
            pltpu.VMEM((224, SIDE), f32),
            pltpu.VMEM((224, SIDE), f32),
            pltpu.VMEM((SIDE, 128), f32),
            pltpu.VMEM((SIDE, 128), f32),
            pltpu.VMEM((2, FACES, HALO, SIDE), f32),
            pltpu.VMEM((2, 3, TALL, 128), f32),
        ],
        compiler_params=params,
        name="heat",
    )(place, seams, member_weights, scaling, density, across, beside, message)
    weighted = lax.all_to_all(weighted.reshape(members, (rows + 1) * 128), "member", 0, 0, tiled=True)
    weighted = weighted.reshape(CELLS + members, 128)
    means = pl.pallas_call(
        mean_kernel,
        out_shape=jax.ShapeDtypeStruct((members, rows, 128), f32),
        in_specs=[vmem],
        out_specs=vmem,
        compiler_params=params,
        name="mean",
    )(weighted)
    means = lax.all_to_all(means, "member", 0, 0)
    fresh, barycenter = pl.pallas_call(
        update_kernel,
        out_shape=(field, field),
        in_specs=[vmem] * 3,
        out_specs=(vmem, vmem),
        compiler_params=params,
        name="update",
    )(means, scaling, marginal)
    return (fresh[None], dual[None], barycenter)


def solution(mesh):
    return jax.shard_map(
        body,
        mesh=mesh,
        in_specs=(
            P("member", None, "tile", None),
            P("member", None, "tile", None),
            P("member"),
            P(),
        ),
        out_specs=(
            P("member", None, "tile", None),
            P("member", None, "tile", None),
            P(None, "tile", None),
        ),
        check_vma=False,
    )
```
